32 devices in a mesh: groups: 2 (over y), tp: 16 (over z, x, core).
Axes of the slice: x: 2, y: 2, z: 4, core: 2. Of those that a mesh axis runs over, the one named last changes fastest.
Arguments:
- queries: bfloat16 [16, 256, 128], P('tp', 'groups'), parts along dimension 1, may hold values from -32 to 32
- cache_keys: bfloat16 [16, 16384, 128], P('tp', 'groups'), parts along dimension 1, may hold values from -6 to 6
- cache_values: bfloat16 [16, 16384, 128], P('tp', 'groups'), parts along dimension 1, may hold values from -6 to 6
- query_positions: int32 [256], P('groups'), parts along dimension 0, may hold values from 0 to 8191, as said below
- out_weight: bfloat16 [2048, 16384], P('tp'), may hold values from -0.75 to 0.75
- residual: bfloat16 [256, 16384], P('groups', 'tp'), parts along dimension 0, may hold values from -80 to 80
- scale_table: int32 [2, 128], replicated, may hold values from 2 to 127
- norm_gain: bfloat16 [16384], replicated, may hold values from 0.099609375 to 1.8984375
- next_query_weight: bfloat16 [16384, 2048], P(None, 'tp'), may hold values from -0.046875 to 0.046875
Outputs:
- hidden_out: bfloat16 [256, 16384], P('groups', 'tp'), parts along dimension 0
- query_next: bfloat16 [256, 2048], P('groups', 'tp'), parts along dimension 0
The draws below stay inside these ranges and needn't reach their ends.
There are 2 independent parts, one for each index of `groups`. The reference program is written for one: setup_inputs(seed, part) draws one part's arguments, and reference() takes and returns one part's arrays. A program takes and returns all parts, laid end to end along the dimension named above; an argument that names none is the same for every part. Nothing has to cross between parts.
Inputs may be any that keep to these rules, and one draw needn't show every extreme that they name: `query_positions`: strictly increasing along the span; the last entry is 8191.
All inputs are finite; a program needn't handle non-finite values.
Results may differ from the reference program's by a relative error of at most 0.0065.
Values may be sent and summed in bfloat16 or wider, within the bound.
No kernel may reach another device: no remote copies, remote signals or barrier semaphores. Data moves between devices by JAX's collectives and lax.ppermute only.
A program may use at most 128 MiB of HBM per device.

```python
import math
import jax
import jax.numpy as jnp
from jax import lax

D = 16384
HD = 128
ROT = 128
TOK = 128
CTX = 8192
HEADS = 16


def span_positions(key):
    gap_sizes = jax.random.randint(jax.random.fold_in(key, 11), (TOK,), 1, CTX // TOK + 1)
    suffix_sums = jnp.cumsum(gap_sizes[::-1])[::-1] - gap_sizes
    return (CTX - 1 - suffix_sums).astype(jnp.int32)


def draw_query_positions(key, part):
    return span_positions(key)


def draw_queries(key, part):
    key = jax.random.fold_in(key, 3)
    entries = jnp.clip(jax.random.normal(key, (HEADS, TOK, HD), jnp.float32), -6.0, 6.0)
    return entries.astype(jnp.bfloat16)


def draw_cache_keys(key, part):
    key = jax.random.fold_in(key, 2)
    entries = jnp.clip(jax.random.normal(key, (HEADS, CTX, HD), jnp.float32), -6.0, 6.0)
    return entries.astype(jnp.bfloat16)


def draw_residual(key, part):
    key = jax.random.fold_in(key, 4)
    column_key, row_key, entry_key = jax.random.split(key, 3)
    ramp = jnp.exp(math.log(3.0) * jnp.arange(D, dtype=jnp.float32) / D)
    column_scale = ramp * jnp.exp(jax.random.uniform(column_key, (D,), jnp.float32, math.log(0.5), math.log(2.0)))
    row_scale = jnp.exp(jax.random.uniform(row_key, (TOK, 1), jnp.float32, math.log(0.5), math.log(2.0)))
    entries = jnp.clip(jax.random.normal(entry_key, (TOK, D), jnp.float32), -6.0, 6.0)
    return (entries * row_scale * column_scale[None, :]).astype(jnp.bfloat16)


def with_ends(drawn, rng, smallest, high):
    longest = drawn.shape.index(max(drawn.shape))
    spots = []
    for shift in (0, 1):
        where = [jax.random.randint(jax.random.fold_in(rng, axis), (), 0, length) for axis, length in enumerate(drawn.shape)]
        where[longest] = (where[longest] + shift) % drawn.shape[longest]
        spots.append(tuple(where))
    return drawn.at[spots[0]].set(smallest).at[spots[1]].set(high)


def with_spikes(values, rng, source, target, shards_of, factor):
    owner, partner = [(jnp.arange(values.shape[dim]) // (values.shape[dim] // shards_of)).reshape([-1 if axis == dim else 1 for axis in range(values.ndim)]) for dim in (source, target)]
    chosen = jax.random.permutation(rng, shards_of)[partner]
    strong = (owner == chosen) | (owner == (partner + shards_of // 2) % shards_of)
    return jnp.where(strong, factor * values, values)


def shard_levels(key, extent, shards, least, high):
    gain = 1.0
    for dim, parts in shards:
        heights = jax.random.uniform(jax.random.fold_in(jax.random.fold_in(key, 6), dim), (parts,), jnp.float32, least / len(shards), high / len(shards))
        gain = gain * jnp.repeat(jnp.exp(heights), extent[dim] // parts).reshape((-1,) + (1,) * (len(extent) - 1 - dim))
    return gain


def gaussian(stream_key, shape, width, bound, cuts=(), held_as=jnp.bfloat16):
    gain = shard_levels(stream_key, shape, cuts, -0.22, 0.18) if cuts else 1.0
    values = jax.random.normal(stream_key, shape, jnp.float32) * width * gain
    return jnp.minimum(jnp.maximum(values, -bound), bound).astype(held_as)


def gaussian_with(stream_key, shape, scale, reach, pieces, heavy, kind=jnp.bfloat16):
    values = scale * jax.random.normal(stream_key, shape, jnp.float32)
    if pieces:
        values = values * shard_levels(stream_key, shape, pieces, -0.22, 0.18)
    return jnp.clip(with_spikes(values, jax.random.fold_in(stream_key, 3), *heavy), -reach, reach).astype(kind)


def setup_inputs(seed: int = 0, part: int = 0) -> dict:
    key_of = jax.random.split(jax.random.key(seed), 10)
    part_splits = jax.random.split(jax.random.fold_in(key_of[9], part), 10)
    queries = draw_queries(jax.random.fold_in(jax.random.fold_in(key_of[9], part), 71), part)
    cache_keys = draw_cache_keys(jax.random.fold_in(jax.random.fold_in(key_of[9], part), 71), part)
    cache_values = gaussian(part_splits[2], (HEADS, CTX, HD), 1.0, 6.0, ((0, 16),))
    query_positions = draw_query_positions(jax.random.fold_in(jax.random.fold_in(key_of[9], part), 71), part)
    out_weight = gaussian_with(key_of[4], (HEADS * HD, D), HD ** -0.5, 0.75, ((0, 16),), (0, 1, 16, 2.0))
    residual = draw_residual(jax.random.fold_in(jax.random.fold_in(key_of[9], part), 71), part)
    scale_table = with_ends(jax.random.randint(key_of[6], (2, D // ROT), 2, 128), jax.random.fold_in(key_of[6], 1), 2, 127).astype(jnp.int32)
    norm_gain = jnp.clip(1.0 + 0.18 * jax.random.normal(key_of[7], (D,), jnp.float32), 0.099609375, 1.8984375).astype(jnp.bfloat16)
    next_query_weight = gaussian(key_of[8], (D, HEADS * HD), D ** -0.5, 0.046875, ((1, 16),))
    return {"queries": queries, "cache_keys": cache_keys, "cache_values": cache_values, "query_positions": query_positions, "out_weight": out_weight, "residual": residual, "scale_table": scale_table, "norm_gain": norm_gain, "next_query_weight": next_query_weight}


def sylvester(length):
    row_ids = lax.broadcasted_iota(jnp.int32, (length, length), 0)
    col_ids = lax.broadcasted_iota(jnp.int32, (length, length), 1)
    common_bits = jnp.bitwise_and(row_ids, col_ids)
    parity = jnp.zeros((length, length), jnp.int32)
    for bit_index in range(length.bit_length()):
        parity = parity + jnp.bitwise_and(jnp.right_shift(common_bits, bit_index), 1)
    sign_table = 1 - 2 * jnp.bitwise_and(parity, 1)
    return sign_table.astype(jnp.float32) / math.sqrt(length)

def rotate(values_in, rotation):
    leading = values_in.shape[:-1]
    blocks = values_in.reshape(leading + (values_in.shape[-1] // ROT, ROT))
    turned = jnp.einsum('...bi,ij->...bj', blocks, rotation, precision=lax.Precision.HIGHEST)
    return turned.reshape(values_in.shape)

def blockwise(values_in, block_scale):
    leading = values_in.shape[:-1]
    blocks = values_in.reshape(leading + (block_scale.shape[0], ROT))
    return (blocks * block_scale[:, None]).reshape(values_in.shape)

def to_grid(values_in, block_scale):
    leading = values_in.shape[:-1]
    blocks = values_in.reshape(leading + (block_scale.shape[0], ROT))
    clipped = jnp.clip(blocks / block_scale[:, None], -127.0, 127.0)
    return clipped.reshape(values_in.shape).astype(jnp.bfloat16)

def attend(query_rows, key_rows, value_rows, positions):
    scores = jnp.einsum('qd,kd->qk', query_rows.astype(jnp.float32), key_rows.astype(jnp.float32)) / math.sqrt(HD)
    slot_ids = lax.broadcasted_iota(jnp.int32, (1, key_rows.shape[0]), 1)
    scores = jnp.where(slot_ids <= positions[:, None], scores, -jnp.inf)
    largest = lax.optimization_barrier(jnp.max(scores, axis=-1, keepdims=True))
    raised = jnp.exp(scores - largest)
    soft_weights = (raised / lax.optimization_barrier(jnp.sum(raised, axis=-1, keepdims=True))).astype(jnp.bfloat16)
    return jnp.dot(soft_weights, value_rows, preferred_element_type=jnp.float32).astype(jnp.bfloat16)

def reference(queries, cache_keys, cache_values, query_positions, out_weight, residual, scale_table, norm_gain, next_query_weight):
    rotation = sylvester(ROT)
    low_scale = scale_table[0].astype(jnp.float32) / 65536.0
    high_scale = scale_table[1].astype(jnp.float32) / 256.0

    def head_step(running, head_index):
        context = attend(queries[head_index], cache_keys[head_index], cache_values[head_index], query_positions)
        weight_rows = lax.dynamic_slice_in_dim(out_weight, head_index * HD, HD, 0)
        partial_value = jnp.dot(context, weight_rows, preferred_element_type=jnp.float32)
        on_grid = to_grid(rotate(partial_value, rotation), low_scale)
        return (running + on_grid.astype(jnp.float32), None)
    summed, unused = lax.scan(head_step, jnp.zeros((TOK, D), jnp.float32), jnp.arange(HEADS, dtype=jnp.int32))
    stream = residual.astype(jnp.float32) + rotate(blockwise(summed, low_scale), rotation)
    hidden_out = stream.astype(jnp.bfloat16)
    regrid = to_grid(rotate(stream, rotation), high_scale)
    restored = rotate(blockwise(regrid.astype(jnp.float32), high_scale), rotation)
    mean_square = lax.optimization_barrier(jnp.mean(restored * restored, axis=-1, keepdims=True))
    normed = (restored * lax.rsqrt(mean_square + 1e-05) * norm_gain.astype(jnp.float32)).astype(jnp.bfloat16)
    query_next = jnp.dot(normed, next_query_weight, preferred_element_type=jnp.float32).astype(jnp.bfloat16)
    return (hidden_out, query_next)
```

```python
import functools
import math

import jax
import jax.numpy as jnp
import numpy as np
from jax import lax
from jax.experimental import pallas as pl
from jax.experimental.pallas import tpu as pltpu
from jax.sharding import PartitionSpec as P

HD = 128
ROT = 128
OUTER = 4
SUM_ORDER = np.array([[3, 2, 1, 0], [3, 2, 0, 1], [0, 1, 3, 2], [0, 1, 2, 3]], np.int32)
GATHER_ORDER = np.array([[0, 1, 2, 3], [1, 0, 2, 3], [2, 3, 1, 0], [3, 2, 1, 0]], np.int32)

F32 = jnp.float32
BF16 = jnp.bfloat16
MIB = 1024 * 1024


def hadamard(length):
    rows = np.arange(length)
    common = rows[:, None] & rows[None, :]
    parity = np.zeros((length, length), np.int64)
    for bit in range(length.bit_length()):
        parity += (common >> bit) & 1
    return (1 - 2 * (parity & 1)).astype(np.float32)


def params(limit=24):
    return pltpu.CompilerParams(vmem_limit_bytes=limit * MIB)


def cost(flops, nbytes, exps=0):
    return pl.CostEstimate(flops=int(flops), bytes_accessed=int(nbytes), transcendentals=int(exps))


def vmem():
    return pl.BlockSpec(memory_space=pltpu.VMEM)


def smem():
    return pl.BlockSpec(memory_space=pltpu.SMEM)


def select_cols_kernel(blocks, cols, info, w_ref, out_ref, sem):
    other = 1 - info[10]
    copies = []
    for j in range(blocks):
        start = pl.multiple_of((2 * j + other) * cols, 128)
        copies.append(
            pltpu.make_async_copy(w_ref.at[:, pl.ds(start, cols)], out_ref.at[j], sem.at[j])
        )
    for copy in copies:
        copy.start()
    for copy in copies:
        copy.wait()


def select_cols(info, weight, blocks, cols):
    rows = weight.shape[0]
    return pl.pallas_call(
        functools.partial(select_cols_kernel, blocks, cols),
        out_shape=jax.ShapeDtypeStruct((blocks, rows, cols), weight.dtype),
        in_specs=[smem(), pl.BlockSpec(memory_space=pl.ANY)],
        out_specs=pl.BlockSpec(memory_space=pl.ANY),
        scratch_shapes=[pltpu.SemaphoreType.DMA((blocks,))],
        cost_estimate=cost(0, 4 * blocks * rows * cols),
        compiler_params=params(4),
        name="select_cols",
    )(info, weight)


def select_rows_kernel(blocks, cols, info, w_ref, out_ref, sem):
    other = 1 - info[10]
    copies = []
    for j in range(blocks):
        start = pl.multiple_of((2 * j + other) * cols, 128)
        copies.append(
            pltpu.make_async_copy(w_ref.at[pl.ds(start, cols)], out_ref.at[j], sem.at[j])
        )
    for copy in copies:
        copy.start()
    for copy in copies:
        copy.wait()


def select_rows(info, weight, blocks, cols):
    return pl.pallas_call(
        functools.partial(select_rows_kernel, blocks, cols),
        out_shape=jax.ShapeDtypeStruct((blocks, cols, weight.shape[1]), weight.dtype),
        in_specs=[smem(), pl.BlockSpec(memory_space=pl.ANY)],
        out_specs=pl.BlockSpec(memory_space=pl.ANY),
        scratch_shapes=[pltpu.SemaphoreType.DMA((blocks,))],
        cost_estimate=cost(0, 4 * blocks * cols * weight.shape[1]),
        compiler_params=params(4),
        name="select_rows",
    )(info, weight)


def attend_kernel(steps, chunk, q_ref, k_ref, v_ref, pos_ref, out_ref, m_ref, l_ref, acc_ref):
    step = pl.program_id(0)
    tok = q_ref.shape[0]

    @pl.when(step == 0)
    def _():
        m_ref[...] = jnp.full_like(m_ref, -jnp.inf)
        l_ref[...] = jnp.zeros_like(l_ref)
        acc_ref[...] = jnp.zeros_like(acc_ref)

    positions = jnp.broadcast_to(pos_ref[...].astype(F32), (tok, tok)).T[:, :1]
    scores = lax.dot_general(
        q_ref[...], k_ref[...], (((1,), (1,)), ((), ())), preferred_element_type=F32
    )
    slots = lax.broadcasted_iota(jnp.int32, (tok, chunk), 1) + step * chunk
    scores = jnp.where(slots <= positions.astype(jnp.int32), scores, -jnp.inf)
    before = m_ref[:, :1]
    largest = jnp.maximum(before, jnp.max(scores, axis=1, keepdims=True))
    factor = math.log2(math.e) / math.sqrt(HD)
    raised = jnp.exp2((scores - largest) * factor)
    shrink = jnp.exp2((before - largest) * factor)
    total = l_ref[:, :1] * shrink + jnp.sum(raised, axis=1, keepdims=True)
    acc = acc_ref[...] * shrink + jnp.dot(
        raised.astype(BF16), v_ref[...], preferred_element_type=F32
    )
    m_ref[...] = jnp.broadcast_to(largest, m_ref.shape)
    l_ref[...] = jnp.broadcast_to(total, l_ref.shape)
    acc_ref[...] = acc

    @pl.when(step == steps - 1)
    def _():
        out_ref[...] = (acc / total).astype(BF16)


def attend(queries, keys, values, positions):
    tok = queries.shape[0]
    slots = keys.shape[0]
    chunk = min(2048, slots)
    steps = slots // chunk
    return pl.pallas_call(
        functools.partial(attend_kernel, steps, chunk),
        out_shape=jax.ShapeDtypeStruct((tok, HD), BF16),
        grid=(steps,),
        in_specs=[
            pl.BlockSpec((tok, HD), lambda i: (0, 0)),
            pl.BlockSpec((chunk, HD), lambda i: (i, 0)),
            pl.BlockSpec((chunk, HD), lambda i: (i, 0)),
            pl.BlockSpec((1, tok), lambda i: (0, 0)),
        ],
        out_specs=pl.BlockSpec((tok, HD), lambda i: (0, 0)),
        scratch_shapes=[pltpu.VMEM((tok, HD), F32)] * 3,
        cost_estimate=cost(4 * tok * slots * HD, 4 * slots * HD, tok * slots),
        compiler_params=params(),
        name="attend",
    )(queries, keys, values, positions[None, :])


def turn_out_kernel(inner, cols, info, scales, own_ref, other_ref, h_ref, out_ref):
    shard = pl.program_id(0) * 2 + info[10]
    for i in range(cols // ROT):
        scale = scales[0, shard * (cols // ROT) + i].astype(F32)
        factor = (65536.0 / math.sqrt(ROT)) / jnp.full((1, ROT), scale, F32)
        part = slice(i * ROT, (i + 1) * ROT)
        for head, ref in enumerate((own_ref, other_ref.at[0])):
            turned = jnp.dot(ref[:, part], h_ref[...], preferred_element_type=F32)
            out_ref[0, head, :, part] = (turned * factor).astype(BF16)


def turn_out(info, scales, weight, other, had):
    blocks, rows, cols = other.shape
    return pl.pallas_call(
        functools.partial(turn_out_kernel, blocks // OUTER, cols),
        out_shape=jax.ShapeDtypeStruct((blocks, 2, rows, cols), BF16),
        grid_spec=pltpu.PrefetchScalarGridSpec(
            num_scalar_prefetch=2,
            grid=(blocks,),
            in_specs=[
                pl.BlockSpec((rows, cols), lambda j, info, scales: (0, 2 * j + info[10])),
                pl.BlockSpec((1, rows, cols), lambda j, info, scales: (j, 0, 0)),
                pl.BlockSpec((ROT, ROT), lambda j, info, scales: (0, 0)),
            ],
            out_specs=pl.BlockSpec((1, 2, rows, cols), lambda j, info, scales: (j, 0, 0, 0)),
        ),
        cost_estimate=cost(4 * blocks * rows * cols * ROT, 8 * blocks * rows * cols),
        compiler_params=params(),
        name="turn_out",
    )(info, scales, weight, other, had)


def partial_kernel(inner, info, own_ref, other_ref, w_ref, keep_ref, *send_refs):
    cols = keep_ref.shape[1]
    step = min(cols, 256)
    for shift in range(inner):
        dest = lax.rem(info[9] + shift, inner)
        for start in range(0, cols, step):
            part = slice(start, start + step)
            total = None
            for head, ctx_ref in enumerate((own_ref, other_ref)):
                value = jnp.dot(ctx_ref[...], w_ref[dest, head, :, part], preferred_element_type=F32)
                value = jnp.clip(value, -127.0, 127.0)
                total = value if total is None else total + value
            if shift == 0:
                keep_ref[:, part] = total
            else:
                send_refs[shift - 1][:, part] = total.astype(BF16)


def partials(phase, info, own, other, weight):
    blocks, _, rows, cols = weight.shape
    inner = blocks // OUTER
    tok = own.shape[0]
    return pl.pallas_call(
        functools.partial(partial_kernel, inner),
        out_shape=[jax.ShapeDtypeStruct((tok, cols), F32)]
        + [jax.ShapeDtypeStruct((tok, cols), BF16)] * (inner - 1),
        grid_spec=pltpu.PrefetchScalarGridSpec(
            num_scalar_prefetch=1,
            grid=(1,),
            in_specs=[
                pl.BlockSpec((tok, rows), lambda j, info: (0, 0)),
                pl.BlockSpec((tok, rows), lambda j, info: (0, 0)),
                pl.BlockSpec((inner, 2, rows, cols), lambda j, info: (info[phase], 0, 0, 0)),
            ],
            out_specs=[pl.BlockSpec((tok, cols), lambda j, info: (0, 0))] * inner,
        ),
        cost_estimate=cost(4 * tok * inner * rows * cols, 4 * inner * rows * cols + 4 * tok * cols * inner),
        compiler_params=params(),
        name="partials",
    )(info, own, other, weight)


def add_kernel(*refs):
    *ins, out_ref = refs
    total = ins[0][...].astype(F32)
    for ref in ins[1:]:
        total = total + ref[...].astype(F32)
    out_ref[...] = total.astype(out_ref.dtype)


def add_up(arrays, dtype=BF16):
    return pl.pallas_call(
        add_kernel,
        out_shape=jax.ShapeDtypeStruct(arrays[0].shape, dtype),
        in_specs=[vmem()] * len(arrays),
        out_specs=vmem(),
        cost_estimate=cost(arrays[0].size * len(arrays), 3 * arrays[0].size * len(arrays)),
        compiler_params=params(),
        name="add_up",
    )(*arrays)


def turn_residual_kernel(res_ref, h_ref, out_ref):
    for i in range(res_ref.shape[1] // ROT):
        part = slice(i * ROT, (i + 1) * ROT)
        turned = jnp.dot(res_ref[:, part], h_ref[...], preferred_element_type=F32)
        out_ref[:, part] = turned * (1.0 / math.sqrt(ROT))


def turn_residual(residual, had):
    return pl.pallas_call(
        turn_residual_kernel,
        out_shape=jax.ShapeDtypeStruct(residual.shape, F32),
        in_specs=[vmem()] * 2,
        out_specs=vmem(),
        cost_estimate=cost(2 * residual.size * ROT, 6 * residual.size),
        compiler_params=params(),
        name="turn_residual",
    )(residual, had)


def regrid_kernel(count, *refs):
    info, scales, turned_ref = refs[:3]
    ins = refs[3 : 3 + count]
    grid_ref, low_ref = refs[3 + count :]
    cols = turned_ref.shape[1]
    for i in range(cols // ROT):
        block = info[11] * (cols // ROT) + i
        low = jnp.full((1, ROT), scales[0, block].astype(F32), F32) * (1.0 / 65536.0)
        high = 256.0 / jnp.full((1, ROT), scales[1, block].astype(F32), F32)
        part = slice(i * ROT, (i + 1) * ROT)
        total = ins[0][:, part].astype(F32)
        for ref in ins[1:]:
            total = total + ref[:, part].astype(F32)
        total = total * low
        low_ref[:, part] = total
        value = (turned_ref[:, part] + total) * high
        grid_ref[:, part] = jnp.clip(value, -127.0, 127.0).astype(BF16)


def regrid(info, scales, turned, arrays):
    return pl.pallas_call(
        functools.partial(regrid_kernel, len(arrays)),
        out_shape=[
            jax.ShapeDtypeStruct(turned.shape, BF16),
            jax.ShapeDtypeStruct(turned.shape, F32),
        ],
        in_specs=[smem(), smem()] + [vmem()] * (1 + len(arrays)),
        out_specs=[vmem(), vmem()],
        cost_estimate=cost(8 * turned.size, 16 * turned.size),
        compiler_params=params(),
        name="regrid",
    )(info, scales, turned, *arrays)


def hidden_kernel(res_ref, low_ref, h_ref, out_ref):
    for i in range(res_ref.shape[1] // ROT):
        part = slice(i * ROT, (i + 1) * ROT)
        value = low_ref[:, part]
        upper = value.astype(BF16)
        lower = (value - upper.astype(F32)).astype(BF16)
        turned = jnp.dot(upper, h_ref[...], preferred_element_type=F32)
        turned = turned + jnp.dot(lower, h_ref[...], preferred_element_type=F32)
        stream = res_ref[:, part].astype(F32) + turned * (1.0 / math.sqrt(ROT))
        out_ref[:, part] = stream.astype(BF16)


def hidden(residual, low, had):
    return pl.pallas_call(
        hidden_kernel,
        out_shape=jax.ShapeDtypeStruct(residual.shape, BF16),
        in_specs=[vmem()] * 3,
        out_specs=vmem(),
        cost_estimate=cost(4 * residual.size * ROT, 8 * residual.size),
        compiler_params=params(),
        name="hidden",
    )(residual, low, had)


def turn_next_kernel(cols, info, scales, own_ref, other_ref, gain_ref, h_ref, out_ref):
    shard = pl.program_id(0) * 2 + info[10]
    for i in range(cols // ROT):
        block = shard * (cols // ROT) + i
        scale = jnp.full((1, HD), scales[1, block].astype(F32), F32)
        factor = scale * (1.0 / (256.0 * math.sqrt(ROT)))
        rotation = (h_ref[...].astype(F32) * gain_ref[pl.ds(block, 1), :]).astype(BF16)
        part = slice(i * ROT, (i + 1) * ROT)
        for half, ref in enumerate((own_ref, other_ref.at[0])):
            turned = jnp.dot(rotation, ref[part, :], preferred_element_type=F32)
            out_ref[0, part, half * HD : (half + 1) * HD] = (turned * factor).astype(BF16)


def turn_next(info, scales, weight, other, gain, had):
    blocks, cols, width = other.shape
    return pl.pallas_call(
        functools.partial(turn_next_kernel, cols),
        out_shape=jax.ShapeDtypeStruct((blocks, cols, 2 * width), BF16),
        grid_spec=pltpu.PrefetchScalarGridSpec(
            num_scalar_prefetch=2,
            grid=(blocks,),
            in_specs=[
                pl.BlockSpec((cols, width), lambda j, info, scales: (2 * j + info[10], 0)),
                pl.BlockSpec((1, cols, width), lambda j, info, scales: (j, 0, 0)),
                pl.BlockSpec(gain.shape, lambda j, info, scales: (0, 0)),
                pl.BlockSpec((ROT, ROT), lambda j, info, scales: (0, 0)),
            ],
            out_specs=pl.BlockSpec((1, cols, 2 * width), lambda j, info, scales: (j, 0, 0)),
        ),
        cost_estimate=cost(4 * blocks * cols * width * ROT, 8 * blocks * cols * width),
        compiler_params=params(),
        name="turn_next",
    )(info, scales, weight, other, gain, had)


def project_kernel(inner, groups, has_acc, *refs):
    info, scales = refs[:2]
    refs = refs[2:]
    weights = refs[: len(groups)]
    refs = refs[len(groups) :]
    acc_in = refs[0] if has_acc else None
    refs = refs[1:] if has_acc else refs
    out_ref = refs[-1]
    refs = refs[:-1]
    cols = weights[0].shape[1]
    width = weights[0].shape[2]
    acc = acc_in[:, :width] if has_acc else 0.0
    squares = acc_in[:, width:] if has_acc else 0.0
    at = 0
    for w_ref, (phase, shift, count) in zip(weights, groups):
        values = refs[at][...]
        for ref in refs[at + 1 : at + count]:
            values = values + ref[...]
        at += count
        acc = acc + jnp.dot(values, w_ref[0], preferred_element_type=F32)
        source = lax.rem(info[9] + inner - shift, inner)
        shard = (info[4 + phase] * inner + source) * 2 + info[10]
        for i in range(cols // ROT):
            scale = scales[1, shard * (cols // ROT) + i].astype(F32)
            high = jnp.full((1, ROT), scale, F32) * (1.0 / 256.0)
            value = values[:, i * ROT : (i + 1) * ROT].astype(F32) * high
            squares = squares + value * value
    out_ref[:, :width] = acc
    out_ref[:, width:] = squares


def project(info, scales, weight, acc, pieces):
    blocks, cols, width = weight.shape
    inner = blocks // OUTER
    tok = pieces[0][2][0].shape[0]
    groups = tuple((phase, shift, len(arrays)) for phase, shift, arrays in pieces)

    def at(phase, shift):
        def index(j, info, scales):
            return (info[4 + phase] * inner + lax.rem(info[9] + inner - shift, inner), 0, 0)

        return index

    arrays = [array for _, _, group in pieces for array in group]
    accs = [] if acc is None else [acc]
    return pl.pallas_call(
        functools.partial(project_kernel, inner, groups, acc is not None),
        out_shape=jax.ShapeDtypeStruct((tok, width + ROT), F32),
        grid_spec=pltpu.PrefetchScalarGridSpec(
            num_scalar_prefetch=2,
            grid=(1,),
            in_specs=[pl.BlockSpec((1, cols, width), at(phase, shift)) for phase, shift, _ in groups]
            + [pl.BlockSpec((tok, width + ROT), lambda j, info, scales: (0, 0))] * len(accs)
            + [pl.BlockSpec((tok, cols), lambda j, info, scales: (0, 0))] * len(arrays),
            out_specs=pl.BlockSpec((tok, width + ROT), lambda j, info, scales: (0, 0)),
        ),
        cost_estimate=cost(2 * len(groups) * tok * cols * width, len(groups) * cols * (width + tok) * 2),
        compiler_params=params(),
        name="project",
    )(info, scales, *([weight] * len(groups)), *accs, *arrays)


def finish_kernel(features, acc_ref, other_ref, out_ref):
    squares = acc_ref[:, 2 * HD :] + other_ref[:, HD:]
    mean = jnp.sum(squares, axis=1, keepdims=True) * (1.0 / features)
    value = (acc_ref[:, :HD] + other_ref[:, :HD]) * lax.rsqrt(mean + 1e-05)
    out_ref[...] = value.astype(BF16)


def finish(acc, other, features):
    tok = acc.shape[0]
    return pl.pallas_call(
        functools.partial(finish_kernel, features),
        out_shape=jax.ShapeDtypeStruct((tok, HD), BF16),
        in_specs=[vmem()] * 2,
        out_specs=vmem(),
        cost_estimate=cost(4 * tok * HD, 4 * acc.size * 2),
        compiler_params=params(),
        name="finish",
    )(acc, other)


def body(
    size,
    queries,
    cache_keys,
    cache_values,
    query_positions,
    out_weight,
    residual,
    scale_table,
    norm_gain,
    next_query_weight,
):
    inner = size // (2 * OUTER)
    blocks = OUTER * inner
    cols = residual.shape[1]
    index = lax.axis_index("tp").astype(jnp.int32)
    core = lax.rem(index, 2)
    mid = lax.rem(index // 2, inner)
    outer = index // (2 * inner)
    info = jnp.concatenate(
        [
            lax.dynamic_index_in_dim(jnp.asarray(SUM_ORDER), outer, 0, False),
            lax.dynamic_index_in_dim(jnp.asarray(GATHER_ORDER), outer, 0, False),
            jnp.stack([outer, mid, core, index]),
        ]
    )
    had = jnp.asarray(hadamard(ROT), BF16)

    def number(a, b, c):
        return (a * inner + b) * 2 + c

    def permute(value, moves):
        return lax.ppermute(value, "tp", moves)

    def swap_core(value):
        return permute(value, [(i, i ^ 1) for i in range(size)])

    def shift_mid(value, shift, outers=range(OUTER)):
        return permute(
            value,
            [
                (number(a, b, c), number(a, (b + shift) % inner, c))
                for a in outers
                for b in range(inner)
                for c in range(2)
            ],
        )

    def along(value, hops):
        return permute(
            value,
            [(number(f, b, c), number(t, b, c)) for f, t in hops for b in range(inner) for c in range(2)],
        )

    inward = [(0, 1), (3, 2)]
    outward = [(1, 0), (2, 3)]
    middle = [(1, 2), (2, 1)]

    out_other = swap_core(select_cols(info, out_weight, blocks, cols))
    context = attend(queries[0], cache_keys[0], cache_values[0], query_positions)
    context_other = swap_core(context)
    turned_out = turn_out(info, scale_table, out_weight, out_other, had)

    keeps, arrived = [], []
    for phase in range(OUTER):
        keep, *sends = partials(phase, info, context, context_other, turned_out)
        keeps.append(keep)
        arrived.append([shift_mid(send, s + 1) for s, send in enumerate(sends)])
    first = add_up([keeps[0], *arrived[0]])
    end1 = along(first, inward)
    second = add_up([keeps[1], *arrived[1]])
    end2 = along(second, inward)
    mid2 = along(add_up([keeps[0], *arrived[0], end1]), middle)
    mid3 = along(add_up([keeps[1], *arrived[1], end2]), middle)
    swap3 = along(add_up([keeps[2], *arrived[2], mid2]), inward + outward)

    turned_residual = turn_residual(residual, had)
    grid, low = regrid(
        info, scale_table, turned_residual, [keeps[3], *arrived[3], swap3, mid3]
    )

    next_other = swap_core(select_rows(info, next_query_weight, blocks, cols))
    gain = norm_gain.astype(F32).reshape(-1, ROT)
    turned_next = turn_next(info, scale_table, next_query_weight, next_other, gain, had)

    shifts = range(1, inner)
    ends, inners = (0, 3), (1, 2)
    x1 = [shift_mid(grid, s) for s in shifts]
    near = along(grid, inward + outward)
    mid1 = along(grid, middle)
    x2 = [shift_mid(near, s) for s in shifts]
    end2 = along(mid1, outward)
    mid2 = along(near, middle)
    x3 = [(shift_mid(end2, s, ends), shift_mid(mid1, s, inners)) for s in shifts]
    end3 = along(mid2, outward)
    x4 = [(shift_mid(end3, s, ends), shift_mid(mid2, s, inners)) for s in shifts]

    hidden_out = hidden(residual, low, had)
    acc = project(
        info,
        scale_table,
        turned_next,
        None,
        [(0, 0, [grid]), (1, 0, [near])] + [(0, s, [x1[s - 1]]) for s in shifts],
    )
    acc = project(
        info,
        scale_table,
        turned_next,
        acc,
        [(2, 0, [end2, mid1])] + [(1, s, [x2[s - 1]]) for s in shifts],
    )
    acc = project(
        info,
        scale_table,
        turned_next,
        acc,
        [(3, 0, [end3, mid2])] + [(2, s, list(x3[s - 1])) for s in shifts],
    )
    acc = project(info, scale_table, turned_next, acc, [(3, s, list(x4[s - 1])) for s in shifts])
    other = swap_core(acc[:, HD:])
    query_next = finish(acc, other, norm_gain.shape[0])
    return (hidden_out, query_next)


def solution(mesh):
    placed = (
        P("tp", "groups", None),
        P("tp", "groups", None),
        P("tp", "groups", None),
        P("groups"),
        P("tp", None),
        P("groups", "tp"),
        P(),
        P(),
        P(None, "tp"),
    )
    return jax.shard_map(
        functools.partial(body, mesh.shape["tp"]),
        mesh=mesh,
        in_specs=placed,
        out_specs=(P("groups", "tp"), P("groups", "tp")),
        check_vma=False,
    )
```

```python
import functools
import math

import jax
import jax.numpy as jnp
import numpy as np
from jax import lax
from jax.experimental import pallas as pl
from jax.experimental.pallas import tpu as pltpu
from jax.sharding import PartitionSpec as P

HD = 128
ROT = 128
OUTER = 4

F32 = jnp.float32
BF16 = jnp.bfloat16
MIB = 1024 * 1024


def hadamard(length):
    rows = np.arange(length)
    common = rows[:, None] & rows[None, :]
    parity = np.zeros((length, length), np.int64)
    for bit in range(length.bit_length()):
        parity += (common >> bit) & 1
    return (1 - 2 * (parity & 1)).astype(np.float32)


def vmem():
    return pl.BlockSpec(memory_space=pltpu.VMEM)


def anywhere():
    return pl.BlockSpec(memory_space=pl.ANY)


def place(inner):
    index = lax.axis_index("tp")
    return lax.div(index, 2 * inner), lax.rem(lax.div(index, 2), inner), lax.rem(index, 2)


def targets(outer):
    low = outer < 2
    near = outer + 1 - 2 * lax.rem(outer, 2)
    return jnp.where(low, 3, 0), jnp.where(low, 2, 1), near, outer


def is_inner(outer):
    return jnp.logical_or(outer == 1, outer == 2)


def kernel_call(kernel, out_shape, arrays, specs, after=(), scratch=(), flops=0, nbytes=0, exps=0, limit=24, name=None):
    count, extra = len(arrays), len(after)

    def ordered(*refs):
        kernel(*refs[:count], *refs[count + extra :])

    return pl.pallas_call(
        ordered,
        out_shape=out_shape,
        in_specs=list(specs) + [anywhere()] * extra,
        out_specs=jax.tree.map(lambda _: vmem(), out_shape),
        scratch_shapes=list(scratch),
        cost_estimate=pl.CostEstimate(
            flops=int(flops), bytes_accessed=int(nbytes), transcendentals=int(exps)
        ),
        compiler_params=pltpu.CompilerParams(vmem_limit_bytes=limit * MIB),
        name=name,
    )(*arrays, *after)


def gridded(context, h_ref, weight, scale_row, store):
    cols = weight.shape[1]
    count = cols // ROT
    value = jnp.dot(context, weight, preferred_element_type=F32).astype(BF16)
    stacked = jnp.concatenate([value[:, i * ROT : (i + 1) * ROT] for i in range(count)], axis=0)
    turned = jnp.dot(stacked, h_ref[...], preferred_element_type=F32)
    tok = value.shape[0]
    for i in range(count):
        part = turned[i * tok : (i + 1) * tok] * scale_row(i)
        store(i, jnp.clip(part, -127.0, 127.0).astype(BF16))


def attend_kernel(
    inner, cols, chunk, q_hbm, k_hbm, v_hbm, w_hbm, pos_ref, table_ref, h_ref,
    ctx_ref, rows_ref, send_ref, k_ref, v_ref, w_ref, s_ref, q_ref, sems,
):
    tok = q_ref.shape[0]
    slots = k_ref.shape[0]
    steps = slots // chunk
    outer, mid, core = place(inner)
    dest = targets(outer)[0]

    def copy_k(j):
        part = pl.ds(j * chunk, chunk)
        return pltpu.make_async_copy(k_hbm.at[0, part], k_ref.at[part], sems.at[1 + j])

    def copy_v(j):
        part = pl.ds(j * chunk, chunk)
        return pltpu.make_async_copy(v_hbm.at[0, part], v_ref.at[part], sems.at[1 + steps + j])

    def shard_of(shift):
        return (dest * inner + lax.rem(mid + shift, inner)) * 2 + 1 - core

    def copy_w(shift):
        start = pl.multiple_of(shard_of(shift) * cols, 128)
        return pltpu.make_async_copy(
            w_hbm.at[:, pl.ds(start, cols)], w_ref.at[shift - 1], sems.at[2 * steps + shift]
        )

    copy_q = pltpu.make_async_copy(q_hbm.at[0], q_ref, sems.at[0])
    copy_q.start()
    for j in range(steps):
        copy_k(j).start()
    for j in range(steps):
        copy_v(j).start()
    for shift in range(1, inner):
        copy_w(shift).start()

    table = table_ref[...].astype(F32)
    count = table.shape[1]
    for i in range(2):
        rows_ref[i] = jnp.broadcast_to(table[i : i + 1], (ROT, count)).T
    positions = jnp.broadcast_to(pos_ref[...].astype(F32), (ROT, tok)).T
    ahead = positions.astype(jnp.int32) - lax.broadcasted_iota(jnp.int32, (tok, ROT), 1)

    copy_q.wait()
    queries = q_ref[...]
    peak = jnp.full((tok, ROT), -jnp.inf, F32)
    for j in range(steps):
        copy_k(j).wait()
        scores = lax.dot_general(
            queries, k_ref[j * chunk : (j + 1) * chunk], (((1,), (1,)), ((), ())),
            preferred_element_type=F32,
        )
        for i in range(chunk // ROT):
            base = j * chunk + i * ROT
            part = jnp.where(ahead >= base, scores[:, i * ROT : (i + 1) * ROT], -jnp.inf)
            s_ref[:, base : base + ROT] = part
            peak = jnp.maximum(peak, part)
    largest = jnp.max(peak, axis=1, keepdims=True)
    factor = math.log2(math.e) / math.sqrt(HD)
    total = jnp.zeros((tok, ROT), F32)
    acc = jnp.zeros((tok, HD), F32)
    for j in range(steps):
        copy_v(j).wait()
        pieces = []
        for i in range(chunk // ROT):
            base = j * chunk + i * ROT
            raised = jnp.exp2((s_ref[:, base : base + ROT] - largest) * factor)
            total = total + raised
            pieces.append(raised.astype(BF16))
        acc = acc + jnp.dot(
            jnp.concatenate(pieces, axis=1), v_ref[j * chunk : (j + 1) * chunk],
            preferred_element_type=F32,
        )
    context = (acc / jnp.sum(total, axis=1, keepdims=True)).astype(BF16)
    ctx_ref[...] = context

    per = cols // ROT
    for shift in range(1, inner):
        copy_w(shift).wait()
        first = shard_of(shift) * per

        def scale_row(i):
            return (65536.0 / math.sqrt(ROT)) / rows_ref[0, pl.ds(first + i, 1), :]

        def store(i, value):
            send_ref[shift - 1, :, i * ROT : (i + 1) * ROT] = value

        gridded(context, h_ref, w_ref[shift - 1], scale_row, store)


def attend(inner, cols, queries, keys, values, weight, positions, table, had):
    tok, slots = queries.shape[1], keys.shape[1]
    chunk = min(1024, slots)
    steps = slots // chunk
    blocks = table.shape[1]
    return kernel_call(
        functools.partial(attend_kernel, inner, cols, chunk),
        [
            jax.ShapeDtypeStruct((tok, HD), BF16),
            jax.ShapeDtypeStruct((2, blocks, ROT), F32),
            jax.ShapeDtypeStruct((inner - 1, tok, cols), BF16),
        ],
        [queries, keys, values, weight, positions[None, :], table, had],
        [pl.BlockSpec(memory_space=pltpu.HBM)] * 4 + [vmem()] * 3,
        scratch=[
            pltpu.VMEM((slots, HD), BF16),
            pltpu.VMEM((slots, HD), BF16),
            pltpu.VMEM((inner - 1, weight.shape[0], cols), BF16),
            pltpu.VMEM((tok, slots), F32),
            pltpu.VMEM((tok, HD), BF16),
            pltpu.SemaphoreType.DMA((2 * steps + inner,)),
        ],
        flops=4 * tok * slots * HD,
        nbytes=4 * slots * HD,
        exps=tok * slots,
        limit=28,
        name="attend",
    )


def partial_kernel(inner, work, ctx_ref, w_ref, rows_ref, h_ref, *out_refs):
    cols = out_refs[0].shape[2]
    per = cols // ROT
    outer, mid, core = place(inner)
    dests = targets(outer)
    context = ctx_ref[...]
    for out_ref, (mine, blocks) in zip(out_refs, work):
        for at, (phase, shift) in enumerate(blocks):
            shard = (dests[phase] * inner + lax.rem(mid + shift, inner)) * 2
            shard = shard + (core if mine else 1 - core)

            def scale_row(i):
                return (65536.0 / math.sqrt(ROT)) / rows_ref[0, pl.ds(shard * per + i, 1), :]

            def store(i, value):
                out_ref[at, :, i * ROT : (i + 1) * ROT] = value

            start = pl.multiple_of(shard * cols, 128)
            gridded(context, h_ref, w_ref[:, pl.ds(start, cols)], scale_row, store)


def partials(inner, cols, work, context, weight, rows, had, after=()):
    tok = context.shape[0]
    count = sum(len(blocks) for _, blocks in work)
    return kernel_call(
        functools.partial(partial_kernel, inner, work),
        [jax.ShapeDtypeStruct((len(blocks), tok, cols), BF16) for _, blocks in work],
        [context, weight, rows, had],
        [vmem()] * 4,
        after=after,
        flops=4 * count * tok * HD * cols,
        nbytes=2 * count * (tok + HD) * cols,
        name="partials",
    )


def add_kernel(inner, inputs, outputs, *refs):
    ins, outs = refs[:inputs], refs[inputs:]
    outer = place(inner)[0]
    for out_ref, items in zip(outs, outputs):
        total = None
        for which, at, inner_only in items:
            value = (ins[which][...] if at is None else ins[which][at]).astype(F32)
            if inner_only:
                value = jnp.where(is_inner(outer), value, 0.0)
            total = value if total is None else total + value
        out_ref[...] = total.astype(BF16)


def add_up(inner, arrays, outputs, after=()):
    shape = arrays[0].shape[-2:]
    terms = sum(len(items) for items in outputs)
    return kernel_call(
        functools.partial(add_kernel, inner, len(arrays), outputs),
        [jax.ShapeDtypeStruct(shape, BF16)] * len(outputs),
        arrays,
        [vmem()] * len(arrays),
        after=after,
        flops=terms * shape[0] * shape[1],
        nbytes=2 * (terms + len(outputs)) * shape[0] * shape[1],
        name="add_up",
    )


def turn_residual_kernel(inner, res_ref, rows_ref, h_ref, out_ref, factor_ref):
    per = res_ref.shape[1] // ROT
    first = lax.axis_index("tp") * per
    for i in range(per):
        part = slice(i * ROT, (i + 1) * ROT)
        high = 256.0 / rows_ref[1, pl.ds(first + i, 1), :]
        low = rows_ref[0, pl.ds(first + i, 1), :] * (1.0 / 65536.0)
        turned = jnp.dot(res_ref[:, part], h_ref[...], preferred_element_type=F32)
        out_ref[:, part] = turned * (high * (1.0 / math.sqrt(ROT)))
        factor_ref[0:1, part] = low * high
        factor_ref[1:2, part] = low


def turn_residual(inner, residual, rows, had, after=()):
    return kernel_call(
        functools.partial(turn_residual_kernel, inner),
        [
            jax.ShapeDtypeStruct(residual.shape, F32),
            jax.ShapeDtypeStruct((2, residual.shape[1]), F32),
        ],
        [residual, rows, had],
        [vmem()] * 3,
        after=after,
        flops=2 * residual.size * ROT,
        nbytes=6 * residual.size,
        name="turn_residual",
    )


def summed_at(inner, items, ins, part):
    outer = place(inner)[0]
    total = None
    for (at, inner_only), ref in zip(items, ins):
        value = (ref[:, part] if at is None else ref[at, :, part]).astype(F32)
        if inner_only:
            value = jnp.where(is_inner(outer), value, 0.0)
        total = value if total is None else total + value
    return total


def regrid_kernel(inner, items, turned_ref, factor_ref, *refs):
    *ins, grid_ref = refs
    for i in range(turned_ref.shape[1] // ROT):
        part = slice(i * ROT, (i + 1) * ROT)
        value = turned_ref[:, part] + summed_at(inner, items, ins, part) * factor_ref[0:1, part]
        grid_ref[:, part] = jnp.clip(value, -127.0, 127.0).astype(BF16)


def regrid(inner, items, turned, factors, arrays, after=()):
    return kernel_call(
        functools.partial(regrid_kernel, inner, items),
        jax.ShapeDtypeStruct(turned.shape, BF16),
        [turned, factors, *arrays],
        [vmem()] * (2 + len(arrays)),
        after=after,
        flops=8 * turned.size,
        nbytes=16 * turned.size,
        name="regrid",
    )


def hidden_kernel(inner, items, res_ref, factor_ref, h_ref, *refs):
    *ins, out_ref = refs
    for i in range(res_ref.shape[1] // ROT):
        part = slice(i * ROT, (i + 1) * ROT)
        value = summed_at(inner, items, ins, part) * factor_ref[1:2, part]
        upper = value.astype(BF16)
        lower = (value - upper.astype(F32)).astype(BF16)
        turned = jnp.dot(upper, h_ref[...], preferred_element_type=F32)
        turned = turned + jnp.dot(lower, h_ref[...], preferred_element_type=F32)
        stream = res_ref[:, part].astype(F32) + turned * (1.0 / math.sqrt(ROT))
        out_ref[:, part] = stream.astype(BF16)


def hidden(inner, items, residual, factors, had, arrays, after=()):
    return kernel_call(
        functools.partial(hidden_kernel, inner, items),
        jax.ShapeDtypeStruct(residual.shape, BF16),
        [residual, factors, had, *arrays],
        [vmem()] * (3 + len(arrays)),
        after=after,
        flops=4 * residual.size * ROT,
        nbytes=12 * residual.size,
        name="hidden",
    )


def choose_kernel(inner, inner_ref, end_ref, out_ref):
    inside = is_inner(place(inner)[0])

    @pl.when(inside)
    def _():
        out_ref[...] = inner_ref[...]

    @pl.when(jnp.logical_not(inside))
    def _():
        out_ref[...] = end_ref[...]


def choose(inner, at_inner, at_end, after=()):
    return kernel_call(
        functools.partial(choose_kernel, inner),
        jax.ShapeDtypeStruct(at_inner.shape, at_inner.dtype),
        [at_inner, at_end],
        [vmem()] * 2,
        after=after,
        nbytes=4 * at_inner.size,
        name="choose",
    )


def select_rows_kernel(inner, cols, w_ref, out_ref):
    other = 1 - place(inner)[2]
    for j in range(out_ref.shape[0]):
        start = pl.multiple_of((2 * j + other) * cols, 128)
        out_ref[j] = w_ref[pl.ds(start, cols), :]


def select_rows(inner, weight, cols, after=()):
    blocks = OUTER * inner
    return kernel_call(
        functools.partial(select_rows_kernel, inner, cols),
        jax.ShapeDtypeStruct((blocks, cols, weight.shape[1]), weight.dtype),
        [weight],
        [vmem()],
        after=after,
        nbytes=4 * blocks * cols * weight.shape[1],
        name="select_rows",
    )


def turn_next_kernel(inner, cols, own_ref, other_ref, gain_ref, rows_ref, h_ref, out_ref):
    core = place(inner)[2]
    for j in range(out_ref.shape[0]):
        shard = j * 2 + core
        for i in range(cols // ROT):
            block = shard * (cols // ROT) + i
            factor = rows_ref[1, pl.ds(block, 1), :] * (1.0 / (256.0 * math.sqrt(ROT)))
            rotation = (h_ref[...].astype(F32) * gain_ref[pl.ds(block, 1), :]).astype(BF16)
            part = slice(i * ROT, (i + 1) * ROT)
            own = own_ref[pl.ds(pl.multiple_of(block * ROT, ROT), ROT), :]
            for half, value in enumerate((own, other_ref[j, part, :])):
                turned = jnp.dot(rotation, value, preferred_element_type=F32)
                out_ref[j, part, half * HD : (half + 1) * HD] = (turned * factor).astype(BF16)


def turn_next(inner, weight, other, gain, rows, had, after=()):
    count, cols, width = other.shape
    return kernel_call(
        functools.partial(turn_next_kernel, inner, cols),
        jax.ShapeDtypeStruct((count, cols, 2 * width), BF16),
        [weight, other, gain, rows, had],
        [vmem()] * 5,
        after=after,
        flops=4 * count * cols * width * ROT,
        nbytes=8 * count * cols * width,
        name="turn_next",
    )


def project_kernel(inner, places, has_acc, split, w_ref, rows_ref, *refs):
    outer, mid, core = place(inner)
    far, third, near, own = targets(outer)
    order = (own, near, third, far)
    acc_in = refs[0] if has_acc else None
    refs = refs[1:] if has_acc else refs
    values_in = refs[: len(places)]
    outs = refs[len(places) :]
    cols, width = w_ref.shape[1:]
    acc = acc_in[:, :width] if has_acc else 0.0
    squares = acc_in[:, width:] if has_acc else 0.0
    for ref, (phase, shift) in zip(values_in, places):
        block = order[phase] * inner + lax.rem(mid + inner - shift, inner)
        values = ref[...]
        acc = acc + jnp.dot(values, w_ref[block], preferred_element_type=F32)
        for i in range(cols // ROT):
            row = (block * 2 + core) * (cols // ROT) + i
            high = rows_ref[1, pl.ds(row, 1), :] * (1.0 / 256.0)
            value = values[:, i * ROT : (i + 1) * ROT].astype(F32) * high
            squares = squares + value * value
    if split:
        own_ref, other_ref = outs
        own_ref[:, :HD] = acc[:, :HD]
        own_ref[:, HD:] = squares
        other_ref[:, :HD] = acc[:, HD:]
        other_ref[:, HD:] = squares
    else:
        outs[0][:, :width] = acc
        outs[0][:, width:] = squares


def project(inner, weight, rows, acc, pieces, split=False, after=()):
    _, cols, width = weight.shape
    arrays = [array for _, _, array in pieces]
    tok = arrays[0].shape[0]
    places = tuple((phase, shift) for phase, shift, _ in pieces)
    accs = [] if acc is None else [acc]
    if split:
        out = [jax.ShapeDtypeStruct((tok, HD + ROT), F32)] * 2
    else:
        out = jax.ShapeDtypeStruct((tok, width + ROT), F32)
    return kernel_call(
        functools.partial(project_kernel, inner, places, acc is not None, split),
        out,
        [weight, rows, *accs, *arrays],
        [vmem()] * (2 + len(accs) + len(arrays)),
        after=after,
        flops=2 * len(places) * tok * cols * width,
        nbytes=2 * len(places) * cols * (width + tok),
        name="project",
    )


def finish_kernel(features, own_ref, other_ref, out_ref):
    squares = own_ref[:, HD:] + other_ref[:, HD:]
    mean = jnp.sum(squares, axis=1, keepdims=True) * (1.0 / features)
    value = (own_ref[:, :HD] + other_ref[:, :HD]) * lax.rsqrt(mean + 1e-05)
    out_ref[...] = value.astype(BF16)


def finish(own, other, features):
    tok = own.shape[0]
    return kernel_call(
        functools.partial(finish_kernel, features),
        jax.ShapeDtypeStruct((tok, HD), BF16),
        [own, other],
        [vmem()] * 2,
        flops=4 * tok * HD,
        nbytes=16 * tok * HD,
        name="finish",
    )


def body(
    size,
    queries,
    cache_keys,
    cache_values,
    query_positions,
    out_weight,
    residual,
    scale_table,
    norm_gain,
    next_query_weight,
):
    inner = size // (2 * OUTER)
    cols = residual.shape[1]
    had = jnp.asarray(hadamard(ROT), BF16)
    shifts = range(1, inner)

    def permute(value, move):
        moves = []
        for i in range(size):
            spot = move(i // (2 * inner), (i // 2) % inner, i % 2)
            moves.append((i, (spot[0] * inner + spot[1]) * 2 + spot[2]))
        return lax.ppermute(value, "tp", moves)

    def swap_core(value):
        return permute(value, lambda a, b, c: (a, b, 1 - c))

    def shift_mid(value, shift):
        return permute(value, lambda a, b, c: (a, (b + shift) % inner, c))

    def swap_pairs(value):
        return permute(value, lambda a, b, c: (a ^ 1, b, c))

    def swap_middle(value):
        return permute(value, lambda a, b, c: ((0, 2, 1, 3)[a], b, c))

    everything = range(inner)
    context, rows, send1 = attend(
        inner, cols, queries, cache_keys, cache_values, out_weight, query_positions, scale_table, had
    )
    other1 = swap_core(send1)
    away1 = tuple((0, s) for s in shifts)
    (keep1,) = partials(inner, cols, ((True, away1),), context, out_weight, rows, had)
    pay1 = add_up(inner, [keep1, other1], [((0, s - 1, False), (1, s - 1, False)) for s in shifts])
    come1 = [shift_mid(pay, s) for s, pay in zip(shifts, pay1)]

    def both(blocks, after):
        work = ((False, blocks), (True, blocks))
        return partials(inner, cols, work, context, out_weight, rows, had, after=after)

    def phase_blocks(phase):
        return tuple((phase, s) for s in everything)

    send2, keep2 = both(((0, 0),) + phase_blocks(1), pay1[:1])
    other2 = swap_core(send2)
    send3, keep3 = both(phase_blocks(2), [keep2])
    other3 = swap_core(send3)

    def pay_out(keep, other, first, after):
        items = [((0, first + s, False), (1, first + s, False)) for s in shifts]
        return add_up(inner, [keep, other], items, after=after)

    pay2 = pay_out(keep2, other2, 1, [keep3])
    come2 = [shift_mid(pay, s) for s, pay in zip(shifts, pay2)]

    n = len(come1)
    sum1 = [(0, 0, False), (1, 0, False)] + [(2 + i, None, False) for i in range(n)]
    sum2 = [(0, 1, False), (1, 1, False)] + [(2 + i, None, False) for i in range(n)]
    relay = [(2 + n, None, True)]
    (end1,) = add_up(inner, [keep2, other2, *come1], [sum1], after=pay2[:1])
    from_end1 = swap_pairs(end1)
    send4, keep4 = both(phase_blocks(3), [end1])
    other4 = swap_core(send4)
    pay3 = pay_out(keep3, other3, 0, [keep4])
    come3 = [shift_mid(pay, s) for s, pay in zip(shifts, pay3)]
    picked = select_rows(inner, next_query_weight, cols, after=pay3[:1])
    next_other = swap_core(picked)
    (end2,) = add_up(inner, [keep2, other2, *come2], [sum2], after=[picked])
    from_end2 = swap_pairs(end2)
    (mid2,) = add_up(inner, [keep2, other2, *come1, from_end1], [sum1 + relay], after=[end2])
    from_mid2 = swap_middle(mid2)
    pay4 = pay_out(keep4, other4, 0, [mid2])
    come4 = [shift_mid(pay, s) for s, pay in zip(shifts, pay4)]
    turned_residual, factors = turn_residual(inner, residual, rows, had, after=pay4[:1])
    gain = norm_gain.astype(F32).reshape(-1, ROT)
    (mid3,) = add_up(
        inner, [keep2, other2, *come2, from_end2], [sum2 + relay], after=[turned_residual]
    )
    from_mid3 = swap_middle(mid3)
    (near3,) = add_up(inner, [keep3, other3, *come3, from_mid2], [sum1 + relay], after=[mid3])
    from_near3 = swap_pairs(near3)
    turned_next = turn_next(inner, next_query_weight, next_other, gain, rows, had, after=[near3])

    last = [keep4, other4, *come4, from_near3, from_mid3]
    items = [(0, False)] * 2 + [(None, False)] * (n + 1) + [(None, True)]
    grid = regrid(inner, items, turned_residual, factors, last, after=[turned_next])

    x1 = [shift_mid(grid, s) for s in shifts]
    near = swap_pairs(grid)
    mid1 = swap_middle(grid)
    x2 = [shift_mid(near, s) for s in shifts]
    ends2 = swap_pairs(mid1)
    mids2 = swap_middle(near)
    acc = project(inner, turned_next, rows, None, [(0, 0, grid)])
    hidden_out = hidden(inner, items, residual, factors, had, last, after=[acc])
    third = choose(inner, mid1, ends2, after=[hidden_out])
    x3 = [shift_mid(third, s) for s in shifts]
    ends3 = swap_pairs(mids2)
    acc = project(
        inner, turned_next, rows, acc, [(1, 0, near)] + [(0, s, x1[s - 1]) for s in shifts], after=[third]
    )
    fourth = choose(inner, mids2, ends3, after=[acc])
    x4 = [shift_mid(fourth, s) for s in shifts]
    acc = project(
        inner, turned_next, rows, acc, [(2, 0, third)] + [(1, s, x2[s - 1]) for s in shifts], after=[fourth]
    )
    acc = project(
        inner, turned_next, rows, acc, [(3, 0, fourth)] + [(2, s, x3[s - 1]) for s in shifts]
    )
    own, other = project(
        inner, turned_next, rows, acc, [(3, s, x4[s - 1]) for s in shifts], split=True
    )
    query_next = finish(own, swap_core(other), norm_gain.shape[0])
    return (hidden_out, query_next)


def solution(mesh):
    placed = (
        P("tp", "groups", None),
        P("tp", "groups", None),
        P("tp", "groups", None),
        P("groups"),
        P("tp", None),
        P("groups", "tp"),
        P(),
        P(),
        P(None, "tp"),
    )
    return jax.shard_map(
        functools.partial(body, mesh.shape["tp"]),
        mesh=mesh,
        in_specs=placed,
        out_specs=(P("groups", "tp"), P("groups", "tp")),
        check_vma=False,
    )
```

```python
import functools
import math

import jax
import jax.numpy as jnp
import numpy as np
from jax import lax
from jax.experimental import pallas as pl
from jax.experimental.pallas import tpu as pltpu
from jax.sharding import PartitionSpec as P

HD = 128
ROT = 128
OUTER = 4

F32 = jnp.float32
BF16 = jnp.bfloat16
MIB = 1024 * 1024


def hadamard(length):
    rows = np.arange(length)
    common = rows[:, None] & rows[None, :]
    parity = np.zeros((length, length), np.int64)
    for bit in range(length.bit_length()):
        parity += (common >> bit) & 1
    return (1 - 2 * (parity & 1)).astype(np.float32)


def vmem():
    return pl.BlockSpec(memory_space=pltpu.VMEM)


def anywhere():
    return pl.BlockSpec(memory_space=pl.ANY)


def place(inner):
    index = lax.axis_index("tp")
    return lax.div(index, 2 * inner), lax.rem(lax.div(index, 2), inner), lax.rem(index, 2)


def targets(outer):
    low = outer < 2
    near = outer + 1 - 2 * lax.rem(outer, 2)
    return jnp.where(low, 3, 0), jnp.where(low, 2, 1), near, outer


def is_inner(outer):
    return jnp.logical_or(outer == 1, outer == 2)


def kernel_call(kernel, out_shape, arrays, specs, after=(), scratch=(), aliases=None, limit=24, name=None):
    count, extra = len(arrays), len(after)

    def ordered(*refs):
        kernel(*refs[:count], *refs[count + extra :])

    return pl.pallas_call(
        ordered,
        out_shape=out_shape,
        in_specs=list(specs) + [anywhere()] * extra,
        out_specs=jax.tree.map(lambda _: vmem(), out_shape),
        scratch_shapes=list(scratch),
        input_output_aliases=aliases or {},
        cost_estimate=pl.CostEstimate(flops=0, bytes_accessed=0, transcendentals=0),
        compiler_params=pltpu.CompilerParams(vmem_limit_bytes=limit * MIB),
        name=name,
    )(*arrays, *after)


def gridded(context, h_ref, weight, scale_row, store):
    cols = weight.shape[1]
    count = cols // ROT
    value = jnp.dot(context, weight, preferred_element_type=F32).astype(BF16)
    stacked = jnp.concatenate([value[:, i * ROT : (i + 1) * ROT] for i in range(count)], axis=0)
    turned = jnp.dot(stacked, h_ref[...], preferred_element_type=F32)
    tok = value.shape[0]
    for i in range(count):
        part = turned[i * tok : (i + 1) * tok] * scale_row(i)
        store(i, jnp.clip(part, -127.0, 127.0).astype(BF16))


def attend_kernel(
    inner, cols, chunk, q_hbm, k_hbm, v_hbm, w_hbm, pos_hbm, table_hbm, h_hbm,
    ctx_ref, rows_ref, send_ref, w_ref, h_ref, k_ref, v_ref, s_ref, q_ref, pos_ref, table_ref, sems,
):
    tok = q_ref.shape[0]
    slots = k_ref.shape[0]
    steps = slots // chunk
    outer, mid, core = place(inner)
    dest = targets(outer)[0]

    def copy_k(j):
        part = pl.ds(j * chunk, chunk)
        return pltpu.make_async_copy(k_hbm.at[0, part], k_ref.at[part], sems.at[1 + j])

    def copy_v(j):
        part = pl.ds(j * chunk, chunk)
        return pltpu.make_async_copy(v_hbm.at[0, part], v_ref.at[part], sems.at[1 + steps + j])

    def shard_of(shift):
        return (dest * inner + lax.rem(mid + shift, inner)) * 2 + 1 - core

    copy_w = pltpu.make_async_copy(w_hbm, w_ref, sems.at[2 * steps + 1])
    copy_q = pltpu.make_async_copy(q_hbm.at[0], q_ref, sems.at[0])
    copy_pos = pltpu.make_async_copy(pos_hbm, pos_ref, sems.at[2 * steps + 2])
    copy_table = pltpu.make_async_copy(table_hbm, table_ref, sems.at[2 * steps + 3])
    copy_h = pltpu.make_async_copy(h_hbm, h_ref, sems.at[2 * steps + 4])
    copy_q.start()
    copy_pos.start()
    for j in range(steps):
        copy_k(j).start()
    copy_table.start()
    copy_h.start()
    for j in range(steps):
        copy_v(j).start()
    copy_w.start()

    copy_pos.wait()
    positions = jnp.broadcast_to(pos_ref[...].astype(F32), (ROT, tok)).T
    ahead = positions.astype(jnp.int32) - lax.broadcasted_iota(jnp.int32, (tok, ROT), 1)

    copy_q.wait()
    queries = q_ref[...]
    peak = jnp.full((tok, ROT), -jnp.inf, F32)
    for j in range(steps):
        copy_k(j).wait()
        scores = lax.dot_general(
            queries, k_ref[j * chunk : (j + 1) * chunk], (((1,), (1,)), ((), ())),
            preferred_element_type=F32,
        )
        for i in range(chunk // ROT):
            base = j * chunk + i * ROT
            part = jnp.where(ahead >= base, scores[:, i * ROT : (i + 1) * ROT], -jnp.inf)
            s_ref[:, base : base + ROT] = part
            peak = jnp.maximum(peak, part)
    copy_table.wait()
    table = table_ref[...].astype(F32)
    count = table.shape[1]
    for i in range(2):
        rows_ref[i] = jnp.broadcast_to(table[i : i + 1], (ROT, count)).T
    largest = jnp.max(peak, axis=1, keepdims=True)
    factor = math.log2(math.e) / math.sqrt(HD)
    total = jnp.zeros((tok, ROT), F32)
    acc = jnp.zeros((tok, HD), F32)
    for j in range(steps):
        copy_v(j).wait()
        pieces = []
        for i in range(chunk // ROT):
            base = j * chunk + i * ROT
            raised = jnp.exp2((s_ref[:, base : base + ROT] - largest) * factor)
            total = total + raised
            pieces.append(raised.astype(BF16))
        acc = acc + jnp.dot(
            jnp.concatenate(pieces, axis=1), v_ref[j * chunk : (j + 1) * chunk],
            preferred_element_type=F32,
        )
    context = (acc / jnp.sum(total, axis=1, keepdims=True)).astype(BF16)
    ctx_ref[...] = context

    per = cols // ROT
    copy_h.wait()
    copy_w.wait()
    for shift in range(1, inner):
        first = shard_of(shift) * per
        start = pl.multiple_of(shard_of(shift) * cols, 128)

        def scale_row(i):
            return (65536.0 / math.sqrt(ROT)) / rows_ref[0, pl.ds(first + i, 1), :]

        def store(i, value):
            send_ref[shift - 1, :, i * ROT : (i + 1) * ROT] = value

        gridded(context, h_ref, w_ref[:, pl.ds(start, cols)], scale_row, store)


def attend(inner, cols, queries, keys, values, weight, positions, table, had):
    tok, slots = queries.shape[1], keys.shape[1]
    chunk = min(1024, slots)
    steps = slots // chunk
    blocks = table.shape[1]
    arrays = [queries, keys, values, weight, positions[None, :], table, had]
    return kernel_call(
        functools.partial(attend_kernel, inner, cols, chunk),
        [
            pltpu.VMEM((tok, HD), BF16),
            pltpu.VMEM((2, blocks, ROT), F32),
            pltpu.VMEM((inner - 1, tok, cols), BF16),
            pltpu.VMEM(weight.shape, BF16),
            pltpu.VMEM(had.shape, BF16),
        ],
        [pltpu.with_memory_space_constraint(array, pltpu.HBM) for array in arrays],
        [pl.BlockSpec(memory_space=pltpu.HBM)] * len(arrays),
        scratch=[
            pltpu.VMEM((slots, HD), BF16),
            pltpu.VMEM((slots, HD), BF16),
            pltpu.VMEM((tok, slots), F32),
            pltpu.VMEM((tok, HD), BF16),
            pltpu.VMEM((1, tok), positions.dtype),
            pltpu.VMEM(table.shape, table.dtype),
            pltpu.SemaphoreType.DMA((2 * steps + 5,)),
        ],
        limit=28,
        name="attend",
    )


def partial_kernel(inner, work, ctx_ref, w_ref, rows_ref, h_ref, *out_refs):
    cols = out_refs[0].shape[2]
    per = cols // ROT
    outer, mid, core = place(inner)
    dests = targets(outer)
    context = ctx_ref[...]
    for out_ref, (mine, blocks) in zip(out_refs, work):
        for at, (phase, shift) in enumerate(blocks):
            shard = (dests[phase] * inner + lax.rem(mid + shift, inner)) * 2
            shard = shard + (core if mine else 1 - core)

            def scale_row(i):
                return (65536.0 / math.sqrt(ROT)) / rows_ref[0, pl.ds(shard * per + i, 1), :]

            def store(i, value):
                out_ref[at, :, i * ROT : (i + 1) * ROT] = value

            start = pl.multiple_of(shard * cols, 128)
            gridded(context, h_ref, w_ref[:, pl.ds(start, cols)], scale_row, store)


def partials(inner, cols, work, context, weight, rows, had, after=()):
    tok = context.shape[0]
    count = sum(len(blocks) for _, blocks in work)
    return kernel_call(
        functools.partial(partial_kernel, inner, work),
        [jax.ShapeDtypeStruct((len(blocks), tok, cols), BF16) for _, blocks in work],
        [context, weight, rows, had],
        [vmem()] * 4,
        after=after,
        name="partials",
    )


def add_kernel(inner, inputs, outputs, *refs):
    ins, outs = refs[:inputs], refs[inputs:]
    outer = place(inner)[0]
    for out_ref, items in zip(outs, outputs):
        total = None
        for which, at, inner_only in items:
            value = (ins[which][...] if at is None else ins[which][at]).astype(F32)
            if inner_only:
                value = jnp.where(is_inner(outer), value, 0.0)
            total = value if total is None else total + value
        out_ref[...] = total.astype(BF16)


def add_up(inner, arrays, outputs, after=()):
    shape = arrays[0].shape[-2:]
    terms = sum(len(items) for items in outputs)
    return kernel_call(
        functools.partial(add_kernel, inner, len(arrays), outputs),
        [jax.ShapeDtypeStruct(shape, BF16)] * len(outputs),
        arrays,
        [vmem()] * len(arrays),
        after=after,
        name="add_up",
    )


def turn_residual_kernel(inner, res_ref, rows_ref, h_ref, out_ref, factor_ref):
    per = res_ref.shape[1] // ROT
    first = lax.axis_index("tp") * per
    for i in range(per):
        part = slice(i * ROT, (i + 1) * ROT)
        high = 256.0 / rows_ref[1, pl.ds(first + i, 1), :]
        low = rows_ref[0, pl.ds(first + i, 1), :] * (1.0 / 65536.0)
        turned = jnp.dot(res_ref[:, part], h_ref[...], preferred_element_type=F32)
        out_ref[:, part] = turned * (high * (1.0 / math.sqrt(ROT)))
        factor_ref[0:1, part] = low * high
        factor_ref[1:2, part] = low


def turn_residual(inner, residual, rows, had, after=()):
    return kernel_call(
        functools.partial(turn_residual_kernel, inner),
        [
            jax.ShapeDtypeStruct(residual.shape, F32),
            jax.ShapeDtypeStruct((2, residual.shape[1]), F32),
        ],
        [residual, rows, had],
        [vmem()] * 3,
        after=after,
        name="turn_residual",
    )


def summed_at(inner, items, ins, part):
    outer = place(inner)[0]
    total = None
    for (at, inner_only), ref in zip(items, ins):
        value = (ref[:, part] if at is None else ref[at, :, part]).astype(F32)
        if inner_only:
            value = jnp.where(is_inner(outer), value, 0.0)
        total = value if total is None else total + value
    return total


def regrid_kernel(inner, items, turned_ref, factor_ref, *refs):
    *ins, grid_ref = refs
    for i in range(turned_ref.shape[1] // ROT):
        part = slice(i * ROT, (i + 1) * ROT)
        value = turned_ref[:, part] + summed_at(inner, items, ins, part) * factor_ref[0:1, part]
        grid_ref[:, part] = jnp.clip(value, -127.0, 127.0).astype(BF16)


def regrid(inner, items, turned, factors, arrays, after=()):
    return kernel_call(
        functools.partial(regrid_kernel, inner, items),
        jax.ShapeDtypeStruct(turned.shape, BF16),
        [turned, factors, *arrays],
        [vmem()] * (2 + len(arrays)),
        after=after,
        name="regrid",
    )


def hidden_kernel(inner, items, res_ref, factor_ref, h_ref, *refs):
    *ins, out_ref, mark_ref = refs
    mark_ref[...] = jnp.zeros_like(mark_ref)
    for i in range(res_ref.shape[1] // ROT):
        part = slice(i * ROT, (i + 1) * ROT)
        value = summed_at(inner, items, ins, part) * factor_ref[1:2, part]
        upper = value.astype(BF16)
        lower = (value - upper.astype(F32)).astype(BF16)
        turned = jnp.dot(upper, h_ref[...], preferred_element_type=F32)
        turned = turned + jnp.dot(lower, h_ref[...], preferred_element_type=F32)
        stream = res_ref[:, part].astype(F32) + turned * (1.0 / math.sqrt(ROT))
        out_ref[:, part] = stream.astype(BF16)


def hidden(inner, items, residual, factors, had, arrays, after=()):
    return kernel_call(
        functools.partial(hidden_kernel, inner, items),
        [jax.ShapeDtypeStruct(residual.shape, BF16), jax.ShapeDtypeStruct((8, ROT), F32)],
        [residual, factors, had, *arrays],
        [vmem()] * (3 + len(arrays)),
        after=after,
        name="hidden",
    )


def choose_kernel(inner, inner_ref, end_ref, out_ref):
    inside = is_inner(place(inner)[0])

    @pl.when(inside)
    def _():
        out_ref[...] = inner_ref[...]

    @pl.when(jnp.logical_not(inside))
    def _():
        out_ref[...] = end_ref[...]


def choose(inner, at_inner, at_end, after=()):
    return kernel_call(
        functools.partial(choose_kernel, inner),
        jax.ShapeDtypeStruct(at_inner.shape, at_inner.dtype),
        [at_inner, at_end],
        [vmem()] * 2,
        after=after,
        name="choose",
    )


def gate(arrays, after):
    def kernel(*refs):
        pass

    shapes = [jax.ShapeDtypeStruct(array.shape, array.dtype) for array in arrays]
    aliases = {i: i for i in range(len(arrays))}
    specs = [vmem()] * len(arrays)
    return kernel_call(kernel, shapes, arrays, specs, after=after, aliases=aliases, name="gate")


def select_rows_kernel(inner, cols, w_ref, *out_refs):
    other = 1 - place(inner)[2]
    each = out_refs[0].shape[0]
    for j in range(each * len(out_refs)):
        start = pl.multiple_of((2 * j + other) * cols, 128)
        out_refs[j // each][j % each] = w_ref[pl.ds(start, cols), :]


def select_rows(inner, weight, cols, after=()):
    parts = 2 * OUTER
    each = OUTER * inner // parts
    return kernel_call(
        functools.partial(select_rows_kernel, inner, cols),
        [jax.ShapeDtypeStruct((each, cols, weight.shape[1]), weight.dtype)] * parts,
        [weight],
        [vmem()],
        after=after,
        name="select_rows",
    )


def turn_next_kernel(inner, cols, own_ref, gain_ref, rows_ref, h_ref, *refs):
    *other_refs, out_ref = refs
    each = other_refs[0].shape[0]
    core = place(inner)[2]
    for j in range(out_ref.shape[0]):
        shard = j * 2 + core
        for i in range(cols // ROT):
            block = shard * (cols // ROT) + i
            factor = rows_ref[1, pl.ds(block, 1), :] * (1.0 / (256.0 * math.sqrt(ROT)))
            rotation = (h_ref[...].astype(F32) * gain_ref[pl.ds(block, 1), :]).astype(BF16)
            part = slice(i * ROT, (i + 1) * ROT)
            own = own_ref[pl.ds(pl.multiple_of(block * ROT, ROT), ROT), :]
            for half, value in enumerate((own, other_refs[j // each][j % each, part, :])):
                turned = jnp.dot(rotation, value, preferred_element_type=F32)
                out_ref[j, part, half * HD : (half + 1) * HD] = (turned * factor).astype(BF16)


def turn_next(inner, weight, others, gain, rows, had, after=()):
    _, cols, width = others[0].shape
    return kernel_call(
        functools.partial(turn_next_kernel, inner, cols),
        jax.ShapeDtypeStruct((OUTER * inner, cols, 2 * width), BF16),
        [weight, gain, rows, had, *others],
        [vmem()] * (4 + len(others)),
        after=after,
        name="turn_next",
    )


def project_kernel(inner, places, has_acc, split, w_ref, rows_ref, *refs):
    outer, mid, core = place(inner)
    far, third, near, own = targets(outer)
    order = (own, near, third, far)
    acc_in = refs[0] if has_acc else None
    refs = refs[1:] if has_acc else refs
    values_in = refs[: len(places)]
    outs = refs[len(places) :]
    cols, width = w_ref.shape[1:]
    acc = acc_in[:, :width] if has_acc else 0.0
    squares = acc_in[:, width:] if has_acc else 0.0
    for ref, (phase, shift) in zip(values_in, places):
        block = order[phase] * inner + lax.rem(mid + inner - shift, inner)
        values = ref[...]
        acc = acc + jnp.dot(values, w_ref[block], preferred_element_type=F32)
        for i in range(cols // ROT):
            row = (block * 2 + core) * (cols // ROT) + i
            high = rows_ref[1, pl.ds(row, 1), :] * (1.0 / 256.0)
            value = values[:, i * ROT : (i + 1) * ROT].astype(F32) * high
            squares = squares + value * value
    if split:
        own_ref, other_ref = outs
        own_ref[:, :HD] = acc[:, :HD]
        own_ref[:, HD:] = squares
        other_ref[:, :HD] = acc[:, HD:]
        other_ref[:, HD:] = squares
    else:
        outs[0][:, :width] = acc
        outs[0][:, width:] = squares


def project(inner, weight, rows, acc, pieces, split=False, after=()):
    _, cols, width = weight.shape
    arrays = [array for _, _, array in pieces]
    tok = arrays[0].shape[0]
    places = tuple((phase, shift) for phase, shift, _ in pieces)
    accs = [] if acc is None else [acc]
    if split:
        out = [jax.ShapeDtypeStruct((tok, HD + ROT), F32)] * 2
    else:
        out = jax.ShapeDtypeStruct((tok, width + ROT), F32)
    return kernel_call(
        functools.partial(project_kernel, inner, places, acc is not None, split),
        out,
        [weight, rows, *accs, *arrays],
        [vmem()] * (2 + len(accs) + len(arrays)),
        after=after,
        name="project",
    )


def finish_kernel(features, own_ref, other_ref, out_ref):
    squares = own_ref[:, HD:] + other_ref[:, HD:]
    mean = jnp.sum(squares, axis=1, keepdims=True) * (1.0 / features)
    value = (own_ref[:, :HD] + other_ref[:, :HD]) * lax.rsqrt(mean + 1e-05)
    out_ref[...] = value.astype(BF16)


def finish(own, other, features):
    tok = own.shape[0]
    return kernel_call(
        functools.partial(finish_kernel, features),
        jax.ShapeDtypeStruct((tok, HD), BF16),
        [own, other],
        [vmem()] * 2,
        name="finish",
    )


def body(
    size,
    queries,
    cache_keys,
    cache_values,
    query_positions,
    out_weight,
    residual,
    scale_table,
    norm_gain,
    next_query_weight,
):
    inner = size // (2 * OUTER)
    cols = residual.shape[1]
    had = jnp.asarray(hadamard(ROT), BF16)
    shifts = range(1, inner)

    def permute(value, move):
        moves = []
        for i in range(size):
            spot = move(i // (2 * inner), (i // 2) % inner, i % 2)
            moves.append((i, (spot[0] * inner + spot[1]) * 2 + spot[2]))
        return lax.ppermute(value, "tp", moves)

    def swap_core(value):
        return permute(value, lambda a, b, c: (a, b, 1 - c))

    def shift_mid(value, shift):
        return permute(value, lambda a, b, c: (a, (b + shift) % inner, c))

    def swap_pairs(value):
        return permute(value, lambda a, b, c: (a ^ 1, b, c))

    def swap_middle(value):
        return permute(value, lambda a, b, c: ((0, 2, 1, 3)[a], b, c))

    everything = range(inner)
    context, rows, send1, out_weight, had = attend(
        inner, cols, queries, cache_keys, cache_values, out_weight, query_positions, scale_table, had
    )
    other1 = swap_core(send1)
    away1 = tuple((0, s) for s in shifts)
    def phase_blocks(phase):
        return tuple((phase, s) for s in everything)

    def grid_blocks(work, after=()):
        return partials(inner, cols, work, context, out_weight, rows, had, after=after)

    blocks2 = ((0, 0),) + phase_blocks(1)
    keep1, keep2, keep3, keep4, *send2 = grid_blocks(
        (
            (True, away1),
            (True, blocks2),
            (True, phase_blocks(2)),
            (True, phase_blocks(3)),
            *((False, (block,)) for block in blocks2),
        )
    )
    other2 = [swap_core(send) for send in send2]
    items1 = [((0, s - 1, False), (1, s - 1, False)) for s in shifts]
    pay1 = add_up(inner, [keep1, other1], items1, after=[keep2])
    come1 = [shift_mid(pay, s) for s, pay in zip(shifts, pay1)]
    (send3,) = grid_blocks(((False, phase_blocks(2)),), pay1[:1])
    other3 = swap_core(send3)
    (send4,) = grid_blocks(((False, phase_blocks(3)),), [send3])
    other4 = swap_core(send4)

    def sums(arrays, outputs, after=()):
        names = list(arrays)
        items = [[(names.index(name), at, only) for name, at, only in output] for output in outputs]
        return add_up(inner, list(arrays.values()), items, after=after)

    def came(step, blocks):
        return {f"came{step}_{s}": block for s, block in zip(shifts, blocks)}

    def added(names):
        return [(name, None, False) for name in names]

    own2 = {"keep2": keep2} | {f"other2_{i}": other for i, other in enumerate(other2)}
    own3 = {"keep3": keep3, "other3": other3}
    own4 = {"keep4": keep4, "other4": other4}

    def part2(i):
        return [("keep2", i, False), (f"other2_{i}", 0, False)]

    def part(step, s):
        return [(f"keep{step}", s, False), (f"other{step}", s, False)]

    came1 = came(1, come1)
    near1 = part2(0) + added(came1)
    *pay2, end1 = sums(own2 | came1, [*(part2(1 + s) for s in shifts), near1], after=[send4])
    came2 = came(2, [shift_mid(pay, s) for s, pay in zip(shifts, pay2)])
    from_end1 = {"end1": swap_pairs(end1)}
    turned_residual, factors = turn_residual(inner, residual, rows, had, after=[end1])
    picked = select_rows(inner, next_query_weight, cols, after=[factors])
    next_other = [swap_core(part) for part in picked]

    near2 = part2(1) + added(came2)
    *pay3, end2, mid2 = sums(
        own2 | own3 | came1 | came2 | from_end1,
        [*(part(3, s) for s in shifts), near2, near1 + [("end1", None, True)]],
        after=picked[:1],
    )
    came3 = came(3, [shift_mid(pay, s) for s, pay in zip(shifts, pay3)])
    from_end2 = {"end2": swap_pairs(end2)}
    from_mid2 = {"mid2": swap_middle(mid2)}

    *pay4, mid3, near3 = sums(
        own2 | own3 | own4 | came2 | came3 | from_end2 | from_mid2,
        [
            *(part(4, s) for s in shifts),
            near2 + [("end2", None, True)],
            part(3, 0) + added(came3) + [("mid2", None, True)],
        ],
        after=next_other,
    )
    come4 = [shift_mid(pay, s) for s, pay in zip(shifts, pay4)]
    from_mid3 = swap_middle(mid3)
    from_near3 = swap_pairs(near3)

    gain = norm_gain.astype(F32).reshape(-1, ROT)
    turned_next = turn_next(inner, next_query_weight, next_other, gain, rows, had, after=[near3])

    last = [keep4, other4, *come4, from_near3, from_mid3]
    items = [(0, False)] * 2 + [(None, False)] * (len(come4) + 1) + [(None, True)]
    grid = regrid(inner, items, turned_residual, factors, last, after=[turned_next])

    x1 = [shift_mid(grid, s) for s in shifts]
    near = swap_pairs(grid)
    mid1 = swap_middle(grid)
    acc = project(inner, turned_next, rows, None, [(0, 0, grid)])
    hidden_out, mark = hidden(inner, items, residual, factors, had, last, after=[acc])
    near, mid1 = gate([near, mid1], after=[*x1, mark])
    x2 = [shift_mid(near, s) for s in shifts]
    ends2 = swap_pairs(mid1)
    mids2 = swap_middle(near)
    acc = project(
        inner, turned_next, rows, acc, [(1, 0, near)] + [(0, s, x1[s - 1]) for s in shifts]
    )
    third = choose(inner, mid1, ends2, after=[*x2, acc])
    x3 = [shift_mid(third, s) for s in shifts]
    ends3 = swap_pairs(mids2)
    acc = project(
        inner, turned_next, rows, acc, [(2, 0, third)] + [(1, s, x2[s - 1]) for s in shifts]
    )
    fourth = choose(inner, mids2, ends3, after=[*x3, acc])
    x4 = [shift_mid(fourth, s) for s in shifts]
    acc = project(
        inner, turned_next, rows, acc, [(3, 0, fourth)] + [(2, s, x3[s - 1]) for s in shifts]
    )
    own, other = project(
        inner, turned_next, rows, acc, [(3, s, x4[s - 1]) for s in shifts], split=True
    )
    query_next = finish(own, swap_core(other), norm_gain.shape[0])
    return (hidden_out, query_next)


def solution(mesh):
    placed = (
        P("tp", "groups", None),
        P("tp", "groups", None),
        P("tp", "groups", None),
        P("groups"),
        P("tp", None),
        P("groups", "tp"),
        P(),
        P(),
        P(None, "tp"),
    )
    return jax.shard_map(
        functools.partial(body, mesh.shape["tp"]),
        mesh=mesh,
        in_specs=placed,
        out_specs=(P("groups", "tp"), P("groups", "tp")),
        check_vma=False,
    )
```

```python
import functools
import math

import jax
import jax.numpy as jnp
import numpy as np
from jax import lax
from jax.experimental import pallas as pl
from jax.experimental.pallas import tpu as pltpu
from jax.sharding import PartitionSpec as P

HD = 128
ROT = 128
OUTER = 4

F32 = jnp.float32
BF16 = jnp.bfloat16
MIB = 1024 * 1024


def hadamard(length):
    rows = np.arange(length)
    common = rows[:, None] & rows[None, :]
    parity = np.zeros((length, length), np.int64)
    for bit in range(length.bit_length()):
        parity += (common >> bit) & 1
    return (1 - 2 * (parity & 1)).astype(np.float32)


def vmem():
    return pl.BlockSpec(memory_space=pltpu.VMEM)


def anywhere():
    return pl.BlockSpec(memory_space=pl.ANY)


def place(inner):
    index = lax.axis_index("tp")
    return lax.div(index, 2 * inner), lax.rem(lax.div(index, 2), inner), lax.rem(index, 2)


def targets(outer):
    low = outer < 2
    near = outer + 1 - 2 * lax.rem(outer, 2)
    return jnp.where(low, 3, 0), jnp.where(low, 2, 1), near, outer


def is_inner(outer):
    return jnp.logical_or(outer == 1, outer == 2)


def kernel_call(kernel, out_shape, arrays, specs, after=(), scratch=(), aliases=None, limit=24, name=None):
    extra = len(after)

    def ordered(*refs):
        kernel(*refs[extra:])

    return pl.pallas_call(
        ordered,
        out_shape=out_shape,
        in_specs=[anywhere()] * extra + list(specs),
        out_specs=jax.tree.map(lambda _: vmem(), out_shape),
        scratch_shapes=list(scratch),
        input_output_aliases=aliases or {},
        cost_estimate=pl.CostEstimate(flops=0, bytes_accessed=0, transcendentals=0),
        compiler_params=pltpu.CompilerParams(vmem_limit_bytes=limit * MIB),
        name=name,
    )(*after, *arrays)


def gridded(context, h_ref, weight, scale_row, store):
    cols = weight.shape[1]
    count = cols // ROT
    value = jnp.dot(context, weight, preferred_element_type=F32).astype(BF16)
    stacked = jnp.concatenate([value[:, i * ROT : (i + 1) * ROT] for i in range(count)], axis=0)
    turned = jnp.dot(stacked, h_ref[...], preferred_element_type=F32)
    tok = value.shape[0]
    for i in range(count):
        part = turned[i * tok : (i + 1) * tok] * scale_row(i)
        store(i, jnp.clip(part, -127.0, 127.0).astype(BF16))


def attend_kernel(
    inner, cols, chunk, q_hbm, k_hbm, v_hbm, w_hbm, pos_hbm, table_hbm, h_hbm,
    ctx_ref, rows_ref, send_ref, w_ref, h_ref, k_ref, v_ref, s_ref, q_ref, pos_ref, table_ref, sems,
):
    tok = q_ref.shape[0]
    slots = k_ref.shape[0]
    steps = slots // chunk
    outer, mid, core = place(inner)
    dest = targets(outer)[0]

    def copy_k(j):
        part = pl.ds(j * chunk, chunk)
        return pltpu.make_async_copy(k_hbm.at[0, part], k_ref.at[part], sems.at[1 + j])

    def copy_v(j):
        part = pl.ds(j * chunk, chunk)
        return pltpu.make_async_copy(v_hbm.at[0, part], v_ref.at[part], sems.at[1 + steps + j])

    def shard_of(shift):
        return (dest * inner + lax.rem(mid + shift, inner)) * 2 + 1 - core

    copy_w = pltpu.make_async_copy(w_hbm, w_ref, sems.at[2 * steps + 1])
    copy_q = pltpu.make_async_copy(q_hbm.at[0], q_ref, sems.at[0])
    copy_pos = pltpu.make_async_copy(pos_hbm, pos_ref, sems.at[2 * steps + 2])
    copy_table = pltpu.make_async_copy(table_hbm, table_ref, sems.at[2 * steps + 3])
    copy_h = pltpu.make_async_copy(h_hbm, h_ref, sems.at[2 * steps + 4])
    copy_q.start()
    copy_pos.start()
    for j in range(steps):
        copy_k(j).start()
    copy_table.start()
    copy_h.start()
    for j in range(steps):
        copy_v(j).start()
    copy_w.start()

    copy_pos.wait()
    positions = jnp.broadcast_to(pos_ref[...].astype(F32), (ROT, tok)).T
    ahead = positions.astype(jnp.int32) - lax.broadcasted_iota(jnp.int32, (tok, ROT), 1)

    copy_q.wait()
    queries = q_ref[...]
    peak = jnp.full((tok, ROT), -jnp.inf, F32)
    for j in range(steps):
        copy_k(j).wait()
        scores = lax.dot_general(
            queries, k_ref[j * chunk : (j + 1) * chunk], (((1,), (1,)), ((), ())),
            preferred_element_type=F32,
        )
        for i in range(chunk // ROT):
            base = j * chunk + i * ROT
            part = jnp.where(ahead >= base, scores[:, i * ROT : (i + 1) * ROT], -jnp.inf)
            s_ref[:, base : base + ROT] = part
            peak = jnp.maximum(peak, part)
    copy_table.wait()
    table = table_ref[...].astype(F32)
    count = table.shape[1]
    for i in range(2):
        rows_ref[i] = jnp.broadcast_to(table[i : i + 1], (ROT, count)).T
    largest = jnp.max(peak, axis=1, keepdims=True)
    factor = math.log2(math.e) / math.sqrt(HD)
    total = jnp.zeros((tok, ROT), F32)
    acc = jnp.zeros((tok, HD), F32)
    for j in range(steps):
        copy_v(j).wait()
        pieces = []
        for i in range(chunk // ROT):
            base = j * chunk + i * ROT
            raised = jnp.exp2((s_ref[:, base : base + ROT] - largest) * factor)
            total = total + raised
            pieces.append(raised.astype(BF16))
        acc = acc + jnp.dot(
            jnp.concatenate(pieces, axis=1), v_ref[j * chunk : (j + 1) * chunk],
            preferred_element_type=F32,
        )
    context = (acc / jnp.sum(total, axis=1, keepdims=True)).astype(BF16)
    ctx_ref[...] = context

    per = cols // ROT
    copy_h.wait()
    copy_w.wait()
    for shift in range(1, inner):
        first = shard_of(shift) * per
        start = pl.multiple_of(shard_of(shift) * cols, 128)

        def scale_row(i):
            return (65536.0 / math.sqrt(ROT)) / rows_ref[0, pl.ds(first + i, 1), :]

        def store(i, value):
            send_ref[shift - 1, :, i * ROT : (i + 1) * ROT] = value

        gridded(context, h_ref, w_ref[:, pl.ds(start, cols)], scale_row, store)


def attend(inner, cols, queries, keys, values, weight, positions, table, had):
    tok, slots = queries.shape[1], keys.shape[1]
    chunk = min(1024, slots)
    steps = slots // chunk
    blocks = table.shape[1]
    arrays = [queries, keys, values, weight, positions[None, :], table, had]
    return kernel_call(
        functools.partial(attend_kernel, inner, cols, chunk),
        [
            pltpu.VMEM((tok, HD), BF16),
            pltpu.VMEM((2, blocks, ROT), F32),
            pltpu.VMEM((inner - 1, tok, cols), BF16),
            pltpu.VMEM(weight.shape, BF16),
            pltpu.VMEM(had.shape, BF16),
        ],
        [pltpu.with_memory_space_constraint(array, pltpu.HBM) for array in arrays],
        [pl.BlockSpec(memory_space=pltpu.HBM)] * len(arrays),
        scratch=[
            pltpu.VMEM((slots, HD), BF16),
            pltpu.VMEM((slots, HD), BF16),
            pltpu.VMEM((tok, slots), F32),
            pltpu.VMEM((tok, HD), BF16),
            pltpu.VMEM((1, tok), positions.dtype),
            pltpu.VMEM(table.shape, table.dtype),
            pltpu.SemaphoreType.DMA((2 * steps + 5,)),
        ],
        limit=28,
        name="attend",
    )


def partial_kernel(inner, work, ctx_ref, w_ref, rows_ref, h_ref, *out_refs):
    cols = out_refs[0].shape[2]
    per = cols // ROT
    outer, mid, core = place(inner)
    dests = targets(outer)
    context = ctx_ref[...]
    for out_ref, (mine, blocks) in zip(out_refs, work):
        for at, (phase, shift) in enumerate(blocks):
            shard = (dests[phase] * inner + lax.rem(mid + shift, inner)) * 2
            shard = shard + (core if mine else 1 - core)

            def scale_row(i):
                return (65536.0 / math.sqrt(ROT)) / rows_ref[0, pl.ds(shard * per + i, 1), :]

            def store(i, value):
                out_ref[at, :, i * ROT : (i + 1) * ROT] = value

            start = pl.multiple_of(shard * cols, 128)
            gridded(context, h_ref, w_ref[:, pl.ds(start, cols)], scale_row, store)


def partials(inner, cols, work, context, weight, rows, had, after=()):
    tok = context.shape[0]
    count = sum(len(blocks) for _, blocks in work)
    return kernel_call(
        functools.partial(partial_kernel, inner, work),
        [jax.ShapeDtypeStruct((len(blocks), tok, cols), BF16) for _, blocks in work],
        [context, weight, rows, had],
        [vmem()] * 4,
        after=after,
        name="partials",
    )


def add_kernel(inner, inputs, outputs, *refs):
    ins, outs = refs[:inputs], refs[inputs:]
    outer = place(inner)[0]
    for out_ref, items in zip(outs, outputs):
        total = None
        for which, at, inner_only in items:
            value = (ins[which][...] if at is None else ins[which][at]).astype(F32)
            if inner_only:
                value = jnp.where(is_inner(outer), value, 0.0)
            total = value if total is None else total + value
        out_ref[...] = total.astype(BF16)


def add_up(inner, arrays, outputs, after=()):
    shape = arrays[0].shape[-2:]
    terms = sum(len(items) for items in outputs)
    return kernel_call(
        functools.partial(add_kernel, inner, len(arrays), outputs),
        [jax.ShapeDtypeStruct(shape, BF16)] * len(outputs),
        arrays,
        [vmem()] * len(arrays),
        after=after,
        name="add_up",
    )


def turn_residual_kernel(inner, res_ref, rows_ref, h_ref, out_ref, factor_ref):
    per = res_ref.shape[1] // ROT
    first = lax.axis_index("tp") * per
    for i in range(per):
        part = slice(i * ROT, (i + 1) * ROT)
        high = 256.0 / rows_ref[1, pl.ds(first + i, 1), :]
        low = rows_ref[0, pl.ds(first + i, 1), :] * (1.0 / 65536.0)
        turned = jnp.dot(res_ref[:, part], h_ref[...], preferred_element_type=F32)
        out_ref[:, part] = turned * (high * (1.0 / math.sqrt(ROT)))
        factor_ref[0:1, part] = low * high
        factor_ref[1:2, part] = low


def turn_residual(inner, residual, rows, had, after=()):
    return kernel_call(
        functools.partial(turn_residual_kernel, inner),
        [
            jax.ShapeDtypeStruct(residual.shape, F32),
            jax.ShapeDtypeStruct((2, residual.shape[1]), F32),
        ],
        [residual, rows, had],
        [vmem()] * 3,
        after=after,
        name="turn_residual",
    )


def summed_at(inner, items, ins, part):
    outer = place(inner)[0]
    total = None
    for (at, inner_only), ref in zip(items, ins):
        value = (ref[:, part] if at is None else ref[at, :, part]).astype(F32)
        if inner_only:
            value = jnp.where(is_inner(outer), value, 0.0)
        total = value if total is None else total + value
    return total


def regrid_kernel(inner, items, *refs):
    *ins, turned_ref, factor_ref, grid_ref = refs
    for i in range(turned_ref.shape[1] // ROT):
        part = slice(i * ROT, (i + 1) * ROT)
        value = turned_ref[:, part] + summed_at(inner, items, ins, part) * factor_ref[0:1, part]
        grid_ref[:, part] = jnp.clip(value, -127.0, 127.0).astype(BF16)


def regrid(inner, items, turned, factors, arrays, after=()):
    return kernel_call(
        functools.partial(regrid_kernel, inner, items),
        jax.ShapeDtypeStruct(turned.shape, BF16),
        [*arrays, turned, factors],
        [vmem()] * (2 + len(arrays)),
        after=after,
        name="regrid",
    )


def hidden_kernel(inner, items, res_ref, factor_ref, h_ref, *refs):
    *ins, out_ref, mark_ref = refs
    mark_ref[...] = jnp.zeros_like(mark_ref)
    for i in range(res_ref.shape[1] // ROT):
        part = slice(i * ROT, (i + 1) * ROT)
        value = summed_at(inner, items, ins, part) * factor_ref[1:2, part]
        upper = value.astype(BF16)
        lower = (value - upper.astype(F32)).astype(BF16)
        turned = jnp.dot(upper, h_ref[...], preferred_element_type=F32)
        turned = turned + jnp.dot(lower, h_ref[...], preferred_element_type=F32)
        stream = res_ref[:, part].astype(F32) + turned * (1.0 / math.sqrt(ROT))
        out_ref[:, part] = stream.astype(BF16)


def hidden(inner, items, residual, factors, had, arrays, after=()):
    return kernel_call(
        functools.partial(hidden_kernel, inner, items),
        [jax.ShapeDtypeStruct(residual.shape, BF16), jax.ShapeDtypeStruct((8, ROT), F32)],
        [residual, factors, had, *arrays],
        [vmem()] * (3 + len(arrays)),
        after=after,
        name="hidden",
    )


def choose_kernel(inner, inner_ref, end_ref, out_ref):
    inside = is_inner(place(inner)[0])

    @pl.when(inside)
    def _():
        out_ref[...] = inner_ref[...]

    @pl.when(jnp.logical_not(inside))
    def _():
        out_ref[...] = end_ref[...]


def choose(inner, at_inner, at_end, after=()):
    return kernel_call(
        functools.partial(choose_kernel, inner),
        jax.ShapeDtypeStruct(at_inner.shape, at_inner.dtype),
        [at_inner, at_end],
        [vmem()] * 2,
        after=after,
        name="choose",
    )


def gate(arrays, after):
    def kernel(*refs):
        pass

    shapes = [jax.ShapeDtypeStruct(array.shape, array.dtype) for array in arrays]
    aliases = {len(after) + i: i for i in range(len(arrays))}
    specs = [vmem()] * len(arrays)
    return kernel_call(kernel, shapes, arrays, specs, after=after, aliases=aliases, name="gate")


def select_rows_kernel(inner, cols, w_ref, *out_refs):
    other = 1 - place(inner)[2]
    each = out_refs[0].shape[0]
    for j in range(each * len(out_refs)):
        start = pl.multiple_of((2 * j + other) * cols, 128)
        out_refs[j // each][j % each] = w_ref[pl.ds(start, cols), :]


def select_rows(inner, weight, cols, after=()):
    parts = 2
    each = OUTER * inner // parts
    return kernel_call(
        functools.partial(select_rows_kernel, inner, cols),
        [jax.ShapeDtypeStruct((each, cols, weight.shape[1]), weight.dtype)] * parts,
        [weight],
        [vmem()],
        after=after,
        name="select_rows",
    )


def turn_next_kernel(inner, cols, own_ref, gain_ref, rows_ref, h_ref, *refs):
    *other_refs, out_ref = refs
    each = other_refs[0].shape[0]
    core = place(inner)[2]
    for j in range(out_ref.shape[0]):
        shard = j * 2 + core
        for i in range(cols // ROT):
            block = shard * (cols // ROT) + i
            factor = rows_ref[1, pl.ds(block, 1), :] * (1.0 / (256.0 * math.sqrt(ROT)))
            rotation = (h_ref[...].astype(F32) * gain_ref[pl.ds(block, 1), :]).astype(BF16)
            part = slice(i * ROT, (i + 1) * ROT)
            own = own_ref[pl.ds(pl.multiple_of(block * ROT, ROT), ROT), :]
            for half, value in enumerate((own, other_refs[j // each][j % each, part, :])):
                turned = jnp.dot(rotation, value, preferred_element_type=F32)
                out_ref[j, part, half * HD : (half + 1) * HD] = (turned * factor).astype(BF16)


def turn_next(inner, weight, others, gain, rows, had, after=()):
    _, cols, width = others[0].shape
    return kernel_call(
        functools.partial(turn_next_kernel, inner, cols),
        jax.ShapeDtypeStruct((OUTER * inner, cols, 2 * width), BF16),
        [weight, gain, rows, had, *others],
        [vmem()] * (4 + len(others)),
        after=after,
        name="turn_next",
    )


def project_kernel(inner, places, has_acc, split, w_ref, rows_ref, *refs):
    outer, mid, core = place(inner)
    far, third, near, own = targets(outer)
    order = (own, near, third, far)
    acc_in = refs[0] if has_acc else None
    refs = refs[1:] if has_acc else refs
    values_in = refs[: len(places)]
    outs = refs[len(places) :]
    cols, width = w_ref.shape[1:]
    acc = acc_in[:, :width] if has_acc else 0.0
    squares = acc_in[:, width:] if has_acc else 0.0
    for ref, (phase, shift) in zip(values_in, places):
        block = order[phase] * inner + lax.rem(mid + inner - shift, inner)
        values = ref[...]
        acc = acc + jnp.dot(values, w_ref[block], preferred_element_type=F32)
        for i in range(cols // ROT):
            row = (block * 2 + core) * (cols // ROT) + i
            high = rows_ref[1, pl.ds(row, 1), :] * (1.0 / 256.0)
            value = values[:, i * ROT : (i + 1) * ROT].astype(F32) * high
            squares = squares + value * value
    if split:
        own_ref, other_ref = outs
        own_ref[:, :HD] = acc[:, :HD]
        own_ref[:, HD:] = squares
        other_ref[:, :HD] = acc[:, HD:]
        other_ref[:, HD:] = squares
    else:
        outs[0][:, :width] = acc
        outs[0][:, width:] = squares


def project(inner, weight, rows, acc, pieces, split=False, after=()):
    _, cols, width = weight.shape
    arrays = [array for _, _, array in pieces]
    tok = arrays[0].shape[0]
    places = tuple((phase, shift) for phase, shift, _ in pieces)
    accs = [] if acc is None else [acc]
    if split:
        out = [jax.ShapeDtypeStruct((tok, HD + ROT), F32)] * 2
    else:
        out = jax.ShapeDtypeStruct((tok, width + ROT), F32)
    return kernel_call(
        functools.partial(project_kernel, inner, places, acc is not None, split),
        out,
        [weight, rows, *accs, *arrays],
        [vmem()] * (2 + len(accs) + len(arrays)),
        after=after,
        name="project",
    )


def finish_kernel(features, own_ref, other_ref, out_ref):
    squares = own_ref[:, HD:] + other_ref[:, HD:]
    mean = jnp.sum(squares, axis=1, keepdims=True) * (1.0 / features)
    value = (own_ref[:, :HD] + other_ref[:, :HD]) * lax.rsqrt(mean + 1e-05)
    out_ref[...] = value.astype(BF16)


def finish(own, other, features):
    tok = own.shape[0]
    return kernel_call(
        functools.partial(finish_kernel, features),
        jax.ShapeDtypeStruct((tok, HD), BF16),
        [own, other],
        [vmem()] * 2,
        name="finish",
    )


def body(
    size,
    queries,
    cache_keys,
    cache_values,
    query_positions,
    out_weight,
    residual,
    scale_table,
    norm_gain,
    next_query_weight,
):
    inner = size // (2 * OUTER)
    cols = residual.shape[1]
    had = jnp.asarray(hadamard(ROT), BF16)
    shifts = range(1, inner)

    def permute(value, move):
        moves = []
        for i in range(size):
            spot = move(i // (2 * inner), (i // 2) % inner, i % 2)
            moves.append((i, (spot[0] * inner + spot[1]) * 2 + spot[2]))
        return lax.ppermute(value, "tp", moves)

    def swap_core(value):
        return permute(value, lambda a, b, c: (a, b, 1 - c))

    def shift_mid(value, shift):
        return permute(value, lambda a, b, c: (a, (b + shift) % inner, c))

    def swap_pairs(value):
        return permute(value, lambda a, b, c: (a ^ 1, b, c))

    def swap_middle(value):
        return permute(value, lambda a, b, c: ((0, 2, 1, 3)[a], b, c))

    everything = range(inner)
    context, rows, send1, out_weight, had = attend(
        inner, cols, queries, cache_keys, cache_values, out_weight, query_positions, scale_table, had
    )
    other1 = swap_core(send1)
    away1 = tuple((0, s) for s in shifts)
    def phase_blocks(phase):
        return tuple((phase, s) for s in everything)

    def grid_blocks(work, after=()):
        return partials(inner, cols, work, context, out_weight, rows, had, after=after)

    blocks2 = ((0, 0),) + phase_blocks(1)
    keep1, keep2, keep3, keep4, *send2 = grid_blocks(
        (
            (True, away1),
            (True, blocks2),
            (True, phase_blocks(2)),
            (True, phase_blocks(3)),
            *((False, (block,)) for block in blocks2),
        )
    )
    other2 = [swap_core(send) for send in send2]
    items1 = [((0, s - 1, False), (1, s - 1, False)) for s in shifts]
    pay1 = add_up(inner, [keep1, other1], items1, after=[keep2])
    come1 = [shift_mid(pay, s) for s, pay in zip(shifts, pay1)]
    (send3,) = grid_blocks(((False, phase_blocks(2)),), pay1[:1])
    other3 = swap_core(send3)
    (send4,) = grid_blocks(((False, phase_blocks(3)),), [send3])
    other4 = swap_core(send4)

    def sums(arrays, outputs, after=()):
        names = list(arrays)
        items = [[(names.index(name), at, only) for name, at, only in output] for output in outputs]
        return add_up(inner, list(arrays.values()), items, after=after)

    def came(step, blocks):
        return {f"came{step}_{s}": block for s, block in zip(shifts, blocks)}

    def added(names):
        return [(name, None, False) for name in names]

    own2 = {"keep2": keep2} | {f"other2_{i}": other for i, other in enumerate(other2)}
    own3 = {"keep3": keep3, "other3": other3}
    own4 = {"keep4": keep4, "other4": other4}

    def part2(i):
        return [("keep2", i, False), (f"other2_{i}", 0, False)]

    def part(step, s):
        return [(f"keep{step}", s, False), (f"other{step}", s, False)]

    came1 = came(1, come1)
    near1 = part2(0) + added(came1)
    *pay2, end1 = sums(came1 | own2, [*(part2(1 + s) for s in shifts), near1], after=[send4])
    came2 = came(2, [shift_mid(pay, s) for s, pay in zip(shifts, pay2)])
    from_end1 = {"end1": swap_pairs(end1)}
    turned_residual, factors = turn_residual(inner, residual, rows, had, after=[end1])
    picked = select_rows(inner, next_query_weight, cols, after=[factors])
    next_other = [swap_core(part) for part in picked]

    near2 = part2(1) + added(came2)
    *pay3, end2, mid2 = sums(
        came2 | from_end1 | own2 | own3 | came1,
        [*(part(3, s) for s in shifts), near2, near1 + [("end1", None, True)]],
        after=picked[:1],
    )
    came3 = came(3, [shift_mid(pay, s) for s, pay in zip(shifts, pay3)])
    from_end2 = {"end2": swap_pairs(end2)}
    from_mid2 = {"mid2": swap_middle(mid2)}

    *pay4, mid3, near3 = sums(
        came3 | from_end2 | from_mid2 | own2 | own3 | own4 | came2,
        [
            *(part(4, s) for s in shifts),
            near2 + [("end2", None, True)],
            part(3, 0) + added(came3) + [("mid2", None, True)],
        ],

    )
    come4 = [shift_mid(pay, s) for s, pay in zip(shifts, pay4)]
    from_mid3 = swap_middle(mid3)
    from_near3 = swap_pairs(near3)

    gain = norm_gain.astype(F32).reshape(-1, ROT)

    last = [*come4, from_near3, from_mid3, keep4, other4]
    items = [(None, False)] * (len(come4) + 1) + [(None, True)] + [(0, False)] * 2
    grid = regrid(inner, items, turned_residual, factors, last)

    x1 = [shift_mid(grid, s) for s in shifts]
    near = swap_pairs(grid)
    mid1 = swap_middle(grid)
    hidden_out, mark = hidden(inner, items, residual, factors, had, last, after=[grid])
    near, mid1 = gate([near, mid1], after=[*x1, mark])
    x2 = [shift_mid(near, s) for s in shifts]
    ends2 = swap_pairs(mid1)
    mids2 = swap_middle(near)
    third = choose(inner, mid1, ends2, after=x2)
    x3 = [shift_mid(third, s) for s in shifts]
    ends3 = swap_pairs(mids2)
    turned_next = turn_next(inner, next_query_weight, next_other, gain, rows, had, after=[third])
    fourth = choose(inner, mids2, ends3, after=[*x3, turned_next])
    x4 = [shift_mid(fourth, s) for s in shifts]
    acc = project(
        inner,
        turned_next,
        rows,
        None,
        [(0, 0, grid), (1, 0, near), (2, 0, third), (3, 0, fourth)]
        + [(phase, s, x[s - 1]) for phase, x in enumerate((x1, x2, x3)) for s in shifts],
    )
    own, other = project(
        inner, turned_next, rows, acc, [(3, s, x4[s - 1]) for s in shifts], split=True
    )
    query_next = finish(own, swap_core(other), norm_gain.shape[0])
    return (hidden_out, query_next)


def solution(mesh):
    placed = (
        P("tp", "groups", None),
        P("tp", "groups", None),
        P("tp", "groups", None),
        P("groups"),
        P("tp", None),
        P("groups", "tp"),
        P(),
        P(),
        P(None, "tp"),
    )
    return jax.shard_map(
        functools.partial(body, mesh.shape["tp"]),
        mesh=mesh,
        in_specs=placed,
        out_specs=(P("groups", "tp"), P("groups", "tp")),
        check_vma=False,
    )
```

```python
import functools
import math

import jax
import jax.numpy as jnp
import numpy as np
from jax import lax
from jax.experimental import pallas as pl
from jax.experimental.pallas import tpu as pltpu
from jax.sharding import PartitionSpec as P

HD = 128
ROT = 128
OUTER = 4

F32 = jnp.float32
BF16 = jnp.bfloat16
MIB = 1024 * 1024


def hadamard(length):
    rows = np.arange(length)
    common = rows[:, None] & rows[None, :]
    parity = np.zeros((length, length), np.int64)
    for bit in range(length.bit_length()):
        parity += (common >> bit) & 1
    return (1 - 2 * (parity & 1)).astype(np.float32)


def vmem():
    return pl.BlockSpec(memory_space=pltpu.VMEM)


def anywhere():
    return pl.BlockSpec(memory_space=pl.ANY)


def place(inner):
    index = lax.axis_index("tp")
    return lax.div(index, 2 * inner), lax.rem(lax.div(index, 2), inner), lax.rem(index, 2)


def targets(outer):
    low = outer < 2
    near = outer + 1 - 2 * lax.rem(outer, 2)
    return jnp.where(low, 3, 0), jnp.where(low, 2, 1), near, outer


def is_inner(outer):
    return jnp.logical_or(outer == 1, outer == 2)


def kernel_call(kernel, out_shape, arrays, specs, after=(), scratch=(), aliases=None, limit=24, name=None):
    extra = len(after)

    def ordered(*refs):
        kernel(*refs[extra:])

    return pl.pallas_call(
        ordered,
        out_shape=out_shape,
        in_specs=[anywhere()] * extra + list(specs),
        out_specs=jax.tree.map(lambda _: vmem(), out_shape),
        scratch_shapes=list(scratch),
        input_output_aliases=aliases or {},
        cost_estimate=pl.CostEstimate(flops=0, bytes_accessed=0, transcendentals=0),
        compiler_params=pltpu.CompilerParams(vmem_limit_bytes=limit * MIB),
        name=name,
    )(*after, *arrays)


def gridded(context, h_ref, weight, scale_row, store):
    cols = weight.shape[1]
    count = cols // ROT
    value = jnp.dot(context, weight, preferred_element_type=F32).astype(BF16)
    stacked = jnp.concatenate([value[:, i * ROT : (i + 1) * ROT] for i in range(count)], axis=0)
    turned = jnp.dot(stacked, h_ref[...], preferred_element_type=F32)
    tok = value.shape[0]
    for i in range(count):
        part = turned[i * tok : (i + 1) * tok] * scale_row(i)
        store(i, jnp.clip(part, -127.0, 127.0).astype(BF16))


def attend_kernel(
    inner, cols, chunk, q_hbm, k_hbm, v_hbm, w_hbm, pos_hbm, table_hbm, h_hbm,
    ctx_ref, rows_ref, send_ref, w_ref, h_ref, k_ref, v_ref, s_ref, q_ref, pos_ref, table_ref, sems,
):
    tok = q_ref.shape[0]
    slots = k_ref.shape[0]
    steps = slots // chunk
    outer, mid, core = place(inner)
    dest = targets(outer)[0]

    def copy_k(j):
        part = pl.ds(j * chunk, chunk)
        return pltpu.make_async_copy(k_hbm.at[0, part], k_ref.at[part], sems.at[1 + j])

    def copy_v(j):
        part = pl.ds(j * chunk, chunk)
        return pltpu.make_async_copy(v_hbm.at[0, part], v_ref.at[part], sems.at[1 + steps + j])

    def shard_of(shift):
        return (dest * inner + lax.rem(mid + shift, inner)) * 2 + 1 - core

    copy_w = pltpu.make_async_copy(w_hbm, w_ref, sems.at[2 * steps + 1])
    copy_q = pltpu.make_async_copy(q_hbm.at[0], q_ref, sems.at[0])
    copy_pos = pltpu.make_async_copy(pos_hbm, pos_ref, sems.at[2 * steps + 2])
    copy_table = pltpu.make_async_copy(table_hbm, table_ref, sems.at[2 * steps + 3])
    copy_h = pltpu.make_async_copy(h_hbm, h_ref, sems.at[2 * steps + 4])
    copy_q.start()
    copy_pos.start()
    for j in range(steps):
        copy_k(j).start()
    copy_table.start()
    copy_h.start()
    for j in range(steps):
        copy_v(j).start()
    copy_w.start()

    copy_pos.wait()
    positions = jnp.broadcast_to(pos_ref[...].astype(F32), (ROT, tok)).T
    ahead = positions.astype(jnp.int32) - lax.broadcasted_iota(jnp.int32, (tok, ROT), 1)

    copy_q.wait()
    queries = q_ref[...]
    peak = jnp.full((tok, ROT), -jnp.inf, F32)
    for j in range(steps):
        copy_k(j).wait()
        scores = lax.dot_general(
            queries, k_ref[j * chunk : (j + 1) * chunk], (((1,), (1,)), ((), ())),
            preferred_element_type=F32,
        )
        for i in range(chunk // ROT):
            base = j * chunk + i * ROT
            part = jnp.where(ahead >= base, scores[:, i * ROT : (i + 1) * ROT], -jnp.inf)
            s_ref[:, base : base + ROT] = part
            peak = jnp.maximum(peak, part)
    copy_table.wait()
    table = table_ref[...].astype(F32)
    count = table.shape[1]
    for i in range(2):
        rows_ref[i] = jnp.broadcast_to(table[i : i + 1], (ROT, count)).T
    largest = jnp.max(peak, axis=1, keepdims=True)
    factor = math.log2(math.e) / math.sqrt(HD)
    total = jnp.zeros((tok, ROT), F32)
    acc = jnp.zeros((tok, HD), F32)
    for j in range(steps):
        copy_v(j).wait()
        pieces = []
        for i in range(chunk // ROT):
            base = j * chunk + i * ROT
            raised = jnp.exp2((s_ref[:, base : base + ROT] - largest) * factor)
            total = total + raised
            pieces.append(raised.astype(BF16))
        acc = acc + jnp.dot(
            jnp.concatenate(pieces, axis=1), v_ref[j * chunk : (j + 1) * chunk],
            preferred_element_type=F32,
        )
    context = (acc / jnp.sum(total, axis=1, keepdims=True)).astype(BF16)
    ctx_ref[...] = context

    per = cols // ROT
    copy_h.wait()
    copy_w.wait()
    for shift in range(1, inner):
        first = shard_of(shift) * per
        start = pl.multiple_of(shard_of(shift) * cols, 128)

        def scale_row(i):
            return (65536.0 / math.sqrt(ROT)) / rows_ref[0, pl.ds(first + i, 1), :]

        def store(i, value):
            send_ref[shift - 1, :, i * ROT : (i + 1) * ROT] = value

        gridded(context, h_ref, w_ref[:, pl.ds(start, cols)], scale_row, store)


def attend(inner, cols, queries, keys, values, weight, positions, table, had):
    tok, slots = queries.shape[1], keys.shape[1]
    chunk = min(1024, slots)
    steps = slots // chunk
    blocks = table.shape[1]
    arrays = [queries, keys, values, weight, positions[None, :], table, had]
    return kernel_call(
        functools.partial(attend_kernel, inner, cols, chunk),
        [
            pltpu.VMEM((tok, HD), BF16),
            pltpu.VMEM((2, blocks, ROT), F32),
            pltpu.VMEM((inner - 1, tok, cols), BF16),
            pltpu.VMEM(weight.shape, BF16),
            pltpu.VMEM(had.shape, BF16),
        ],
        [pltpu.with_memory_space_constraint(array, pltpu.HBM) for array in arrays],
        [pl.BlockSpec(memory_space=pltpu.HBM)] * len(arrays),
        scratch=[
            pltpu.VMEM((slots, HD), BF16),
            pltpu.VMEM((slots, HD), BF16),
            pltpu.VMEM((tok, slots), F32),
            pltpu.VMEM((tok, HD), BF16),
            pltpu.VMEM((1, tok), positions.dtype),
            pltpu.VMEM(table.shape, table.dtype),
            pltpu.SemaphoreType.DMA((2 * steps + 5,)),
        ],
        limit=28,
        name="attend",
    )


def partial_kernel(inner, work, ctx_ref, w_ref, rows_ref, h_ref, *out_refs):
    cols = out_refs[0].shape[2]
    per = cols // ROT
    outer, mid, core = place(inner)
    dests = targets(outer)
    context = ctx_ref[...]
    for out_ref, (mine, blocks) in zip(out_refs, work):
        for at, (phase, shift) in enumerate(blocks):
            shard = (dests[phase] * inner + lax.rem(mid + shift, inner)) * 2
            shard = shard + (core if mine else 1 - core)

            def scale_row(i):
                return (65536.0 / math.sqrt(ROT)) / rows_ref[0, pl.ds(shard * per + i, 1), :]

            def store(i, value):
                out_ref[at, :, i * ROT : (i + 1) * ROT] = value

            start = pl.multiple_of(shard * cols, 128)
            gridded(context, h_ref, w_ref[:, pl.ds(start, cols)], scale_row, store)


def partials(inner, cols, work, context, weight, rows, had, after=()):
    tok = context.shape[0]
    count = sum(len(blocks) for _, blocks in work)
    return kernel_call(
        functools.partial(partial_kernel, inner, work),
        [jax.ShapeDtypeStruct((len(blocks), tok, cols), BF16) for _, blocks in work],
        [context, weight, rows, had],
        [vmem()] * 4,
        after=after,
        name="partials",
    )


def add_kernel(inner, inputs, outputs, *refs):
    ins, outs = refs[:inputs], refs[inputs:]
    outer = place(inner)[0]
    for out_ref, items in zip(outs, outputs):
        total = None
        for which, at, inner_only in items:
            value = (ins[which][...] if at is None else ins[which][at]).astype(F32)
            if inner_only:
                value = jnp.where(is_inner(outer), value, 0.0)
            total = value if total is None else total + value
        out_ref[...] = total.astype(BF16)


def add_up(inner, arrays, outputs, after=()):
    shape = arrays[0].shape[-2:]
    terms = sum(len(items) for items in outputs)
    return kernel_call(
        functools.partial(add_kernel, inner, len(arrays), outputs),
        [jax.ShapeDtypeStruct(shape, BF16)] * len(outputs),
        arrays,
        [vmem()] * len(arrays),
        after=after,
        name="add_up",
    )


def turn_residual_kernel(inner, res_ref, rows_ref, h_ref, out_ref, factor_ref):
    per = res_ref.shape[1] // ROT
    first = lax.axis_index("tp") * per
    for i in range(per):
        part = slice(i * ROT, (i + 1) * ROT)
        high = 256.0 / rows_ref[1, pl.ds(first + i, 1), :]
        low = rows_ref[0, pl.ds(first + i, 1), :] * (1.0 / 65536.0)
        turned = jnp.dot(res_ref[:, part], h_ref[...], preferred_element_type=F32)
        out_ref[:, part] = turned * (high * (1.0 / math.sqrt(ROT)))
        factor_ref[0:1, part] = low * high
        factor_ref[1:2, part] = low


def turn_residual(inner, residual, rows, had, after=()):
    return kernel_call(
        functools.partial(turn_residual_kernel, inner),
        [
            jax.ShapeDtypeStruct(residual.shape, F32),
            jax.ShapeDtypeStruct((2, residual.shape[1]), F32),
        ],
        [residual, rows, had],
        [vmem()] * 3,
        after=after,
        name="turn_residual",
    )


def summed_at(inner, items, ins, part):
    outer = place(inner)[0]
    total = None
    for (at, inner_only), ref in zip(items, ins):
        value = (ref[:, part] if at is None else ref[at, :, part]).astype(F32)
        if inner_only:
            value = jnp.where(is_inner(outer), value, 0.0)
        total = value if total is None else total + value
    return total


def regrid_kernel(inner, items, *refs):
    *ins, turned_ref, factor_ref, grid_ref = refs
    for i in range(turned_ref.shape[1] // ROT):
        part = slice(i * ROT, (i + 1) * ROT)
        value = turned_ref[:, part] + summed_at(inner, items, ins, part) * factor_ref[0:1, part]
        grid_ref[:, part] = jnp.clip(value, -127.0, 127.0).astype(BF16)


def regrid(inner, items, turned, factors, arrays, after=()):
    return kernel_call(
        functools.partial(regrid_kernel, inner, items),
        jax.ShapeDtypeStruct(turned.shape, BF16),
        [*arrays, turned, factors],
        [vmem()] * (2 + len(arrays)),
        after=after,
        name="regrid",
    )


def hidden_kernel(inner, items, res_ref, factor_ref, h_ref, *refs):
    *ins, out_ref, mark_ref = refs
    mark_ref[...] = jnp.zeros_like(mark_ref)
    for i in range(res_ref.shape[1] // ROT):
        part = slice(i * ROT, (i + 1) * ROT)
        value = summed_at(inner, items, ins, part) * factor_ref[1:2, part]
        upper = value.astype(BF16)
        lower = (value - upper.astype(F32)).astype(BF16)
        turned = jnp.dot(upper, h_ref[...], preferred_element_type=F32)
        turned = turned + jnp.dot(lower, h_ref[...], preferred_element_type=F32)
        stream = res_ref[:, part].astype(F32) + turned * (1.0 / math.sqrt(ROT))
        out_ref[:, part] = stream.astype(BF16)


def hidden(inner, items, residual, factors, had, arrays, after=()):
    return kernel_call(
        functools.partial(hidden_kernel, inner, items),
        [jax.ShapeDtypeStruct(residual.shape, BF16), jax.ShapeDtypeStruct((8, ROT), F32)],
        [residual, factors, had, *arrays],
        [vmem()] * (3 + len(arrays)),
        after=after,
        name="hidden",
    )


def choose_kernel(inner, inner_ref, end_ref, out_ref):
    inside = is_inner(place(inner)[0])

    @pl.when(inside)
    def _():
        out_ref[...] = inner_ref[...]

    @pl.when(jnp.logical_not(inside))
    def _():
        out_ref[...] = end_ref[...]


def choose(inner, at_inner, at_end, after=()):
    return kernel_call(
        functools.partial(choose_kernel, inner),
        jax.ShapeDtypeStruct(at_inner.shape, at_inner.dtype),
        [at_inner, at_end],
        [vmem()] * 2,
        after=after,
        name="choose",
    )


def gate(arrays, after):
    def kernel(*refs):
        pass

    shapes = [jax.ShapeDtypeStruct(array.shape, array.dtype) for array in arrays]
    aliases = {len(after) + i: i for i in range(len(arrays))}
    specs = [vmem()] * len(arrays)
    return kernel_call(kernel, shapes, arrays, specs, after=after, aliases=aliases, name="gate")


def select_rows_kernel(inner, cols, w_ref, *out_refs):
    other = 1 - place(inner)[2]
    each = out_refs[0].shape[0]
    for j in range(each * len(out_refs)):
        start = pl.multiple_of((2 * j + other) * cols, 128)
        out_refs[j // each][j % each] = w_ref[pl.ds(start, cols), :]


def select_rows(inner, weight, cols, after=()):
    parts = 2
    each = OUTER * inner // parts
    return kernel_call(
        functools.partial(select_rows_kernel, inner, cols),
        [jax.ShapeDtypeStruct((each, cols, weight.shape[1]), weight.dtype)] * parts,
        [weight],
        [vmem()],
        after=after,
        name="select_rows",
    )


def turn_next_kernel(inner, cols, own_ref, gain_ref, rows_ref, h_ref, *refs):
    *other_refs, out_ref = refs
    each = other_refs[0].shape[0]
    core = place(inner)[2]
    for j in range(out_ref.shape[0]):
        shard = j * 2 + core
        for i in range(cols // ROT):
            block = shard * (cols // ROT) + i
            factor = rows_ref[1, pl.ds(block, 1), :] * (1.0 / (256.0 * math.sqrt(ROT)))
            rotation = (h_ref[...].astype(F32) * gain_ref[pl.ds(block, 1), :]).astype(BF16)
            part = slice(i * ROT, (i + 1) * ROT)
            own = own_ref[pl.ds(pl.multiple_of(block * ROT, ROT), ROT), :]
            for half, value in enumerate((own, other_refs[j // each][j % each, part, :])):
                turned = jnp.dot(rotation, value, preferred_element_type=F32)
                out_ref[j, part, half * HD : (half + 1) * HD] = (turned * factor).astype(BF16)


def turn_next(inner, weight, others, gain, rows, had, after=()):
    _, cols, width = others[0].shape
    return kernel_call(
        functools.partial(turn_next_kernel, inner, cols),
        jax.ShapeDtypeStruct((OUTER * inner, cols, 2 * width), BF16),
        [weight, gain, rows, had, *others],
        [vmem()] * (4 + len(others)),
        after=after,
        name="turn_next",
    )


def project_kernel(inner, places, has_acc, split, w_ref, rows_ref, *refs):
    outer, mid, core = place(inner)
    far, third, near, own = targets(outer)
    order = (own, near, third, far)
    acc_in = refs[0] if has_acc else None
    refs = refs[1:] if has_acc else refs
    values_in = refs[: len(places)]
    outs = refs[len(places) :]
    cols, width = w_ref.shape[1:]
    acc = acc_in[:, :width] if has_acc else 0.0
    squares = acc_in[:, width:] if has_acc else 0.0
    for ref, (phase, shift) in zip(values_in, places):
        block = order[phase] * inner + lax.rem(mid + inner - shift, inner)
        values = ref[...]
        acc = acc + jnp.dot(values, w_ref[block], preferred_element_type=F32)
        for i in range(cols // ROT):
            row = (block * 2 + core) * (cols // ROT) + i
            high = rows_ref[1, pl.ds(row, 1), :] * (1.0 / 256.0)
            value = values[:, i * ROT : (i + 1) * ROT].astype(F32) * high
            squares = squares + value * value
    if split:
        own_ref, other_ref = outs
        own_ref[:, :HD] = acc[:, :HD]
        own_ref[:, HD:] = squares
        other_ref[:, :HD] = acc[:, HD:]
        other_ref[:, HD:] = squares
    else:
        outs[0][:, :width] = acc
        outs[0][:, width:] = squares


def project(inner, weight, rows, acc, pieces, split=False, after=()):
    _, cols, width = weight.shape
    arrays = [array for _, _, array in pieces]
    tok = arrays[0].shape[0]
    places = tuple((phase, shift) for phase, shift, _ in pieces)
    accs = [] if acc is None else [acc]
    if split:
        out = [jax.ShapeDtypeStruct((tok, HD + ROT), F32)] * 2
    else:
        out = jax.ShapeDtypeStruct((tok, width + ROT), F32)
    return kernel_call(
        functools.partial(project_kernel, inner, places, acc is not None, split),
        out,
        [weight, rows, *accs, *arrays],
        [vmem()] * (2 + len(accs) + len(arrays)),
        after=after,
        name="project",
    )


def finish_kernel(features, own_ref, other_ref, out_ref):
    squares = own_ref[:, HD:] + other_ref[:, HD:]
    mean = jnp.sum(squares, axis=1, keepdims=True) * (1.0 / features)
    value = (own_ref[:, :HD] + other_ref[:, :HD]) * lax.rsqrt(mean + 1e-05)
    out_ref[...] = value.astype(BF16)


def finish(own, other, features):
    tok = own.shape[0]
    return kernel_call(
        functools.partial(finish_kernel, features),
        jax.ShapeDtypeStruct((tok, HD), BF16),
        [own, other],
        [vmem()] * 2,
        name="finish",
    )


def body(
    size,
    queries,
    cache_keys,
    cache_values,
    query_positions,
    out_weight,
    residual,
    scale_table,
    norm_gain,
    next_query_weight,
):
    inner = size // (2 * OUTER)
    cols = residual.shape[1]
    had = jnp.asarray(hadamard(ROT), BF16)
    shifts = range(1, inner)

    def permute(value, move):
        moves = []
        for i in range(size):
            spot = move(i // (2 * inner), (i // 2) % inner, i % 2)
            moves.append((i, (spot[0] * inner + spot[1]) * 2 + spot[2]))
        return lax.ppermute(value, "tp", moves)

    def swap_core(value):
        return permute(value, lambda a, b, c: (a, b, 1 - c))

    def shift_mid(value, shift):
        return permute(value, lambda a, b, c: (a, (b + shift) % inner, c))

    def swap_pairs(value):
        return permute(value, lambda a, b, c: (a ^ 1, b, c))

    def swap_middle(value):
        return permute(value, lambda a, b, c: (a, b, 1 - c) if a in (0, 3) else (3 - a, b, c))

    everything = range(inner)
    context, rows, send1, out_weight, had = attend(
        inner, cols, queries, cache_keys, cache_values, out_weight, query_positions, scale_table, had
    )
    other1 = swap_core(send1)
    away1 = tuple((0, s) for s in shifts)
    def phase_blocks(phase):
        return tuple((phase, s) for s in everything)

    def grid_blocks(work, after=()):
        return partials(inner, cols, work, context, out_weight, rows, had, after=after)

    blocks2 = ((0, 0),) + phase_blocks(1)
    keep1, keep2, keep3, keep4, *send2 = grid_blocks(
        (
            (True, away1),
            (True, blocks2),
            (True, phase_blocks(2)),
            (True, phase_blocks(3)),
            *((False, (block,)) for block in blocks2),
        )
    )
    other2 = [swap_core(send) for send in send2]
    items1 = [((0, s - 1, False), (1, s - 1, False)) for s in shifts]
    pay1 = add_up(inner, [keep1, other1], items1, after=[keep2])
    come1 = [shift_mid(pay, s) for s, pay in zip(shifts, pay1)]
    (send3,) = grid_blocks(((False, phase_blocks(2)),), pay1[:1])
    other3 = swap_core(send3)
    (send4,) = grid_blocks(((False, phase_blocks(3)),), [send3])
    other4 = swap_core(send4)

    def sums(arrays, outputs, after=()):
        names = list(arrays)
        items = [[(names.index(name), at, only) for name, at, only in output] for output in outputs]
        return add_up(inner, list(arrays.values()), items, after=after)

    def came(step, blocks):
        return {f"came{step}_{s}": block for s, block in zip(shifts, blocks)}

    def added(names):
        return [(name, None, False) for name in names]

    own2 = {"keep2": keep2} | {f"other2_{i}": other for i, other in enumerate(other2)}
    own3 = {"keep3": keep3, "other3": other3}
    own4 = {"keep4": keep4, "other4": other4}

    def part2(i):
        return [("keep2", i, False), (f"other2_{i}", 0, False)]

    def part(step, s):
        return [(f"keep{step}", s, False), (f"other{step}", s, False)]

    came1 = came(1, come1)
    near1 = part2(0) + added(came1)
    *pay2, end1 = sums(came1 | own2, [*(part2(1 + s) for s in shifts), near1], after=[send4])
    came2 = came(2, [shift_mid(pay, s) for s, pay in zip(shifts, pay2)])
    from_end1 = {"end1": swap_pairs(end1)}
    turned_residual, factors = turn_residual(inner, residual, rows, had, after=[end1])
    picked = select_rows(inner, next_query_weight, cols, after=[factors])
    next_other = [swap_core(part) for part in picked]

    near2 = part2(1) + added(came2)
    *pay3, end2, mid2 = sums(
        came2 | from_end1 | own2 | own3 | came1,
        [*(part(3, s) for s in shifts), near2, near1 + [("end1", None, True)]],
        after=picked[:1],
    )
    came3 = came(3, [shift_mid(pay, s) for s, pay in zip(shifts, pay3)])
    from_end2 = {"end2": swap_pairs(end2)}
    from_mid2 = {"mid2": swap_middle(mid2)}

    *pay4, mid3, near3 = sums(
        came3 | from_end2 | from_mid2 | own2 | own3 | own4 | came2,
        [
            *(part(4, s) for s in shifts),
            near2 + [("end2", None, True)],
            part(3, 0) + added(came3) + [("mid2", None, True)],
        ],

    )
    come4 = [shift_mid(pay, s) for s, pay in zip(shifts, pay4)]
    from_mid3 = swap_middle(mid3)
    from_near3 = swap_pairs(near3)

    gain = norm_gain.astype(F32).reshape(-1, ROT)

    last = [*come4, from_near3, from_mid3, keep4, other4]
    items = [(None, False)] * (len(come4) + 1) + [(None, True)] + [(0, False)] * 2
    grid = regrid(inner, items, turned_residual, factors, last)

    x1 = [shift_mid(grid, s) for s in shifts]
    near = swap_pairs(grid)
    mid1 = swap_middle(grid)
    hidden_out, mark = hidden(inner, items, residual, factors, had, last, after=[grid])
    near, mid1 = gate([near, mid1], after=[*x1, mark])
    x2 = [shift_mid(near, s) for s in shifts]
    ends2 = swap_pairs(mid1)
    mids2 = swap_middle(near)
    third = choose(inner, mid1, ends2, after=x2)
    x3 = [shift_mid(third, s) for s in shifts]
    ends3 = swap_pairs(mids2)
    turned_next = turn_next(inner, next_query_weight, next_other, gain, rows, had, after=[third])
    fourth = choose(inner, mids2, ends3, after=[*x3, turned_next])
    x4 = [shift_mid(fourth, s) for s in shifts]
    acc = project(
        inner,
        turned_next,
        rows,
        None,
        [(0, 0, grid), (1, 0, near), (2, 0, third), (3, 0, fourth)]
        + [(phase, s, x[s - 1]) for phase, x in enumerate((x1, x2, x3)) for s in shifts],
    )
    own, other = project(
        inner, turned_next, rows, acc, [(3, s, x4[s - 1]) for s in shifts], split=True
    )
    query_next = finish(own, swap_core(other), norm_gain.shape[0])
    return (hidden_out, query_next)


def solution(mesh):
    placed = (
        P("tp", "groups", None),
        P("tp", "groups", None),
        P("tp", "groups", None),
        P("groups"),
        P("tp", None),
        P("groups", "tp"),
        P(),
        P(),
        P(None, "tp"),
    )
    return jax.shard_map(
        functools.partial(body, mesh.shape["tp"]),
        mesh=mesh,
        in_specs=placed,
        out_specs=(P("groups", "tp"), P("groups", "tp")),
        check_vma=False,
    )
```

```python
import functools
import math

import jax
import jax.numpy as jnp
import numpy as np
from jax import lax
from jax.experimental import pallas as pl
from jax.experimental.pallas import tpu as pltpu
from jax.sharding import PartitionSpec as P

HD = 128
ROT = 128
OUTER = 4

F32 = jnp.float32
BF16 = jnp.bfloat16
MIB = 1024 * 1024


def hadamard(length):
    rows = np.arange(length)
    common = rows[:, None] & rows[None, :]
    parity = np.zeros((length, length), np.int64)
    for bit in range(length.bit_length()):
        parity += (common >> bit) & 1
    return (1 - 2 * (parity & 1)).astype(np.float32)


def vmem():
    return pl.BlockSpec(memory_space=pltpu.VMEM)


def anywhere():
    return pl.BlockSpec(memory_space=pl.ANY)


def place(inner):
    index = lax.axis_index("tp")
    return lax.div(index, 2 * inner), lax.rem(lax.div(index, 2), inner), lax.rem(index, 2)


def targets(outer):
    low = outer < 2
    near = outer + 1 - 2 * lax.rem(outer, 2)
    return jnp.where(low, 3, 0), jnp.where(low, 2, 1), near, outer


def is_inner(outer):
    return jnp.logical_or(outer == 1, outer == 2)


def kernel_call(kernel, out_shape, arrays, specs, after=(), scratch=(), aliases=None, limit=24, name=None):
    extra = len(after)

    def ordered(*refs):
        kernel(*refs[extra:])

    return pl.pallas_call(
        ordered,
        out_shape=out_shape,
        in_specs=[anywhere()] * extra + list(specs),
        out_specs=jax.tree.map(lambda _: vmem(), out_shape),
        scratch_shapes=list(scratch),
        input_output_aliases=aliases or {},
        cost_estimate=pl.CostEstimate(flops=0, bytes_accessed=0, transcendentals=0),
        compiler_params=pltpu.CompilerParams(vmem_limit_bytes=limit * MIB),
        name=name,
    )(*after, *arrays)


def gridded(context, h_ref, weight, scale_row, store):
    cols = weight.shape[1]
    count = cols // ROT
    value = jnp.dot(context, weight, preferred_element_type=F32).astype(BF16)
    stacked = jnp.concatenate([value[:, i * ROT : (i + 1) * ROT] for i in range(count)], axis=0)
    turned = jnp.dot(stacked, h_ref[...], preferred_element_type=F32)
    tok = value.shape[0]
    for i in range(count):
        part = turned[i * tok : (i + 1) * tok] * scale_row(i)
        store(i, jnp.clip(part, -127.0, 127.0).astype(BF16))


def attend_kernel(
    inner, cols, chunk, q_hbm, k_hbm, v_hbm, w_hbm, pos_hbm, table_hbm, h_hbm,
    ctx_ref, rows_ref, send_ref, w_ref, h_ref, k_ref, v_ref, s_ref, q_ref, pos_ref, table_ref, sems,
):
    tok = q_ref.shape[0]
    slots = k_ref.shape[0]
    steps = slots // chunk
    outer, mid, core = place(inner)
    dest = targets(outer)[0]

    copies = min(4, steps)
    per_copy = steps // copies
    size = slots // copies

    def copy_k(j):
        part = pl.ds(j * size, size)
        return pltpu.make_async_copy(k_hbm.at[0, part], k_ref.at[part], sems.at[1 + j])

    def copy_v(j):
        part = pl.ds(j * size, size)
        return pltpu.make_async_copy(v_hbm.at[0, part], v_ref.at[part], sems.at[1 + steps + j])

    def shard_of(shift):
        return (dest * inner + lax.rem(mid + shift, inner)) * 2 + 1 - core

    copy_w = pltpu.make_async_copy(w_hbm, w_ref, sems.at[2 * steps + 1])
    copy_q = pltpu.make_async_copy(q_hbm.at[0], q_ref, sems.at[0])
    copy_pos = pltpu.make_async_copy(pos_hbm, pos_ref, sems.at[2 * steps + 2])
    copy_table = pltpu.make_async_copy(table_hbm, table_ref, sems.at[2 * steps + 3])
    copy_h = pltpu.make_async_copy(h_hbm, h_ref, sems.at[2 * steps + 4])
    copy_q.start()
    copy_pos.start()
    for j in range(copies):
        copy_k(j).start()
    copy_table.start()
    copy_h.start()
    for j in range(copies):
        copy_v(j).start()
    copy_w.start()

    copy_pos.wait()
    positions = jnp.broadcast_to(pos_ref[...].astype(F32), (ROT, tok)).T
    ahead = positions.astype(jnp.int32) - lax.broadcasted_iota(jnp.int32, (tok, ROT), 1)

    copy_q.wait()
    queries = q_ref[...]
    peak = jnp.full((tok, ROT), -jnp.inf, F32)
    for j in range(steps):
        if j % per_copy == 0:
            copy_k(j // per_copy).wait()
        scores = lax.dot_general(
            queries, k_ref[j * chunk : (j + 1) * chunk], (((1,), (1,)), ((), ())),
            preferred_element_type=F32,
        )
        for i in range(chunk // ROT):
            base = j * chunk + i * ROT
            part = jnp.where(ahead >= base, scores[:, i * ROT : (i + 1) * ROT], -jnp.inf)
            s_ref[:, base : base + ROT] = part
            peak = jnp.maximum(peak, part)
    copy_table.wait()
    table = table_ref[...].astype(F32)
    count = table.shape[1]
    for i in range(2):
        rows_ref[i] = jnp.broadcast_to(table[i : i + 1], (ROT, count)).T
    largest = jnp.max(peak, axis=1, keepdims=True)
    factor = math.log2(math.e) / math.sqrt(HD)
    total = jnp.zeros((tok, ROT), F32)
    acc = jnp.zeros((tok, HD), F32)
    for j in range(copies):
        copy_v(j).wait()
    for j in range(steps):
        pieces = []
        for i in range(chunk // ROT):
            base = j * chunk + i * ROT
            raised = jnp.exp2((s_ref[:, base : base + ROT] - largest) * factor)
            total = total + raised
            pieces.append(raised.astype(BF16))
        acc = acc + jnp.dot(
            jnp.concatenate(pieces, axis=1), v_ref[j * chunk : (j + 1) * chunk],
            preferred_element_type=F32,
        )
    context = (acc / jnp.sum(total, axis=1, keepdims=True)).astype(BF16)
    ctx_ref[...] = context

    per = cols // ROT
    copy_h.wait()
    copy_w.wait()
    for shift in range(1, inner):
        first = shard_of(shift) * per
        start = pl.multiple_of(shard_of(shift) * cols, 128)

        def scale_row(i):
            return (65536.0 / math.sqrt(ROT)) / rows_ref[0, pl.ds(first + i, 1), :]

        def store(i, value):
            send_ref[shift - 1, :, i * ROT : (i + 1) * ROT] = value

        gridded(context, h_ref, w_ref[:, pl.ds(start, cols)], scale_row, store)


def attend(inner, cols, queries, keys, values, weight, positions, table, had):
    tok, slots = queries.shape[1], keys.shape[1]
    chunk = min(1024, slots)
    steps = slots // chunk
    blocks = table.shape[1]
    arrays = [queries, keys, values, weight, positions[None, :], table, had]
    return kernel_call(
        functools.partial(attend_kernel, inner, cols, chunk),
        [
            pltpu.VMEM((tok, HD), BF16),
            pltpu.VMEM((2, blocks, ROT), F32),
            pltpu.VMEM((inner - 1, tok, cols), BF16),
            pltpu.VMEM(weight.shape, BF16),
            pltpu.VMEM(had.shape, BF16),
        ],
        [pltpu.with_memory_space_constraint(array, pltpu.HBM) for array in arrays],
        [pl.BlockSpec(memory_space=pltpu.HBM)] * len(arrays),
        scratch=[
            pltpu.VMEM((slots, HD), BF16),
            pltpu.VMEM((slots, HD), BF16),
            pltpu.VMEM((tok, slots), F32),
            pltpu.VMEM((tok, HD), BF16),
            pltpu.VMEM((1, tok), positions.dtype),
            pltpu.VMEM(table.shape, table.dtype),
            pltpu.SemaphoreType.DMA((2 * steps + 5,)),
        ],
        limit=28,
        name="attend",
    )


def partial_kernel(inner, work, ctx_ref, w_ref, rows_ref, h_ref, *out_refs):
    cols = out_refs[0].shape[2]
    per = cols // ROT
    outer, mid, core = place(inner)
    dests = targets(outer)
    context = ctx_ref[...]
    for out_ref, (mine, blocks) in zip(out_refs, work):
        for at, (phase, shift) in enumerate(blocks):
            shard = (dests[phase] * inner + lax.rem(mid + shift, inner)) * 2
            shard = shard + (core if mine else 1 - core)

            def scale_row(i):
                return (65536.0 / math.sqrt(ROT)) / rows_ref[0, pl.ds(shard * per + i, 1), :]

            def store(i, value):
                out_ref[at, :, i * ROT : (i + 1) * ROT] = value

            start = pl.multiple_of(shard * cols, 128)
            gridded(context, h_ref, w_ref[:, pl.ds(start, cols)], scale_row, store)


def partials(inner, cols, work, context, weight, rows, had, after=()):
    tok = context.shape[0]
    count = sum(len(blocks) for _, blocks in work)
    return kernel_call(
        functools.partial(partial_kernel, inner, work),
        [jax.ShapeDtypeStruct((len(blocks), tok, cols), BF16) for _, blocks in work],
        [context, weight, rows, had],
        [vmem()] * 4,
        after=after,
        name="partials",
    )


def add_kernel(inner, inputs, outputs, *refs):
    ins, outs = refs[:inputs], refs[inputs:]
    outer = place(inner)[0]
    for out_ref, items in zip(outs, outputs):
        total = None
        for which, at, inner_only in items:
            value = (ins[which][...] if at is None else ins[which][at]).astype(F32)
            if inner_only:
                value = jnp.where(is_inner(outer), value, 0.0)
            total = value if total is None else total + value
        out_ref[...] = total.astype(BF16)


def add_up(inner, arrays, outputs, after=()):
    shape = arrays[0].shape[-2:]
    terms = sum(len(items) for items in outputs)
    return kernel_call(
        functools.partial(add_kernel, inner, len(arrays), outputs),
        [jax.ShapeDtypeStruct(shape, BF16)] * len(outputs),
        arrays,
        [vmem()] * len(arrays),
        after=after,
        name="add_up",
    )


def turn_residual_kernel(inner, res_ref, rows_ref, h_ref, out_ref, factor_ref):
    per = res_ref.shape[1] // ROT
    first = lax.axis_index("tp") * per
    for i in range(per):
        part = slice(i * ROT, (i + 1) * ROT)
        high = 256.0 / rows_ref[1, pl.ds(first + i, 1), :]
        low = rows_ref[0, pl.ds(first + i, 1), :] * (1.0 / 65536.0)
        turned = jnp.dot(res_ref[:, part], h_ref[...], preferred_element_type=F32)
        out_ref[:, part] = turned * (high * (1.0 / math.sqrt(ROT)))
        factor_ref[0:1, part] = low * high
        factor_ref[1:2, part] = low


def turn_residual(inner, residual, rows, had, after=()):
    return kernel_call(
        functools.partial(turn_residual_kernel, inner),
        [
            jax.ShapeDtypeStruct(residual.shape, F32),
            jax.ShapeDtypeStruct((2, residual.shape[1]), F32),
        ],
        [residual, rows, had],
        [vmem()] * 3,
        after=after,
        name="turn_residual",
    )


def summed_at(inner, items, ins, part):
    outer = place(inner)[0]
    total = None
    for (at, inner_only), ref in zip(items, ins):
        value = (ref[:, part] if at is None else ref[at, :, part]).astype(F32)
        if inner_only:
            value = jnp.where(is_inner(outer), value, 0.0)
        total = value if total is None else total + value
    return total


def regrid_kernel(inner, items, *refs):
    *ins, turned_ref, factor_ref, grid_ref = refs
    for i in range(turned_ref.shape[1] // ROT):
        part = slice(i * ROT, (i + 1) * ROT)
        value = turned_ref[:, part] + summed_at(inner, items, ins, part) * factor_ref[0:1, part]
        grid_ref[:, part] = jnp.clip(value, -127.0, 127.0).astype(BF16)


def regrid(inner, items, turned, factors, arrays, after=()):
    return kernel_call(
        functools.partial(regrid_kernel, inner, items),
        jax.ShapeDtypeStruct(turned.shape, BF16),
        [*arrays, turned, factors],
        [vmem()] * (2 + len(arrays)),
        after=after,
        name="regrid",
    )


def hidden_kernel(inner, items, res_ref, factor_ref, h_ref, *refs):
    *ins, out_ref, mark_ref = refs
    mark_ref[...] = jnp.zeros_like(mark_ref)
    for i in range(res_ref.shape[1] // ROT):
        part = slice(i * ROT, (i + 1) * ROT)
        value = summed_at(inner, items, ins, part) * factor_ref[1:2, part]
        upper = value.astype(BF16)
        lower = (value - upper.astype(F32)).astype(BF16)
        turned = jnp.dot(upper, h_ref[...], preferred_element_type=F32)
        turned = turned + jnp.dot(lower, h_ref[...], preferred_element_type=F32)
        stream = res_ref[:, part].astype(F32) + turned * (1.0 / math.sqrt(ROT))
        out_ref[:, part] = stream.astype(BF16)


def hidden(inner, items, residual, factors, had, arrays, after=()):
    return kernel_call(
        functools.partial(hidden_kernel, inner, items),
        [jax.ShapeDtypeStruct(residual.shape, BF16), jax.ShapeDtypeStruct((8, ROT), F32)],
        [residual, factors, had, *arrays],
        [vmem()] * (3 + len(arrays)),
        after=after,
        name="hidden",
    )


HALVES = 2


def halves(shape):
    rows = shape[0] // HALVES
    return [jax.ShapeDtypeStruct((rows, *shape[1:]), BF16)] * HALVES


def split_rows(value_ref, out_refs):
    rows = out_refs[0].shape[0]
    for i, out_ref in enumerate(out_refs):
        out_ref[...] = value_ref[i * rows : (i + 1) * rows]


def choose_kernel(inner, inner_ref, end_ref, *out_refs):
    inside = is_inner(place(inner)[0])

    @pl.when(inside)
    def _():
        split_rows(inner_ref, out_refs)

    @pl.when(jnp.logical_not(inside))
    def _():
        split_rows(end_ref, out_refs)


def choose(inner, at_inner, at_end, after=()):
    return kernel_call(
        functools.partial(choose_kernel, inner),
        halves(at_inner.shape),
        [at_inner, at_end],
        [vmem()] * 2,
        after=after,
        name="choose",
    )


def gate(arrays, after):
    def kernel(*refs):
        pass

    shapes = [jax.ShapeDtypeStruct(array.shape, array.dtype) for array in arrays]
    aliases = {len(after) + i: i for i in range(len(arrays))}
    specs = [vmem()] * len(arrays)
    return kernel_call(kernel, shapes, arrays, specs, after=after, aliases=aliases, name="gate")


def select_rows_kernel(inner, cols, w_ref, *out_refs):
    other = 1 - place(inner)[2]
    each = out_refs[0].shape[0]
    for j in range(each * len(out_refs)):
        start = pl.multiple_of((2 * j + other) * cols, 128)
        out_refs[j // each][j % each] = w_ref[pl.ds(start, cols), :]


def select_rows(inner, weight, cols, after=()):
    parts = 2
    each = OUTER * inner // parts
    return kernel_call(
        functools.partial(select_rows_kernel, inner, cols),
        [jax.ShapeDtypeStruct((each, cols, weight.shape[1]), weight.dtype)] * parts,
        [weight],
        [vmem()],
        after=after,
        name="select_rows",
    )


def turn_next_kernel(inner, cols, own_ref, gain_ref, rows_ref, h_ref, *refs):
    *other_refs, out_ref = refs
    each = other_refs[0].shape[0]
    core = place(inner)[2]
    for j in range(out_ref.shape[0]):
        shard = j * 2 + core
        for i in range(cols // ROT):
            block = shard * (cols // ROT) + i
            factor = rows_ref[1, pl.ds(block, 1), :] * (1.0 / (256.0 * math.sqrt(ROT)))
            rotation = (h_ref[...].astype(F32) * gain_ref[pl.ds(block, 1), :]).astype(BF16)
            part = slice(i * ROT, (i + 1) * ROT)
            own = own_ref[pl.ds(pl.multiple_of(block * ROT, ROT), ROT), :]
            for half, value in enumerate((own, other_refs[j // each][j % each, part, :])):
                turned = jnp.dot(rotation, value, preferred_element_type=F32)
                out_ref[j, part, half * HD : (half + 1) * HD] = (turned * factor).astype(BF16)


def turn_next(inner, weight, others, gain, rows, had, after=()):
    _, cols, width = others[0].shape
    return kernel_call(
        functools.partial(turn_next_kernel, inner, cols),
        jax.ShapeDtypeStruct((OUTER * inner, cols, 2 * width), BF16),
        [weight, gain, rows, had, *others],
        [vmem()] * (4 + len(others)),
        after=after,
        name="turn_next",
    )


def project_kernel(inner, places, has_acc, split, w_ref, rows_ref, *refs):
    outer, mid, core = place(inner)
    far, third, near, own = targets(outer)
    order = (own, near, third, far)
    acc_in = refs[0] if has_acc else None
    refs = refs[1:] if has_acc else refs
    count = sum(parts for _, _, parts in places)
    values_in = list(refs[:count])
    outs = refs[count:]
    cols, width = w_ref.shape[1:]
    acc = acc_in[:, :width] if has_acc else 0.0
    squares = acc_in[:, width:] if has_acc else 0.0
    for phase, shift, parts in places:
        block = order[phase] * inner + lax.rem(mid + inner - shift, inner)
        values = [values_in.pop(0)[...] for _ in range(parts)]
        values = values[0] if parts == 1 else jnp.concatenate(values, axis=0)
        acc = acc + jnp.dot(values, w_ref[block], preferred_element_type=F32)
        for i in range(cols // ROT):
            row = (block * 2 + core) * (cols // ROT) + i
            high = rows_ref[1, pl.ds(row, 1), :] * (1.0 / 256.0)
            value = values[:, i * ROT : (i + 1) * ROT].astype(F32) * high
            squares = squares + value * value
    if split:
        own_ref, other_ref = outs
        own_ref[:, :HD] = acc[:, :HD]
        own_ref[:, HD:] = squares
        other_ref[:, :HD] = acc[:, HD:]
        other_ref[:, HD:] = squares
    else:
        outs[0][:, :width] = acc
        outs[0][:, width:] = squares


def project(inner, weight, rows, acc, pieces, split=False, after=()):
    _, cols, width = weight.shape
    arrays = [part for _, _, parts in pieces for part in parts]
    tok = sum(part.shape[0] for part in pieces[0][2])
    places = tuple((phase, shift, len(parts)) for phase, shift, parts in pieces)
    accs = [] if acc is None else [acc]
    if split:
        out = [jax.ShapeDtypeStruct((tok, HD + ROT), F32)] * 2
    else:
        out = jax.ShapeDtypeStruct((tok, width + ROT), F32)
    return kernel_call(
        functools.partial(project_kernel, inner, places, acc is not None, split),
        out,
        [weight, rows, *accs, *arrays],
        [vmem()] * (2 + len(accs) + len(arrays)),
        after=after,
        name="project",
    )


def finish_kernel(features, own_ref, other_ref, out_ref):
    squares = own_ref[:, HD:] + other_ref[:, HD:]
    mean = jnp.sum(squares, axis=1, keepdims=True) * (1.0 / features)
    value = (own_ref[:, :HD] + other_ref[:, :HD]) * lax.rsqrt(mean + 1e-05)
    out_ref[...] = value.astype(BF16)


def finish(own, other, features):
    tok = own.shape[0]
    return kernel_call(
        functools.partial(finish_kernel, features),
        jax.ShapeDtypeStruct((tok, HD), BF16),
        [own, other],
        [vmem()] * 2,
        name="finish",
    )


def body(
    size,
    queries,
    cache_keys,
    cache_values,
    query_positions,
    out_weight,
    residual,
    scale_table,
    norm_gain,
    next_query_weight,
):
    inner = size // (2 * OUTER)
    cols = residual.shape[1]
    had = jnp.asarray(hadamard(ROT), BF16)
    shifts = range(1, inner)

    def permute(value, move):
        moves = []
        for i in range(size):
            spot = move(i // (2 * inner), (i // 2) % inner, i % 2)
            moves.append((i, (spot[0] * inner + spot[1]) * 2 + spot[2]))
        return lax.ppermute(value, "tp", moves)

    def swap_core(value):
        return permute(value, lambda a, b, c: (a, b, 1 - c))

    def shift_mid(value, shift):
        return permute(value, lambda a, b, c: (a, (b + shift) % inner, c))

    def swap_pairs(value):
        return permute(value, lambda a, b, c: (a ^ 1, b, c))

    def swap_middle(value):
        return permute(value, lambda a, b, c: (a, b, 1 - c) if a in (0, 3) else (3 - a, b, c))

    everything = range(inner)
    context, rows, send1, out_weight, had = attend(
        inner, cols, queries, cache_keys, cache_values, out_weight, query_positions, scale_table, had
    )
    other1 = swap_core(send1)
    away1 = tuple((0, s) for s in shifts)
    def phase_blocks(phase):
        return tuple((phase, s) for s in everything)

    def grid_blocks(work, after=()):
        return partials(inner, cols, work, context, out_weight, rows, had, after=after)

    blocks2 = ((0, 0),) + tuple((1, s) for s in shifts)
    keep1, keep2, *send2 = grid_blocks(
        ((True, away1), (True, blocks2), *((False, (block,)) for block in blocks2))
    )
    other2 = [swap_core(send) for send in send2]
    items1 = [((0, s - 1, False), (1, s - 1, False)) for s in shifts]
    pay1 = add_up(inner, [keep1, other1], items1, after=[keep2])
    come1 = [shift_mid(pay, s) for s, pay in zip(shifts, pay1)]
    near_block = ((1, 0),)
    send2n, send3 = grid_blocks(((False, near_block), (False, phase_blocks(2))), pay1[:1])
    other2n, other3 = swap_core(send2n), swap_core(send3)
    send4, keep2n, keep3, keep4 = grid_blocks(
        (
            (False, phase_blocks(3)),
            (True, near_block),
            (True, phase_blocks(2)),
            (True, phase_blocks(3)),
        ),
        [send3],
    )
    other4 = swap_core(send4)

    def sums(arrays, outputs, after=()):
        names = list(arrays)
        items = [[(names.index(name), at, only) for name, at, only in output] for output in outputs]
        return add_up(inner, list(arrays.values()), items, after=after)

    def came(step, blocks):
        return {f"came{step}_{s}": block for s, block in zip(shifts, blocks)}

    def added(names):
        return [(name, None, False) for name in names]

    own2 = {"keep2": keep2} | {f"other2_{i}": other for i, other in enumerate(other2)}
    own2n = {"keep2n": keep2n, "other2n": other2n}
    own3 = {"keep3": keep3, "other3": other3}
    own4 = {"keep4": keep4, "other4": other4}

    def part2(i):
        return [("keep2", i, False), (f"other2_{i}", 0, False)]

    def part(step, s):
        return [(f"keep{step}", s, False), (f"other{step}", s, False)]

    came1 = came(1, come1)
    near1 = part2(0) + added(came1)
    *pay2, end1 = sums(came1 | own2, [*(part2(s) for s in shifts), near1], after=[send4])
    came2 = came(2, [shift_mid(pay, s) for s, pay in zip(shifts, pay2)])
    from_end1 = {"end1": swap_pairs(end1)}
    turned_residual, factors = turn_residual(inner, residual, rows, had, after=[end1])
    picked = select_rows(inner, next_query_weight, cols, after=[factors])
    next_other = [swap_core(part) for part in picked]

    near2 = part("2n", 0) + added(came2)
    *pay3, end2, mid2 = sums(
        came2 | from_end1 | own2 | own2n | own3 | came1,
        [*(part(3, s) for s in shifts), near2, near1 + [("end1", None, True)]],
        after=picked[:1],
    )
    came3 = came(3, [shift_mid(pay, s) for s, pay in zip(shifts, pay3)])
    from_end2 = {"end2": swap_pairs(end2)}
    from_mid2 = {"mid2": swap_middle(mid2)}

    *pay4, mid3, near3 = sums(
        came3 | from_end2 | from_mid2 | own2n | own3 | own4 | came2,
        [
            *(part(4, s) for s in shifts),
            near2 + [("end2", None, True)],
            part(3, 0) + added(came3) + [("mid2", None, True)],
        ],

    )
    come4 = [shift_mid(pay, s) for s, pay in zip(shifts, pay4)]
    from_mid3 = swap_middle(mid3)
    from_near3 = swap_pairs(near3)

    gain = norm_gain.astype(F32).reshape(-1, ROT)

    last = [*come4, from_near3, from_mid3, keep4, other4]
    items = [(None, False)] * (len(come4) + 1) + [(None, True)] + [(0, False)] * 2
    grid = regrid(inner, items, turned_residual, factors, last)

    x1 = [shift_mid(grid, s) for s in shifts]
    near = swap_pairs(grid)
    mid1 = swap_middle(grid)
    hidden_out, mark = hidden(inner, items, residual, factors, had, last, after=[grid])
    near, mid1 = gate([near, mid1], after=[*x1, mark])

    def shift_parts(parts, shift):
        return [shift_mid(part, shift) for part in parts]

    x2 = [shift_mid(near, s) for s in shifts]
    ends2 = swap_pairs(mid1)
    mids2 = swap_middle(near)
    third = choose(inner, mid1, ends2, after=x2)
    x3 = [shift_parts(third, s) for s in shifts]
    ends3 = swap_pairs(mids2)
    turned_next = turn_next(
        inner, next_query_weight, next_other, gain, rows, had, after=third[:1]
    )
    fourth = choose(inner, mids2, ends3, after=[*sum(x3, []), turned_next])
    x4 = [shift_parts(fourth, s) for s in shifts]
    acc = project(
        inner,
        turned_next,
        rows,
        None,
        [(0, 0, [grid]), (1, 0, [near]), (2, 0, third), (3, 0, fourth)]
        + [(phase, s, [x[s - 1]]) for phase, x in enumerate((x1, x2)) for s in shifts]
        + [(2, s, x3[s - 1]) for s in shifts],
    )
    own, other = project(
        inner, turned_next, rows, acc, [(3, s, x4[s - 1]) for s in shifts], split=True
    )
    query_next = finish(own, swap_core(other), norm_gain.shape[0])
    return (hidden_out, query_next)


def solution(mesh):
    placed = (
        P("tp", "groups", None),
        P("tp", "groups", None),
        P("tp", "groups", None),
        P("groups"),
        P("tp", None),
        P("groups", "tp"),
        P(),
        P(),
        P(None, "tp"),
    )
    return jax.shard_map(
        functools.partial(body, mesh.shape["tp"]),
        mesh=mesh,
        in_specs=placed,
        out_specs=(P("groups", "tp"), P("groups", "tp")),
        check_vma=False,
    )
```

```python
import functools
import math

import jax
import jax.numpy as jnp
import numpy as np
from jax import lax
from jax.experimental import pallas as pl
from jax.experimental.pallas import tpu as pltpu
from jax.sharding import PartitionSpec as P

HD = 128
ROT = 128
OUTER = 4

F32 = jnp.float32
BF16 = jnp.bfloat16
MIB = 1024 * 1024


def hadamard(length):
    rows = np.arange(length)
    common = rows[:, None] & rows[None, :]
    parity = np.zeros((length, length), np.int64)
    for bit in range(length.bit_length()):
        parity += (common >> bit) & 1
    return (1 - 2 * (parity & 1)).astype(np.float32)


def vmem():
    return pl.BlockSpec(memory_space=pltpu.VMEM)


def anywhere():
    return pl.BlockSpec(memory_space=pl.ANY)


def place(inner):
    index = lax.axis_index("tp")
    return lax.div(index, 2 * inner), lax.rem(lax.div(index, 2), inner), lax.rem(index, 2)


def targets(outer):
    low = outer < 2
    near = outer + 1 - 2 * lax.rem(outer, 2)
    return jnp.where(low, 3, 0), jnp.where(low, 2, 1), near, outer


def is_inner(outer):
    return jnp.logical_or(outer == 1, outer == 2)


def kernel_call(kernel, out_shape, arrays, specs, after=(), scratch=(), aliases=None, limit=24, name=None):
    extra = len(after)

    def ordered(*refs):
        kernel(*refs[extra:])

    return pl.pallas_call(
        ordered,
        out_shape=out_shape,
        in_specs=[anywhere()] * extra + list(specs),
        out_specs=jax.tree.map(lambda _: vmem(), out_shape),
        scratch_shapes=list(scratch),
        input_output_aliases=aliases or {},
        cost_estimate=pl.CostEstimate(flops=0, bytes_accessed=0, transcendentals=0),
        compiler_params=pltpu.CompilerParams(vmem_limit_bytes=limit * MIB),
        name=name,
    )(*after, *arrays)


def gridded(context, h_ref, weight, scale_row, store):
    cols = weight.shape[1]
    count = cols // ROT
    value = jnp.dot(context, weight, preferred_element_type=F32).astype(BF16)
    stacked = jnp.concatenate([value[:, i * ROT : (i + 1) * ROT] for i in range(count)], axis=0)
    turned = jnp.dot(stacked, h_ref[...], preferred_element_type=F32)
    tok = value.shape[0]
    for i in range(count):
        part = turned[i * tok : (i + 1) * tok] * scale_row(i)
        store(i, jnp.clip(part, -127.0, 127.0).astype(BF16))


def attend_kernel(
    inner, cols, chunk, q_hbm, k_hbm, v_hbm, w_hbm, pos_hbm, table_hbm, h_hbm,
    ctx_ref, rows_ref, send_ref, w_ref, h_ref, k_ref, v_ref, s_ref, q_ref, pos_ref, table_ref, sems,
):
    tok = q_ref.shape[0]
    slots = k_ref.shape[0]
    steps = slots // chunk
    outer, mid, core = place(inner)
    dest = targets(outer)[0]

    copies = min(4, steps)
    per_copy = steps // copies
    size = slots // copies

    def copy_k(j):
        part = pl.ds(j * size, size)
        return pltpu.make_async_copy(k_hbm.at[0, part], k_ref.at[part], sems.at[1 + j])

    def copy_v(j):
        part = pl.ds(j * size, size)
        return pltpu.make_async_copy(v_hbm.at[0, part], v_ref.at[part], sems.at[1 + steps + j])

    def shard_of(shift):
        return (dest * inner + lax.rem(mid + shift, inner)) * 2 + 1 - core

    copy_w = pltpu.make_async_copy(w_hbm, w_ref, sems.at[2 * steps + 1])
    copy_q = pltpu.make_async_copy(q_hbm.at[0], q_ref, sems.at[0])
    copy_pos = pltpu.make_async_copy(pos_hbm, pos_ref, sems.at[2 * steps + 2])
    copy_table = pltpu.make_async_copy(table_hbm, table_ref, sems.at[2 * steps + 3])
    copy_h = pltpu.make_async_copy(h_hbm, h_ref, sems.at[2 * steps + 4])
    copy_q.start()
    copy_pos.start()
    for j in range(copies):
        copy_k(j).start()
    copy_table.start()
    copy_h.start()
    for j in range(copies):
        copy_v(j).start()
    copy_w.start()

    copy_pos.wait()
    positions = jnp.broadcast_to(pos_ref[...].astype(F32), (ROT, tok)).T
    ahead = positions.astype(jnp.int32) - lax.broadcasted_iota(jnp.int32, (tok, ROT), 1)

    copy_q.wait()
    queries = q_ref[...]
    peak = jnp.full((tok, ROT), -jnp.inf, F32)
    for j in range(steps):
        if j % per_copy == 0:
            copy_k(j // per_copy).wait()
        scores = lax.dot_general(
            queries, k_ref[j * chunk : (j + 1) * chunk], (((1,), (1,)), ((), ())),
            preferred_element_type=F32,
        )
        for i in range(chunk // ROT):
            base = j * chunk + i * ROT
            part = jnp.where(ahead >= base, scores[:, i * ROT : (i + 1) * ROT], -jnp.inf)
            s_ref[:, base : base + ROT] = part
            peak = jnp.maximum(peak, part)
    copy_table.wait()
    table = table_ref[...].astype(F32)
    count = table.shape[1]
    for i in range(2):
        rows_ref[i] = jnp.broadcast_to(table[i : i + 1], (ROT, count)).T
    largest = jnp.max(peak, axis=1, keepdims=True)
    factor = math.log2(math.e) / math.sqrt(HD)
    total = jnp.zeros((tok, ROT), F32)
    acc = jnp.zeros((tok, HD), F32)
    for j in range(copies):
        copy_v(j).wait()
    for j in range(steps):
        pieces = []
        for i in range(chunk // ROT):
            base = j * chunk + i * ROT
            raised = jnp.exp2((s_ref[:, base : base + ROT] - largest) * factor)
            total = total + raised
            pieces.append(raised.astype(BF16))
        acc = acc + jnp.dot(
            jnp.concatenate(pieces, axis=1), v_ref[j * chunk : (j + 1) * chunk],
            preferred_element_type=F32,
        )
    context = (acc / jnp.sum(total, axis=1, keepdims=True)).astype(BF16)
    ctx_ref[...] = context

    per = cols // ROT
    copy_h.wait()
    copy_w.wait()
    for shift in range(1, inner):
        first = shard_of(shift) * per
        start = pl.multiple_of(shard_of(shift) * cols, 128)

        def scale_row(i):
            return (65536.0 / math.sqrt(ROT)) / rows_ref[0, pl.ds(first + i, 1), :]

        def store(i, value):
            send_ref[shift - 1, :, i * ROT : (i + 1) * ROT] = value

        gridded(context, h_ref, w_ref[:, pl.ds(start, cols)], scale_row, store)


def attend(inner, cols, queries, keys, values, weight, positions, table, had):
    tok, slots = queries.shape[1], keys.shape[1]
    chunk = min(1024, slots)
    steps = slots // chunk
    blocks = table.shape[1]
    arrays = [queries, keys, values, weight, positions[None, :], table, had]
    return kernel_call(
        functools.partial(attend_kernel, inner, cols, chunk),
        [
            pltpu.VMEM((tok, HD), BF16),
            pltpu.VMEM((2, blocks, ROT), F32),
            pltpu.VMEM((inner - 1, tok, cols), BF16),
            pltpu.VMEM(weight.shape, BF16),
            pltpu.VMEM(had.shape, BF16),
        ],
        [pltpu.with_memory_space_constraint(array, pltpu.HBM) for array in arrays],
        [pl.BlockSpec(memory_space=pltpu.HBM)] * len(arrays),
        scratch=[
            pltpu.VMEM((slots, HD), BF16),
            pltpu.VMEM((slots, HD), BF16),
            pltpu.VMEM((tok, slots), F32),
            pltpu.VMEM((tok, HD), BF16),
            pltpu.VMEM((1, tok), positions.dtype),
            pltpu.VMEM(table.shape, table.dtype),
            pltpu.SemaphoreType.DMA((2 * steps + 5,)),
        ],
        limit=28,
        name="attend",
    )


def partial_kernel(inner, work, ctx_ref, w_ref, rows_ref, h_ref, *out_refs):
    cols = out_refs[0].shape[2]
    per = cols // ROT
    outer, mid, core = place(inner)
    dests = targets(outer)
    context = ctx_ref[...]
    for out_ref, (mine, blocks) in zip(out_refs, work):
        for at, (phase, shift) in enumerate(blocks):
            shard = (dests[phase] * inner + lax.rem(mid + shift, inner)) * 2
            shard = shard + (core if mine else 1 - core)

            def scale_row(i):
                return (65536.0 / math.sqrt(ROT)) / rows_ref[0, pl.ds(shard * per + i, 1), :]

            def store(i, value):
                out_ref[at, :, i * ROT : (i + 1) * ROT] = value

            start = pl.multiple_of(shard * cols, 128)
            gridded(context, h_ref, w_ref[:, pl.ds(start, cols)], scale_row, store)


def partials(inner, cols, work, context, weight, rows, had, after=()):
    tok = context.shape[0]
    count = sum(len(blocks) for _, blocks in work)
    return kernel_call(
        functools.partial(partial_kernel, inner, work),
        [jax.ShapeDtypeStruct((len(blocks), tok, cols), BF16) for _, blocks in work],
        [context, weight, rows, had],
        [vmem()] * 4,
        after=after,
        name="partials",
    )


def add_kernel(inner, inputs, outputs, *refs):
    ins, outs = refs[:inputs], refs[inputs:]
    outer = place(inner)[0]
    for out_ref, items in zip(outs, outputs):
        total = None
        for which, at, inner_only in items:
            value = (ins[which][...] if at is None else ins[which][at]).astype(F32)
            if inner_only:
                value = jnp.where(is_inner(outer), value, 0.0)
            total = value if total is None else total + value
        out_ref[...] = total.astype(BF16)


def add_up(inner, arrays, outputs, after=()):
    shape = arrays[0].shape[-2:]
    terms = sum(len(items) for items in outputs)
    return kernel_call(
        functools.partial(add_kernel, inner, len(arrays), outputs),
        [jax.ShapeDtypeStruct(shape, BF16)] * len(outputs),
        arrays,
        [vmem()] * len(arrays),
        after=after,
        name="add_up",
    )


def turn_residual_kernel(inner, res_ref, rows_ref, h_ref, out_ref, factor_ref):
    per = res_ref.shape[1] // ROT
    first = lax.axis_index("tp") * per
    for i in range(per):
        part = slice(i * ROT, (i + 1) * ROT)
        high = 256.0 / rows_ref[1, pl.ds(first + i, 1), :]
        low = rows_ref[0, pl.ds(first + i, 1), :] * (1.0 / 65536.0)
        turned = jnp.dot(res_ref[:, part], h_ref[...], preferred_element_type=F32)
        out_ref[:, part] = turned * (high * (1.0 / math.sqrt(ROT)))
        factor_ref[0:1, part] = low * high
        factor_ref[1:2, part] = low


def turn_residual(inner, residual, rows, had, after=()):
    return kernel_call(
        functools.partial(turn_residual_kernel, inner),
        [
            jax.ShapeDtypeStruct(residual.shape, F32),
            jax.ShapeDtypeStruct((2, residual.shape[1]), F32),
        ],
        [residual, rows, had],
        [vmem()] * 3,
        after=after,
        name="turn_residual",
    )


def summed_at(inner, items, ins, part):
    outer = place(inner)[0]
    total = None
    for (at, inner_only), ref in zip(items, ins):
        value = (ref[:, part] if at is None else ref[at, :, part]).astype(F32)
        if inner_only:
            value = jnp.where(is_inner(outer), value, 0.0)
        total = value if total is None else total + value
    return total


def regrid_kernel(inner, items, *refs):
    *ins, turned_ref, factor_ref, grid_ref = refs
    for i in range(turned_ref.shape[1] // ROT):
        part = slice(i * ROT, (i + 1) * ROT)
        value = turned_ref[:, part] + summed_at(inner, items, ins, part) * factor_ref[0:1, part]
        grid_ref[:, part] = jnp.clip(value, -127.0, 127.0).astype(BF16)


def regrid(inner, items, turned, factors, arrays, after=()):
    return kernel_call(
        functools.partial(regrid_kernel, inner, items),
        jax.ShapeDtypeStruct(turned.shape, BF16),
        [*arrays, turned, factors],
        [vmem()] * (2 + len(arrays)),
        after=after,
        name="regrid",
    )


def hidden_kernel(inner, items, res_ref, factor_ref, h_ref, *refs):
    *ins, out_ref, mark_ref = refs
    mark_ref[...] = jnp.zeros_like(mark_ref)
    for i in range(res_ref.shape[1] // ROT):
        part = slice(i * ROT, (i + 1) * ROT)
        value = summed_at(inner, items, ins, part) * factor_ref[1:2, part]
        upper = value.astype(BF16)
        lower = (value - upper.astype(F32)).astype(BF16)
        turned = jnp.dot(upper, h_ref[...], preferred_element_type=F32)
        turned = turned + jnp.dot(lower, h_ref[...], preferred_element_type=F32)
        stream = res_ref[:, part].astype(F32) + turned * (1.0 / math.sqrt(ROT))
        out_ref[:, part] = stream.astype(BF16)


def hidden(inner, items, residual, factors, had, arrays, after=()):
    return kernel_call(
        functools.partial(hidden_kernel, inner, items),
        [jax.ShapeDtypeStruct(residual.shape, BF16), jax.ShapeDtypeStruct((8, ROT), F32)],
        [residual, factors, had, *arrays],
        [vmem()] * (3 + len(arrays)),
        after=after,
        name="hidden",
    )


def choose_kernel(inner, count, inner_ref, end_ref, *refs):
    inside = is_inner(place(inner)[0])
    others, out_ref, outs = refs[:count], refs[count], refs[count + 1 :]
    lower, upper = outs[:count], outs[count:]

    def put(ref):
        out_ref[...] = ref[...]
        for half in upper:
            half[...] = ref[: half.shape[0]]

    @pl.when(inside)
    def _():
        put(inner_ref)

    @pl.when(jnp.logical_not(inside))
    def _():
        put(end_ref)

    for ref, half in zip(others, lower):
        half[...] = ref[half.shape[0] :]


def choose(inner, at_inner, at_end, others=(), halved=False, after=()):
    rows, cols = at_inner.shape
    half = jax.ShapeDtypeStruct((rows // 2, cols), BF16)
    return kernel_call(
        functools.partial(choose_kernel, inner, len(others)),
        [jax.ShapeDtypeStruct((rows, cols), BF16)] + [half] * (len(others) + halved),
        [at_inner, at_end, *others],
        [vmem()] * (2 + len(others)),
        after=after,
        name="choose",
    )


def gate_kernel(count, *refs):
    for ref, half in zip(refs[:count], refs[-count:]):
        half[...] = ref[half.shape[0] :]


def gate(arrays, others, after):
    rows, cols = arrays[0].shape
    shapes = [jax.ShapeDtypeStruct((rows, cols), BF16)] * len(arrays)
    half = jax.ShapeDtypeStruct((rows // 2, cols), BF16)
    aliases = {len(after) + len(others) + i: i for i in range(len(arrays))}
    return kernel_call(
        functools.partial(gate_kernel, len(others)),
        shapes + [half] * len(others),
        [*others, *arrays],
        [vmem()] * (len(others) + len(arrays)),
        after=after,
        aliases=aliases,
        name="gate",
    )


def select_rows_kernel(inner, cols, w_ref, *out_refs):
    other = 1 - place(inner)[2]
    each = out_refs[0].shape[0]
    for j in range(each * len(out_refs)):
        start = pl.multiple_of((2 * j + other) * cols, 128)
        out_refs[j // each][j % each] = w_ref[pl.ds(start, cols), :]


def select_rows(inner, weight, cols, after=()):
    parts = 2
    each = OUTER * inner // parts
    return kernel_call(
        functools.partial(select_rows_kernel, inner, cols),
        [jax.ShapeDtypeStruct((each, cols, weight.shape[1]), weight.dtype)] * parts,
        [weight],
        [vmem()],
        after=after,
        name="select_rows",
    )


def turn_next_kernel(inner, cols, own_ref, gain_ref, rows_ref, h_ref, *refs):
    *other_refs, out_ref = refs
    each = other_refs[0].shape[0]
    core = place(inner)[2]
    for j in range(out_ref.shape[0]):
        shard = j * 2 + core
        for i in range(cols // ROT):
            block = shard * (cols // ROT) + i
            factor = rows_ref[1, pl.ds(block, 1), :] * (1.0 / (256.0 * math.sqrt(ROT)))
            rotation = (h_ref[...].astype(F32) * gain_ref[pl.ds(block, 1), :]).astype(BF16)
            part = slice(i * ROT, (i + 1) * ROT)
            own = own_ref[pl.ds(pl.multiple_of(block * ROT, ROT), ROT), :]
            for half, value in enumerate((own, other_refs[j // each][j % each, part, :])):
                turned = jnp.dot(rotation, value, preferred_element_type=F32)
                out_ref[j, part, half * HD : (half + 1) * HD] = (turned * factor).astype(BF16)


def turn_next(inner, weight, others, gain, rows, had, after=()):
    _, cols, width = others[0].shape
    return kernel_call(
        functools.partial(turn_next_kernel, inner, cols),
        jax.ShapeDtypeStruct((OUTER * inner, cols, 2 * width), BF16),
        [weight, gain, rows, had, *others],
        [vmem()] * (4 + len(others)),
        after=after,
        name="turn_next",
    )


def project_kernel(inner, places, has_acc, split, w_ref, rows_ref, *refs):
    outer, mid, core = place(inner)
    order = (outer, targets(outer)[2], lax.rem(outer + 2, OUTER), OUTER - 1 - outer)
    acc_in = refs[0] if has_acc else None
    refs = refs[1:] if has_acc else refs
    count = sum(parts for _, _, parts in places)
    values_in = list(refs[:count])
    outs = refs[count:]
    cols, width = w_ref.shape[1:]
    acc = acc_in[:, :width] if has_acc else 0.0
    squares = acc_in[:, width:] if has_acc else 0.0
    for phase, shift, parts in places:
        block = order[phase] * inner + lax.rem(mid + inner - shift, inner)
        values = values_in.pop(0)[...]
        if parts == 3:
            at_inner, at_end = values_in.pop(0)[...], values_in.pop(0)[...]
            lower = jnp.where(is_inner(outer), at_inner, at_end)
            values = jnp.concatenate([values, lower], axis=0)
        acc = acc + jnp.dot(values, w_ref[block], preferred_element_type=F32)
        for i in range(cols // ROT):
            row = (block * 2 + core) * (cols // ROT) + i
            high = rows_ref[1, pl.ds(row, 1), :] * (1.0 / 256.0)
            value = values[:, i * ROT : (i + 1) * ROT].astype(F32) * high
            squares = squares + value * value
    if split:
        own_ref, other_ref = outs
        own_ref[:, :HD] = acc[:, :HD]
        own_ref[:, HD:] = squares
        other_ref[:, :HD] = acc[:, HD:]
        other_ref[:, HD:] = squares
    else:
        outs[0][:, :width] = acc
        outs[0][:, width:] = squares


def project(inner, weight, rows, acc, pieces, split=False, after=()):
    _, cols, width = weight.shape
    arrays = [part for _, _, parts in pieces for part in parts]
    first = pieces[0][2]
    tok = first[0].shape[0] * (1 if len(first) == 1 else 2)
    places = tuple((phase, shift, len(parts)) for phase, shift, parts in pieces)
    accs = [] if acc is None else [acc]
    if split:
        out = [jax.ShapeDtypeStruct((tok, HD + ROT), F32)] * 2
    else:
        out = jax.ShapeDtypeStruct((tok, width + ROT), F32)
    return kernel_call(
        functools.partial(project_kernel, inner, places, acc is not None, split),
        out,
        [weight, rows, *accs, *arrays],
        [vmem()] * (2 + len(accs) + len(arrays)),
        after=after,
        name="project",
    )


def finish_kernel(features, own_ref, other_ref, out_ref):
    squares = own_ref[:, HD:] + other_ref[:, HD:]
    mean = jnp.sum(squares, axis=1, keepdims=True) * (1.0 / features)
    value = (own_ref[:, :HD] + other_ref[:, :HD]) * lax.rsqrt(mean + 1e-05)
    out_ref[...] = value.astype(BF16)


def finish(own, other, features):
    tok = own.shape[0]
    return kernel_call(
        functools.partial(finish_kernel, features),
        jax.ShapeDtypeStruct((tok, HD), BF16),
        [own, other],
        [vmem()] * 2,
        name="finish",
    )


def body(
    size,
    queries,
    cache_keys,
    cache_values,
    query_positions,
    out_weight,
    residual,
    scale_table,
    norm_gain,
    next_query_weight,
):
    inner = size // (2 * OUTER)
    cols = residual.shape[1]
    had = jnp.asarray(hadamard(ROT), BF16)
    shifts = range(1, inner)

    def permute(value, move):
        moves = []
        for i in range(size):
            spot = move(i // (2 * inner), (i // 2) % inner, i % 2)
            moves.append((i, (spot[0] * inner + spot[1]) * 2 + spot[2]))
        return lax.ppermute(value, "tp", moves)

    def swap_core(value):
        return permute(value, lambda a, b, c: (a, b, 1 - c))

    def shift_mid(value, shift):
        return permute(value, lambda a, b, c: (a, (b + shift) % inner, c))

    def swap_pairs(value):
        return permute(value, lambda a, b, c: (a ^ 1, b, c))

    def swap_middle(value):
        return permute(value, lambda a, b, c: (a, b, 1 - c) if a in (0, 3) else (3 - a, b, c))

    everything = range(inner)
    context, rows, send1, out_weight, had = attend(
        inner, cols, queries, cache_keys, cache_values, out_weight, query_positions, scale_table, had
    )
    other1 = swap_core(send1)
    away1 = tuple((0, s) for s in shifts)
    def phase_blocks(phase):
        return tuple((phase, s) for s in everything)

    def grid_blocks(work, after=()):
        return partials(inner, cols, work, context, out_weight, rows, had, after=after)

    blocks2 = ((0, 0),) + tuple((1, s) for s in shifts)
    keep1, keep2, *send2 = grid_blocks(
        ((True, away1), (True, blocks2), *((False, (block,)) for block in blocks2))
    )
    other2 = [swap_core(send) for send in send2]
    items1 = [((0, s - 1, False), (1, s - 1, False)) for s in shifts]
    pay1 = add_up(inner, [keep1, other1], items1, after=[keep2])
    come1 = [shift_mid(pay, s) for s, pay in zip(shifts, pay1)]
    near_block = ((1, 0),)
    send2n, send3 = grid_blocks(((False, near_block), (False, phase_blocks(2))), pay1[:1])
    other2n, other3 = swap_core(send2n), swap_core(send3)
    send4, keep2n, keep3, keep4 = grid_blocks(
        (
            (False, phase_blocks(3)),
            (True, near_block),
            (True, phase_blocks(2)),
            (True, phase_blocks(3)),
        ),
        [send3],
    )
    other4 = swap_core(send4)

    def sums(arrays, outputs, after=()):
        names = list(arrays)
        items = [[(names.index(name), at, only) for name, at, only in output] for output in outputs]
        return add_up(inner, list(arrays.values()), items, after=after)

    def came(step, blocks):
        return {f"came{step}_{s}": block for s, block in zip(shifts, blocks)}

    def added(names):
        return [(name, None, False) for name in names]

    own2 = {"keep2": keep2} | {f"other2_{i}": other for i, other in enumerate(other2)}
    own2n = {"keep2n": keep2n, "other2n": other2n}
    own3 = {"keep3": keep3, "other3": other3}
    own4 = {"keep4": keep4, "other4": other4}

    def part2(i):
        return [("keep2", i, False), (f"other2_{i}", 0, False)]

    def part(step, s):
        return [(f"keep{step}", s, False), (f"other{step}", s, False)]

    came1 = came(1, come1)
    near1 = part2(0) + added(came1)
    *pay2, end1 = sums(came1 | own2, [*(part2(s) for s in shifts), near1], after=[send4])
    came2 = came(2, [shift_mid(pay, s) for s, pay in zip(shifts, pay2)])
    from_end1 = {"end1": swap_pairs(end1)}
    turned_residual, factors = turn_residual(inner, residual, rows, had, after=[end1])
    picked = select_rows(inner, next_query_weight, cols, after=[factors])
    next_other = [swap_core(part) for part in picked]

    near2 = part("2n", 0) + added(came2)
    *pay3, end2, mid2 = sums(
        came2 | from_end1 | own2 | own2n | own3 | came1,
        [*(part(3, s) for s in shifts), near2, near1 + [("end1", None, True)]],
        after=picked[:1],
    )
    came3 = came(3, [shift_mid(pay, s) for s, pay in zip(shifts, pay3)])
    from_end2 = {"end2": swap_pairs(end2)}
    from_mid2 = {"mid2": swap_middle(mid2)}

    *pay4, mid3, near3 = sums(
        came3 | from_end2 | from_mid2 | own2n | own3 | own4 | came2,
        [
            *(part(4, s) for s in shifts),
            near2 + [("end2", None, True)],
            part(3, 0) + added(came3) + [("mid2", None, True)],
        ],

    )
    come4 = [shift_mid(pay, s) for s, pay in zip(shifts, pay4)]
    from_mid3 = swap_middle(mid3)
    from_near3 = swap_pairs(near3)

    gain = norm_gain.astype(F32).reshape(-1, ROT)

    last = [*come4, from_near3, from_mid3, keep4, other4]
    items = [(None, False)] * (len(come4) + 1) + [(None, True)] + [(0, False)] * 2
    grid = regrid(inner, items, turned_residual, factors, last)

    x1 = [shift_mid(grid, s) for s in shifts]
    near = swap_pairs(grid)
    mid1 = swap_middle(grid)
    hidden_out, mark = hidden(inner, items, residual, factors, had, last, after=[grid])
    near, mid1, *low1 = gate([near, mid1], x1, after=[mark])
    x2 = [shift_mid(near, s) for s in shifts]
    ends2 = swap_pairs(mid1)
    mids2 = swap_middle(near)
    (third,) = choose(inner, mids2, ends2, after=x2)
    x3 = [shift_mid(third, s) for s in shifts]
    ends3 = swap_pairs(mids2)
    side_middle = [swap_middle(low) for low in low1]
    turned_next = turn_next(inner, next_query_weight, next_other, gain, rows, had, after=[third])
    fourth, *low3, up4 = choose(inner, mid1, ends3, x3, True, after=[turned_next])
    x4 = [shift_mid(up4, s) for s in shifts]
    side_pairs = [swap_pairs(low) for low in low3]
    acc = project(
        inner,
        turned_next,
        rows,
        None,
        [(0, 0, [grid]), (1, 0, [near]), (2, 0, [third]), (3, 0, [fourth])]
        + [(phase, s, [x[s - 1]]) for phase, x in enumerate((x1, x2, x3)) for s in shifts],
    )
    own, other = project(
        inner,
        turned_next,
        rows,
        acc,
        [(3, s, [x4[s - 1], side_middle[s - 1], side_pairs[s - 1]]) for s in shifts],
        split=True,
    )
    query_next = finish(own, swap_core(other), norm_gain.shape[0])
    return (hidden_out, query_next)


def solution(mesh):
    placed = (
        P("tp", "groups", None),
        P("tp", "groups", None),
        P("tp", "groups", None),
        P("groups"),
        P("tp", None),
        P("groups", "tp"),
        P(),
        P(),
        P(None, "tp"),
    )
    return jax.shard_map(
        functools.partial(body, mesh.shape["tp"]),
        mesh=mesh,
        in_specs=placed,
        out_specs=(P("groups", "tp"), P("groups", "tp")),
        check_vma=False,
    )
```

```python
import functools
import math

import jax
import jax.numpy as jnp
import numpy as np
from jax import lax
from jax.experimental import pallas as pl
from jax.experimental.pallas import tpu as pltpu
from jax.sharding import PartitionSpec as P

HD = 128
ROT = 128
OUTER = 4

F32 = jnp.float32
BF16 = jnp.bfloat16
MIB = 1024 * 1024


def hadamard(length):
    rows = np.arange(length)
    common = rows[:, None] & rows[None, :]
    parity = np.zeros((length, length), np.int64)
    for bit in range(length.bit_length()):
        parity += (common >> bit) & 1
    return (1 - 2 * (parity & 1)).astype(np.float32)


def vmem():
    return pl.BlockSpec(memory_space=pltpu.VMEM)


def anywhere():
    return pl.BlockSpec(memory_space=pl.ANY)


def place(inner):
    index = lax.axis_index("tp")
    return lax.div(index, 2 * inner), lax.rem(lax.div(index, 2), inner), lax.rem(index, 2)


def targets(outer):
    near = outer + 1 - 2 * lax.rem(outer, 2)
    return OUTER - 1 - outer, lax.rem(outer + 2, OUTER), near, outer


def is_inner(outer):
    return jnp.logical_or(outer == 1, outer == 2)


def kernel_call(kernel, out_shape, arrays, specs, after=(), scratch=(), aliases=None, limit=24, name=None):
    extra = len(after)

    def ordered(*refs):
        kernel(*refs[extra:])

    return pl.pallas_call(
        ordered,
        out_shape=out_shape,
        in_specs=[anywhere()] * extra + list(specs),
        out_specs=jax.tree.map(lambda _: vmem(), out_shape),
        scratch_shapes=list(scratch),
        input_output_aliases=aliases or {},
        cost_estimate=pl.CostEstimate(flops=0, bytes_accessed=0, transcendentals=0),
        compiler_params=pltpu.CompilerParams(vmem_limit_bytes=limit * MIB),
        name=name,
    )(*after, *arrays)


def gridded(context, h_ref, weight, scale_row, store):
    cols = weight.shape[1]
    count = cols // ROT
    value = jnp.dot(context, weight, preferred_element_type=F32).astype(BF16)
    stacked = jnp.concatenate([value[:, i * ROT : (i + 1) * ROT] for i in range(count)], axis=0)
    turned = jnp.dot(stacked, h_ref[...], preferred_element_type=F32)
    tok = value.shape[0]
    for i in range(count):
        part = turned[i * tok : (i + 1) * tok] * scale_row(i)
        store(i, jnp.clip(part, -127.0, 127.0).astype(BF16))


def attend_kernel(
    inner, cols, chunk, q_hbm, k_hbm, v_hbm, w_hbm, pos_hbm, table_hbm, h_hbm,
    ctx_ref, rows_ref, send_ref, w_ref, h_ref, k_ref, v_ref, s_ref, q_ref, pos_ref, table_ref, sems,
):
    tok = q_ref.shape[0]
    slots = k_ref.shape[0]
    steps = slots // chunk
    outer, mid, core = place(inner)
    dest = targets(outer)[0]

    copies = min(4, steps)
    per_copy = steps // copies
    size = slots // copies

    def copy_k(j):
        part = pl.ds(j * size, size)
        return pltpu.make_async_copy(k_hbm.at[0, part], k_ref.at[part], sems.at[1 + j])

    def copy_v(j):
        part = pl.ds(j * size, size)
        return pltpu.make_async_copy(v_hbm.at[0, part], v_ref.at[part], sems.at[1 + steps + j])

    def shard_of(shift):
        return (dest * inner + lax.rem(mid + shift, inner)) * 2 + 1 - core

    copy_w = pltpu.make_async_copy(w_hbm, w_ref, sems.at[2 * steps + 1])
    copy_q = pltpu.make_async_copy(q_hbm.at[0], q_ref, sems.at[0])
    copy_pos = pltpu.make_async_copy(pos_hbm, pos_ref, sems.at[2 * steps + 2])
    copy_table = pltpu.make_async_copy(table_hbm, table_ref, sems.at[2 * steps + 3])
    copy_h = pltpu.make_async_copy(h_hbm, h_ref, sems.at[2 * steps + 4])
    copy_q.start()
    copy_pos.start()
    for j in range(copies):
        copy_k(j).start()
    copy_table.start()
    copy_h.start()
    for j in range(copies):
        copy_v(j).start()
    copy_w.start()

    copy_pos.wait()
    positions = jnp.broadcast_to(pos_ref[...].astype(F32), (ROT, tok)).T
    ahead = positions.astype(jnp.int32) - lax.broadcasted_iota(jnp.int32, (tok, ROT), 1)

    copy_q.wait()
    queries = q_ref[...]
    peak = jnp.full((tok, ROT), -jnp.inf, F32)
    for j in range(steps):
        if j % per_copy == 0:
            copy_k(j // per_copy).wait()
        scores = lax.dot_general(
            queries, k_ref[j * chunk : (j + 1) * chunk], (((1,), (1,)), ((), ())),
            preferred_element_type=F32,
        )
        for i in range(chunk // ROT):
            base = j * chunk + i * ROT
            part = jnp.where(ahead >= base, scores[:, i * ROT : (i + 1) * ROT], -jnp.inf)
            s_ref[:, base : base + ROT] = part
            peak = jnp.maximum(peak, part)
    copy_table.wait()
    table = table_ref[...].astype(F32)
    count = table.shape[1]
    for i in range(2):
        rows_ref[i] = jnp.broadcast_to(table[i : i + 1], (ROT, count)).T
    largest = jnp.max(peak, axis=1, keepdims=True)
    factor = math.log2(math.e) / math.sqrt(HD)
    total = jnp.zeros((tok, ROT), F32)
    acc = jnp.zeros((tok, HD), F32)
    for j in range(copies):
        copy_v(j).wait()
    for j in range(steps):
        pieces = []
        for i in range(chunk // ROT):
            base = j * chunk + i * ROT
            raised = jnp.exp2((s_ref[:, base : base + ROT] - largest) * factor)
            total = total + raised
            pieces.append(raised.astype(BF16))
        acc = acc + jnp.dot(
            jnp.concatenate(pieces, axis=1), v_ref[j * chunk : (j + 1) * chunk],
            preferred_element_type=F32,
        )
    context = (acc / jnp.sum(total, axis=1, keepdims=True)).astype(BF16)
    ctx_ref[...] = context

    per = cols // ROT
    copy_h.wait()
    copy_w.wait()
    for shift in range(1, inner):
        first = shard_of(shift) * per
        start = pl.multiple_of(shard_of(shift) * cols, 128)

        def scale_row(i):
            return (65536.0 / math.sqrt(ROT)) / rows_ref[0, pl.ds(first + i, 1), :]

        def store(i, value):
            send_ref[shift - 1, :, i * ROT : (i + 1) * ROT] = value

        gridded(context, h_ref, w_ref[:, pl.ds(start, cols)], scale_row, store)


def attend(inner, cols, queries, keys, values, weight, positions, table, had):
    tok, slots = queries.shape[1], keys.shape[1]
    chunk = min(1024, slots)
    steps = slots // chunk
    blocks = table.shape[1]
    arrays = [queries, keys, values, weight, positions[None, :], table, had]
    return kernel_call(
        functools.partial(attend_kernel, inner, cols, chunk),
        [
            pltpu.VMEM((tok, HD), BF16),
            pltpu.VMEM((2, blocks, ROT), F32),
            pltpu.VMEM((inner - 1, tok, cols), BF16),
            pltpu.VMEM(weight.shape, BF16),
            pltpu.VMEM(had.shape, BF16),
        ],
        [pltpu.with_memory_space_constraint(array, pltpu.HBM) for array in arrays],
        [pl.BlockSpec(memory_space=pltpu.HBM)] * len(arrays),
        scratch=[
            pltpu.VMEM((slots, HD), BF16),
            pltpu.VMEM((slots, HD), BF16),
            pltpu.VMEM((tok, slots), F32),
            pltpu.VMEM((tok, HD), BF16),
            pltpu.VMEM((1, tok), positions.dtype),
            pltpu.VMEM(table.shape, table.dtype),
            pltpu.SemaphoreType.DMA((2 * steps + 5,)),
        ],
        limit=28,
        name="attend",
    )


def partial_kernel(inner, work, ctx_ref, w_ref, rows_ref, h_ref, *out_refs):
    cols = out_refs[0].shape[2]
    per = cols // ROT
    outer, mid, core = place(inner)
    dests = targets(outer)
    context = ctx_ref[...]
    for out_ref, (mine, blocks) in zip(out_refs, work):
        for at, (phase, shift) in enumerate(blocks):
            shard = (dests[phase] * inner + lax.rem(mid + shift, inner)) * 2
            shard = shard + (core if mine else 1 - core)

            def scale_row(i):
                return (65536.0 / math.sqrt(ROT)) / rows_ref[0, pl.ds(shard * per + i, 1), :]

            def store(i, value):
                out_ref[at, :, i * ROT : (i + 1) * ROT] = value

            start = pl.multiple_of(shard * cols, 128)
            gridded(context, h_ref, w_ref[:, pl.ds(start, cols)], scale_row, store)


def partials(inner, cols, work, context, weight, rows, had, after=()):
    tok = context.shape[0]
    count = sum(len(blocks) for _, blocks in work)
    return kernel_call(
        functools.partial(partial_kernel, inner, work),
        [jax.ShapeDtypeStruct((len(blocks), tok, cols), BF16) for _, blocks in work],
        [context, weight, rows, had],
        [vmem()] * 4,
        after=after,
        name="partials",
    )


UPPER, LOWER = 0, 1


def add_kernel(inner, inputs, outputs, *refs):
    ins, outs = refs[:inputs], refs[inputs:]
    outer = place(inner)[0]
    rows = ins[0].shape[-2] // 2
    for out_ref, (items, which_half) in zip(outs, outputs):
        for half in (UPPER, LOWER) if which_half is None else (which_half,):
            part = slice(half * rows, (half + 1) * rows)
            total = None
            for which, at, inner_only, item_half in items:
                if item_half is not None and item_half != half:
                    continue
                ref = ins[which] if at is None else ins[which].at[at]
                value = (ref[part] if item_half is None else ref[...]).astype(F32)
                if inner_only:
                    value = jnp.where(is_inner(outer), value, 0.0)
                total = value if total is None else total + value
            if which_half is None:
                out_ref[part] = total.astype(BF16)
            else:
                out_ref[...] = total.astype(BF16)


def add_up(inner, arrays, outputs, after=()):
    rows, cols = arrays[0].shape[-2:]
    shapes = [
        jax.ShapeDtypeStruct((rows if half is None else rows // 2, cols), BF16) for _, half in outputs
    ]
    return kernel_call(
        functools.partial(add_kernel, inner, len(arrays), outputs),
        shapes,
        arrays,
        [vmem()] * len(arrays),
        after=after,
        name="add_up",
    )


def turn_residual_kernel(inner, res_ref, rows_ref, h_ref, out_ref, factor_ref):
    per = res_ref.shape[1] // ROT
    first = lax.axis_index("tp") * per
    for i in range(per):
        part = slice(i * ROT, (i + 1) * ROT)
        high = 256.0 / rows_ref[1, pl.ds(first + i, 1), :]
        low = rows_ref[0, pl.ds(first + i, 1), :] * (1.0 / 65536.0)
        turned = jnp.dot(res_ref[:, part], h_ref[...], preferred_element_type=F32)
        out_ref[:, part] = turned * (high * (1.0 / math.sqrt(ROT)))
        factor_ref[0:1, part] = low * high
        factor_ref[1:2, part] = low


def turn_residual(inner, residual, rows, had, after=()):
    return kernel_call(
        functools.partial(turn_residual_kernel, inner),
        [
            jax.ShapeDtypeStruct(residual.shape, F32),
            jax.ShapeDtypeStruct((2, residual.shape[1]), F32),
        ],
        [residual, rows, had],
        [vmem()] * 3,
        after=after,
        name="turn_residual",
    )


def summed_at(inner, items, ins, part):
    outer = place(inner)[0]
    total = None
    for (at, inner_only), ref in zip(items, ins):
        value = (ref[:, part] if at is None else ref[at, :, part]).astype(F32)
        if inner_only:
            value = jnp.where(is_inner(outer), value, 0.0)
        total = value if total is None else total + value
    return total


def regrid_kernel(inner, items, *refs):
    *ins, turned_ref, factor_ref, grid_ref = refs
    for i in range(turned_ref.shape[1] // ROT):
        part = slice(i * ROT, (i + 1) * ROT)
        value = turned_ref[:, part] + summed_at(inner, items, ins, part) * factor_ref[0:1, part]
        grid_ref[:, part] = jnp.clip(value, -127.0, 127.0).astype(BF16)


def regrid(inner, items, turned, factors, arrays, after=()):
    return kernel_call(
        functools.partial(regrid_kernel, inner, items),
        jax.ShapeDtypeStruct(turned.shape, BF16),
        [*arrays, turned, factors],
        [vmem()] * (2 + len(arrays)),
        after=after,
        name="regrid",
    )


def hidden_kernel(inner, items, res_ref, factor_ref, h_ref, *refs):
    *ins, out_ref, mark_ref = refs
    mark_ref[...] = jnp.zeros_like(mark_ref)
    for i in range(res_ref.shape[1] // ROT):
        part = slice(i * ROT, (i + 1) * ROT)
        value = summed_at(inner, items, ins, part) * factor_ref[1:2, part]
        upper = value.astype(BF16)
        lower = (value - upper.astype(F32)).astype(BF16)
        turned = jnp.dot(upper, h_ref[...], preferred_element_type=F32)
        turned = turned + jnp.dot(lower, h_ref[...], preferred_element_type=F32)
        stream = res_ref[:, part].astype(F32) + turned * (1.0 / math.sqrt(ROT))
        out_ref[:, part] = stream.astype(BF16)


def hidden(inner, items, residual, factors, had, arrays, after=()):
    return kernel_call(
        functools.partial(hidden_kernel, inner, items),
        [jax.ShapeDtypeStruct(residual.shape, BF16), jax.ShapeDtypeStruct((8, ROT), F32)],
        [residual, factors, had, *arrays],
        [vmem()] * (3 + len(arrays)),
        after=after,
        name="hidden",
    )


def choose_kernel(inner, count, inner_ref, end_ref, *refs):
    inside = is_inner(place(inner)[0])
    others, out_ref, outs = refs[:count], refs[count], refs[count + 1 :]
    lower, upper = outs[:count], outs[count:]

    def put(ref):
        out_ref[...] = ref[...]
        for half in upper:
            half[...] = ref[: half.shape[0]]

    @pl.when(inside)
    def _():
        put(inner_ref)

    @pl.when(jnp.logical_not(inside))
    def _():
        put(end_ref)

    for ref, half in zip(others, lower):
        half[...] = ref[half.shape[0] :]


def choose(inner, at_inner, at_end, others=(), halved=False, after=()):
    rows, cols = at_inner.shape
    half = jax.ShapeDtypeStruct((rows // 2, cols), BF16)
    return kernel_call(
        functools.partial(choose_kernel, inner, len(others)),
        [jax.ShapeDtypeStruct((rows, cols), BF16)] + [half] * (len(others) + halved),
        [at_inner, at_end, *others],
        [vmem()] * (2 + len(others)),
        after=after,
        name="choose",
    )


def gate_kernel(count, *refs):
    for ref, half in zip(refs[:count], refs[-count:]):
        half[...] = ref[half.shape[0] :]


def gate(arrays, others, after):
    rows, cols = arrays[0].shape
    shapes = [jax.ShapeDtypeStruct((rows, cols), BF16)] * len(arrays)
    half = jax.ShapeDtypeStruct((rows // 2, cols), BF16)
    aliases = {len(after) + len(others) + i: i for i in range(len(arrays))}
    return kernel_call(
        functools.partial(gate_kernel, len(others)),
        shapes + [half] * len(others),
        [*others, *arrays],
        [vmem()] * (len(others) + len(arrays)),
        after=after,
        aliases=aliases,
        name="gate",
    )


def select_rows_kernel(inner, cols, w_ref, *out_refs):
    other = 1 - place(inner)[2]
    each = out_refs[0].shape[0]
    for j in range(each * len(out_refs)):
        start = pl.multiple_of((2 * j + other) * cols, 128)
        out_refs[j // each][j % each] = w_ref[pl.ds(start, cols), :]


def select_rows(inner, weight, cols, after=()):
    parts = 2
    each = OUTER * inner // parts
    return kernel_call(
        functools.partial(select_rows_kernel, inner, cols),
        [jax.ShapeDtypeStruct((each, cols, weight.shape[1]), weight.dtype)] * parts,
        [weight],
        [vmem()],
        after=after,
        name="select_rows",
    )


def turn_next_kernel(inner, cols, own_ref, gain_ref, rows_ref, h_ref, *refs):
    *other_refs, out_ref = refs
    each = other_refs[0].shape[0]
    core = place(inner)[2]
    for j in range(out_ref.shape[0]):
        shard = j * 2 + core
        for i in range(cols // ROT):
            block = shard * (cols // ROT) + i
            factor = rows_ref[1, pl.ds(block, 1), :] * (1.0 / (256.0 * math.sqrt(ROT)))
            rotation = (h_ref[...].astype(F32) * gain_ref[pl.ds(block, 1), :]).astype(BF16)
            part = slice(i * ROT, (i + 1) * ROT)
            own = own_ref[pl.ds(pl.multiple_of(block * ROT, ROT), ROT), :]
            for half, value in enumerate((own, other_refs[j // each][j % each, part, :])):
                turned = jnp.dot(rotation, value, preferred_element_type=F32)
                out_ref[j, part, half * HD : (half + 1) * HD] = (turned * factor).astype(BF16)


def turn_next(inner, weight, others, gain, rows, had, after=()):
    _, cols, width = others[0].shape
    return kernel_call(
        functools.partial(turn_next_kernel, inner, cols),
        jax.ShapeDtypeStruct((OUTER * inner, cols, 2 * width), BF16),
        [weight, gain, rows, had, *others],
        [vmem()] * (4 + len(others)),
        after=after,
        name="turn_next",
    )


def project_kernel(inner, places, has_acc, split, w_ref, rows_ref, *refs):
    outer, mid, core = place(inner)
    order = targets(outer)[::-1]
    acc_in = refs[0] if has_acc else None
    refs = refs[1:] if has_acc else refs
    count = sum(parts for _, _, parts in places)
    values_in = list(refs[:count])
    outs = refs[count:]
    cols, width = w_ref.shape[1:]
    acc = acc_in[:, :width] if has_acc else 0.0
    squares = acc_in[:, width:] if has_acc else 0.0
    for phase, shift, parts in places:
        block = order[phase] * inner + lax.rem(mid + inner - shift, inner)
        values = values_in.pop(0)[...]
        if parts == 3:
            at_inner, at_end = values_in.pop(0)[...], values_in.pop(0)[...]
            lower = jnp.where(is_inner(outer), at_inner, at_end)
            values = jnp.concatenate([values, lower], axis=0)
        acc = acc + jnp.dot(values, w_ref[block], preferred_element_type=F32)
        for i in range(cols // ROT):
            row = (block * 2 + core) * (cols // ROT) + i
            high = rows_ref[1, pl.ds(row, 1), :] * (1.0 / 256.0)
            value = values[:, i * ROT : (i + 1) * ROT].astype(F32) * high
            squares = squares + value * value
    if split:
        own_ref, other_ref = outs
        own_ref[:, :HD] = acc[:, :HD]
        own_ref[:, HD:] = squares
        other_ref[:, :HD] = acc[:, HD:]
        other_ref[:, HD:] = squares
    else:
        outs[0][:, :width] = acc
        outs[0][:, width:] = squares


def project(inner, weight, rows, acc, pieces, split=False, after=()):
    _, cols, width = weight.shape
    arrays = [part for _, _, parts in pieces for part in parts]
    first = pieces[0][2]
    tok = first[0].shape[0] * (1 if len(first) == 1 else 2)
    places = tuple((phase, shift, len(parts)) for phase, shift, parts in pieces)
    accs = [] if acc is None else [acc]
    if split:
        out = [jax.ShapeDtypeStruct((tok, HD + ROT), F32)] * 2
    else:
        out = jax.ShapeDtypeStruct((tok, width + ROT), F32)
    return kernel_call(
        functools.partial(project_kernel, inner, places, acc is not None, split),
        out,
        [weight, rows, *accs, *arrays],
        [vmem()] * (2 + len(accs) + len(arrays)),
        after=after,
        name="project",
    )


def finish_kernel(features, own_ref, other_ref, out_ref):
    squares = own_ref[:, HD:] + other_ref[:, HD:]
    mean = jnp.sum(squares, axis=1, keepdims=True) * (1.0 / features)
    value = (own_ref[:, :HD] + other_ref[:, :HD]) * lax.rsqrt(mean + 1e-05)
    out_ref[...] = value.astype(BF16)


def finish(own, other, features):
    tok = own.shape[0]
    return kernel_call(
        functools.partial(finish_kernel, features),
        jax.ShapeDtypeStruct((tok, HD), BF16),
        [own, other],
        [vmem()] * 2,
        name="finish",
    )


def body(
    size,
    queries,
    cache_keys,
    cache_values,
    query_positions,
    out_weight,
    residual,
    scale_table,
    norm_gain,
    next_query_weight,
):
    inner = size // (2 * OUTER)
    cols = residual.shape[1]
    had = jnp.asarray(hadamard(ROT), BF16)
    shifts = range(1, inner)

    def permute(value, move):
        moves = []
        for i in range(size):
            spot = move(i // (2 * inner), (i // 2) % inner, i % 2)
            moves.append((i, (spot[0] * inner + spot[1]) * 2 + spot[2]))
        return lax.ppermute(value, "tp", moves)

    def swap_core(value):
        return permute(value, lambda a, b, c: (a, b, 1 - c))

    def shift_mid(value, shift):
        return permute(value, lambda a, b, c: (a, (b + shift) % inner, c))

    def swap_pairs(value):
        return permute(value, lambda a, b, c: (a ^ 1, b, c))

    def swap_middle(value):
        return permute(value, lambda a, b, c: (a, b, 1 - c) if a in (0, 3) else (3 - a, b, c))

    everything = range(inner)
    context, rows, send1, out_weight, had = attend(
        inner, cols, queries, cache_keys, cache_values, out_weight, query_positions, scale_table, had
    )
    other1 = swap_core(send1)
    away1 = tuple((0, s) for s in shifts)
    def phase_blocks(phase):
        return tuple((phase, s) for s in everything)

    def grid_blocks(work, after=()):
        return partials(inner, cols, work, context, out_weight, rows, had, after=after)

    blocks2 = ((0, 0),) + tuple((1, s) for s in shifts)
    keep1, keep2, *send2 = grid_blocks(
        ((True, away1), (True, blocks2), *((False, (block,)) for block in blocks2))
    )
    other2 = [swap_core(send) for send in send2]
    items1 = [[(0, s - 1, False, None), (1, s - 1, False, None)] for s in shifts]
    first = add_up(
        inner,
        [keep1, other1],
        [(items, UPPER) for items in items1] + [(items, LOWER) for items in items1],
        after=[keep2],
    )
    pay1, low1 = first[: len(shifts)], first[len(shifts) :]
    come1 = [shift_mid(pay, s) for s, pay in zip(shifts, pay1)]
    low_pairs = [swap_pairs(low) for low in low1]
    low_middle = [swap_middle(low) for low in low1]
    near_block = ((1, 0),)
    send2n, send3 = grid_blocks(((False, near_block), (False, phase_blocks(2))), pay1[:1])
    other2n, other3 = swap_core(send2n), swap_core(send3)
    send4, keep2n, keep3, keep4 = grid_blocks(
        (
            (False, phase_blocks(3)),
            (True, near_block),
            (True, phase_blocks(2)),
            (True, phase_blocks(3)),
        ),
        [send3],
    )
    other4 = swap_core(send4)

    def sums(arrays, outputs, after=()):
        names = list(arrays)
        items = [
            ([(names.index(name), *rest) for name, *rest in output], None) for output in outputs
        ]
        return add_up(inner, list(arrays.values()), items, after=after)

    def named(name, blocks):
        return {f"{name}_{s}": block for s, block in zip(shifts, blocks)}

    def added(names, half=None):
        return [(name, None, False, half) for name in names]

    own2 = {"keep2": keep2} | {f"other2_{i}": other for i, other in enumerate(other2)}
    own2n = {"keep2n": keep2n, "other2n": other2n}
    own3 = {"keep3": keep3, "other3": other3}
    own4 = {"keep4": keep4, "other4": other4}

    def part2(i):
        return [("keep2", i, False, None), (f"other2_{i}", 0, False, None)]

    def part(step, s):
        return [(f"keep{step}", s, False, None), (f"other{step}", s, False, None)]

    def passed(name, s):
        return [(f"{name}_{s}", None, True, LOWER)]

    def relayed(name):
        return [(name, None, True, None)]

    came1, from_pairs = named("came1", come1), named("pairs", low_pairs)
    from_middle = named("middle", low_middle)
    near1 = part2(0) + added(came1, UPPER)
    *pay2, end1 = sums(
        own2 | came1 | from_pairs,
        [*(part2(s) + passed("pairs", s) for s in shifts), near1],
        after=[*come1, send4],
    )
    came2 = named("came2", [shift_mid(pay, s) for s, pay in zip(shifts, pay2)])
    from_end1 = {"end1": swap_pairs(end1)}
    turned_residual, factors = turn_residual(inner, residual, rows, had, after=[end1])
    picked = select_rows(inner, next_query_weight, cols, after=[factors])
    next_other = [swap_core(part) for part in picked]

    near2 = part("2n", 0) + added(came2)
    *pay3, sum2 = sums(
        came2 | from_end1 | own2n | own3,
        [*(part(3, s) for s in shifts), near2 + relayed("end1")],
        after=picked[:1],
    )
    came3 = named("came3", [shift_mid(pay, s) for s, pay in zip(shifts, pay3)])
    from_end2 = {"end2": swap_pairs(sum2)}
    from_mid2 = {"mid2": swap_middle(sum2)}

    *pay4, near3, mid3 = sums(
        came3 | from_end2 | from_mid2 | own2 | own3 | own4 | came1 | from_middle,
        [
            *(part(4, s) + passed("middle", s) for s in shifts),
            part(3, 0) + added(came3) + relayed("mid2"),
            near1 + relayed("end2"),
        ],
    )
    come4 = [shift_mid(pay, s) for s, pay in zip(shifts, pay4)]
    from_mid3 = swap_middle(mid3)
    from_near3 = swap_pairs(near3)

    gain = norm_gain.astype(F32).reshape(-1, ROT)

    last = [*come4, from_near3, from_mid3, keep4, other4]
    items = [(None, False)] * (len(come4) + 1) + [(None, True)] + [(0, False)] * 2
    grid = regrid(inner, items, turned_residual, factors, last)

    x1 = [shift_mid(grid, s) for s in shifts]
    near = swap_pairs(grid)
    mid1 = swap_middle(grid)
    hidden_out, mark = hidden(inner, items, residual, factors, had, last, after=[grid])
    near, *low1 = gate([near], x1, after=[mark])
    x2 = [shift_mid(near, s) for s in shifts]
    ends2 = swap_pairs(mid1)
    mids2 = swap_middle(near)
    (third,) = choose(inner, mids2, ends2, after=x2)
    x3 = [shift_mid(third, s) for s in shifts]
    ends3 = swap_pairs(mids2)
    side_middle = [swap_middle(low) for low in low1]
    turned_next = turn_next(inner, next_query_weight, next_other, gain, rows, had, after=[third])
    fourth, *low3, up4 = choose(inner, mid1, ends3, x3, True, after=[turned_next])
    x4 = [shift_mid(up4, s) for s in shifts]
    side_pairs = [swap_pairs(low) for low in low3]
    acc = project(
        inner,
        turned_next,
        rows,
        None,
        [(0, 0, [grid]), (1, 0, [near]), (2, 0, [third]), (3, 0, [fourth])]
        + [(phase, s, [x[s - 1]]) for phase, x in enumerate((x1, x2, x3)) for s in shifts],
    )
    own, other = project(
        inner,
        turned_next,
        rows,
        acc,
        [(3, s, [x4[s - 1], side_middle[s - 1], side_pairs[s - 1]]) for s in shifts],
        split=True,
    )
    query_next = finish(own, swap_core(other), norm_gain.shape[0])
    return (hidden_out, query_next)


def solution(mesh):
    placed = (
        P("tp", "groups", None),
        P("tp", "groups", None),
        P("tp", "groups", None),
        P("groups"),
        P("tp", None),
        P("groups", "tp"),
        P(),
        P(),
        P(None, "tp"),
    )
    return jax.shard_map(
        functools.partial(body, mesh.shape["tp"]),
        mesh=mesh,
        in_specs=placed,
        out_specs=(P("groups", "tp"), P("groups", "tp")),
        check_vma=False,
    )
```

```python
import functools
import math

import jax
import jax.numpy as jnp
import numpy as np
from jax import lax
from jax.experimental import pallas as pl
from jax.experimental.pallas import tpu as pltpu
from jax.sharding import PartitionSpec as P

HD = 128
ROT = 128
OUTER = 4

F32 = jnp.float32
BF16 = jnp.bfloat16
MIB = 1024 * 1024


def hadamard(length):
    rows = np.arange(length)
    common = rows[:, None] & rows[None, :]
    parity = np.zeros((length, length), np.int64)
    for bit in range(length.bit_length()):
        parity += (common >> bit) & 1
    return (1 - 2 * (parity & 1)).astype(np.float32)


def vmem():
    return pl.BlockSpec(memory_space=pltpu.VMEM)


def anywhere():
    return pl.BlockSpec(memory_space=pl.ANY)


def place(inner):
    index = lax.axis_index("tp")
    return lax.div(index, 2 * inner), lax.rem(lax.div(index, 2), inner), lax.rem(index, 2)


def targets(outer):
    near = outer + 1 - 2 * lax.rem(outer, 2)
    return OUTER - 1 - outer, lax.rem(outer + 2, OUTER), near, outer


def is_inner(outer):
    return jnp.logical_or(outer == 1, outer == 2)


def kernel_call(kernel, out_shape, arrays, specs, after=(), scratch=(), aliases=None, limit=24, name=None):
    extra = len(after)

    def ordered(*refs):
        kernel(*refs[extra:])

    return pl.pallas_call(
        ordered,
        out_shape=out_shape,
        in_specs=[anywhere()] * extra + list(specs),
        out_specs=jax.tree.map(lambda _: vmem(), out_shape),
        scratch_shapes=list(scratch),
        input_output_aliases=aliases or {},
        cost_estimate=pl.CostEstimate(flops=0, bytes_accessed=0, transcendentals=0),
        compiler_params=pltpu.CompilerParams(vmem_limit_bytes=limit * MIB),
        name=name,
    )(*after, *arrays)


def gridded(context, h_ref, weight, scale_row, store):
    cols = weight.shape[1]
    count = cols // ROT
    value = jnp.dot(context, weight, preferred_element_type=F32).astype(BF16)
    stacked = jnp.concatenate([value[:, i * ROT : (i + 1) * ROT] for i in range(count)], axis=0)
    turned = jnp.dot(stacked, h_ref[...], preferred_element_type=F32)
    tok = value.shape[0]
    for i in range(count):
        part = turned[i * tok : (i + 1) * tok] * scale_row(i)
        store(i, jnp.clip(part, -127.0, 127.0).astype(BF16))


def attend_kernel(
    inner, cols, chunk, q_hbm, k_hbm, v_hbm, w_hbm, pos_hbm, table_hbm, h_hbm,
    ctx_ref, rows_ref, send_ref, w_ref, h_ref, k_ref, v_ref, s_ref, q_ref, pos_ref, table_ref, sems,
):
    tok = q_ref.shape[0]
    slots = k_ref.shape[0]
    steps = slots // chunk
    outer, mid, core = place(inner)
    dest = targets(outer)[0]

    copies = min(4, steps)
    per_copy = steps // copies
    size = slots // copies

    def copy_k(j):
        part = pl.ds(j * size, size)
        return pltpu.make_async_copy(k_hbm.at[0, part], k_ref.at[part], sems.at[1 + j])

    def copy_v(j):
        part = pl.ds(j * size, size)
        return pltpu.make_async_copy(v_hbm.at[0, part], v_ref.at[part], sems.at[1 + steps + j])

    def shard_of(shift):
        return (dest * inner + lax.rem(mid + shift, inner)) * 2 + 1 - core

    copy_w = pltpu.make_async_copy(w_hbm, w_ref, sems.at[2 * steps + 1])
    copy_q = pltpu.make_async_copy(q_hbm.at[0], q_ref, sems.at[0])
    copy_pos = pltpu.make_async_copy(pos_hbm, pos_ref, sems.at[2 * steps + 2])
    copy_table = pltpu.make_async_copy(table_hbm, table_ref, sems.at[2 * steps + 3])
    copy_h = pltpu.make_async_copy(h_hbm, h_ref, sems.at[2 * steps + 4])
    copy_q.start()
    copy_pos.start()
    for j in range(copies):
        copy_k(j).start()
    copy_table.start()
    copy_h.start()
    for j in range(copies):
        copy_v(j).start()
    copy_w.start()

    copy_pos.wait()
    positions = jnp.broadcast_to(pos_ref[...].astype(F32), (ROT, tok)).T
    ahead = positions.astype(jnp.int32) - lax.broadcasted_iota(jnp.int32, (tok, ROT), 1)

    copy_q.wait()
    queries = q_ref[...]
    peak = jnp.full((tok, ROT), -jnp.inf, F32)
    for j in range(steps):
        if j % per_copy == 0:
            copy_k(j // per_copy).wait()
        scores = lax.dot_general(
            queries, k_ref[j * chunk : (j + 1) * chunk], (((1,), (1,)), ((), ())),
            preferred_element_type=F32,
        )
        for i in range(chunk // ROT):
            base = j * chunk + i * ROT
            part = jnp.where(ahead >= base, scores[:, i * ROT : (i + 1) * ROT], -jnp.inf)
            s_ref[:, base : base + ROT] = part
            peak = jnp.maximum(peak, part)
    copy_table.wait()
    table = table_ref[...].astype(F32)
    count = table.shape[1]
    for i in range(2):
        rows_ref[i] = jnp.broadcast_to(table[i : i + 1], (ROT, count)).T
    largest = jnp.max(peak, axis=1, keepdims=True)
    factor = math.log2(math.e) / math.sqrt(HD)
    total = jnp.zeros((tok, ROT), F32)
    acc = jnp.zeros((tok, HD), F32)
    for j in range(copies):
        copy_v(j).wait()
    for j in range(steps):
        pieces = []
        for i in range(chunk // ROT):
            base = j * chunk + i * ROT
            raised = jnp.exp2((s_ref[:, base : base + ROT] - largest) * factor)
            total = total + raised
            pieces.append(raised.astype(BF16))
        acc = acc + jnp.dot(
            jnp.concatenate(pieces, axis=1), v_ref[j * chunk : (j + 1) * chunk],
            preferred_element_type=F32,
        )
    context = (acc / jnp.sum(total, axis=1, keepdims=True)).astype(BF16)
    ctx_ref[...] = context

    per = cols // ROT
    copy_h.wait()
    copy_w.wait()
    for shift in range(1, inner):
        first = shard_of(shift) * per
        start = pl.multiple_of(shard_of(shift) * cols, 128)

        def scale_row(i):
            return (65536.0 / math.sqrt(ROT)) / rows_ref[0, pl.ds(first + i, 1), :]

        def store(i, value):
            send_ref[shift - 1, :, i * ROT : (i + 1) * ROT] = value

        gridded(context, h_ref, w_ref[:, pl.ds(start, cols)], scale_row, store)


def attend(inner, cols, queries, keys, values, weight, positions, table, had):
    tok, slots = queries.shape[1], keys.shape[1]
    chunk = min(1024, slots)
    steps = slots // chunk
    blocks = table.shape[1]
    arrays = [queries, keys, values, weight, positions[None, :], table, had]
    return kernel_call(
        functools.partial(attend_kernel, inner, cols, chunk),
        [
            pltpu.VMEM((tok, HD), BF16),
            pltpu.VMEM((2, blocks, ROT), F32),
            pltpu.VMEM((inner - 1, tok, cols), BF16),
            pltpu.VMEM(weight.shape, BF16),
            pltpu.VMEM(had.shape, BF16),
        ],
        [pltpu.with_memory_space_constraint(array, pltpu.HBM) for array in arrays],
        [pl.BlockSpec(memory_space=pltpu.HBM)] * len(arrays),
        scratch=[
            pltpu.VMEM((slots, HD), BF16),
            pltpu.VMEM((slots, HD), BF16),
            pltpu.VMEM((tok, slots), F32),
            pltpu.VMEM((tok, HD), BF16),
            pltpu.VMEM((1, tok), positions.dtype),
            pltpu.VMEM(table.shape, table.dtype),
            pltpu.SemaphoreType.DMA((2 * steps + 5,)),
        ],
        limit=28,
        name="attend",
    )


def partial_kernel(inner, work, ctx_ref, w_ref, rows_ref, h_ref, *out_refs):
    cols = out_refs[0].shape[2]
    per = cols // ROT
    outer, mid, core = place(inner)
    dests = targets(outer)
    context = ctx_ref[...]
    for out_ref, (mine, blocks) in zip(out_refs, work):
        for at, (phase, shift) in enumerate(blocks):
            shard = (dests[phase] * inner + lax.rem(mid + shift, inner)) * 2
            shard = shard + (core if mine else 1 - core)

            def scale_row(i):
                return (65536.0 / math.sqrt(ROT)) / rows_ref[0, pl.ds(shard * per + i, 1), :]

            def store(i, value):
                out_ref[at, :, i * ROT : (i + 1) * ROT] = value

            start = pl.multiple_of(shard * cols, 128)
            gridded(context, h_ref, w_ref[:, pl.ds(start, cols)], scale_row, store)


def partials(inner, cols, work, context, weight, rows, had, after=()):
    tok = context.shape[0]
    count = sum(len(blocks) for _, blocks in work)
    return kernel_call(
        functools.partial(partial_kernel, inner, work),
        [jax.ShapeDtypeStruct((len(blocks), tok, cols), BF16) for _, blocks in work],
        [context, weight, rows, had],
        [vmem()] * 4,
        after=after,
        name="partials",
    )


UPPER, LOWER = 0, 1


def add_kernel(inner, inputs, outputs, *refs):
    ins, outs = refs[:inputs], refs[inputs:]
    outer = place(inner)[0]
    rows = ins[0].shape[-2] // 2
    for out_ref, (items, which_half) in zip(outs, outputs):
        for half in (UPPER, LOWER) if which_half is None else (which_half,):
            part = slice(half * rows, (half + 1) * rows)
            total = None
            for which, at, inner_only, item_half in items:
                if item_half is not None and item_half != half:
                    continue
                ref = ins[which] if at is None else ins[which].at[at]
                value = (ref[part] if item_half is None else ref[...]).astype(F32)
                if inner_only:
                    value = jnp.where(is_inner(outer), value, 0.0)
                total = value if total is None else total + value
            if which_half is None:
                out_ref[part] = total.astype(BF16)
            else:
                out_ref[...] = total.astype(BF16)


def add_up(inner, arrays, outputs, after=()):
    rows, cols = arrays[0].shape[-2:]
    shapes = [
        jax.ShapeDtypeStruct((rows if half is None else rows // 2, cols), BF16) for _, half in outputs
    ]
    return kernel_call(
        functools.partial(add_kernel, inner, len(arrays), outputs),
        shapes,
        arrays,
        [vmem()] * len(arrays),
        after=after,
        name="add_up",
    )


def turn_residual_kernel(inner, res_ref, rows_ref, h_ref, out_ref, factor_ref):
    per = res_ref.shape[1] // ROT
    first = lax.axis_index("tp") * per
    for i in range(per):
        part = slice(i * ROT, (i + 1) * ROT)
        high = 256.0 / rows_ref[1, pl.ds(first + i, 1), :]
        low = rows_ref[0, pl.ds(first + i, 1), :] * (1.0 / 65536.0)
        turned = jnp.dot(res_ref[:, part], h_ref[...], preferred_element_type=F32)
        out_ref[:, part] = turned * (high * (1.0 / math.sqrt(ROT)))
        factor_ref[0:1, part] = low * high
        factor_ref[1:2, part] = low


def turn_residual(inner, residual, rows, had, after=()):
    return kernel_call(
        functools.partial(turn_residual_kernel, inner),
        [
            jax.ShapeDtypeStruct(residual.shape, F32),
            jax.ShapeDtypeStruct((2, residual.shape[1]), F32),
        ],
        [residual, rows, had],
        [vmem()] * 3,
        after=after,
        name="turn_residual",
    )


def summed_at(inner, items, ins, part):
    outer = place(inner)[0]
    total = None
    for (at, inner_only), ref in zip(items, ins):
        value = (ref[:, part] if at is None else ref[at, :, part]).astype(F32)
        if inner_only:
            value = jnp.where(is_inner(outer), value, 0.0)
        total = value if total is None else total + value
    return total


def regrid_kernel(inner, items, *refs):
    *ins, turned_ref, factor_ref, grid_ref = refs
    for i in range(turned_ref.shape[1] // ROT):
        part = slice(i * ROT, (i + 1) * ROT)
        value = turned_ref[:, part] + summed_at(inner, items, ins, part) * factor_ref[0:1, part]
        grid_ref[:, part] = jnp.clip(value, -127.0, 127.0).astype(BF16)


def regrid(inner, items, turned, factors, arrays, after=()):
    return kernel_call(
        functools.partial(regrid_kernel, inner, items),
        jax.ShapeDtypeStruct(turned.shape, BF16),
        [*arrays, turned, factors],
        [vmem()] * (2 + len(arrays)),
        after=after,
        name="regrid",
    )


def hidden_kernel(inner, items, res_ref, factor_ref, h_ref, *refs):
    *ins, out_ref, mark_ref = refs
    mark_ref[...] = jnp.zeros_like(mark_ref)
    for i in range(res_ref.shape[1] // ROT):
        part = slice(i * ROT, (i + 1) * ROT)
        value = summed_at(inner, items, ins, part) * factor_ref[1:2, part]
        upper = value.astype(BF16)
        lower = (value - upper.astype(F32)).astype(BF16)
        turned = jnp.dot(upper, h_ref[...], preferred_element_type=F32)
        turned = turned + jnp.dot(lower, h_ref[...], preferred_element_type=F32)
        stream = res_ref[:, part].astype(F32) + turned * (1.0 / math.sqrt(ROT))
        out_ref[:, part] = stream.astype(BF16)


def hidden(inner, items, residual, factors, had, arrays, after=()):
    return kernel_call(
        functools.partial(hidden_kernel, inner, items),
        [jax.ShapeDtypeStruct(residual.shape, BF16), jax.ShapeDtypeStruct((8, ROT), F32)],
        [residual, factors, had, *arrays],
        [vmem()] * (3 + len(arrays)),
        after=after,
        name="hidden",
    )


def choose_kernel(inner, count, *refs):
    inside = is_inner(place(inner)[0])
    others, (inner_ref, end_ref, out_ref, *outs) = refs[:count], refs[count:]
    lower, upper = outs[:count], outs[count:]

    def put(ref):
        out_ref[...] = ref[...]
        for half in upper:
            half[...] = ref[: half.shape[0]]

    @pl.when(inside)
    def _():
        put(inner_ref)

    @pl.when(jnp.logical_not(inside))
    def _():
        put(end_ref)

    for ref, half in zip(others, lower):
        half[...] = ref[half.shape[0] :]


def choose(inner, at_inner, at_end, others=(), halved=False, after=()):
    rows, cols = at_inner.shape
    half = jax.ShapeDtypeStruct((rows // 2, cols), BF16)
    return kernel_call(
        functools.partial(choose_kernel, inner, len(others)),
        [jax.ShapeDtypeStruct((rows, cols), BF16)] + [half] * (len(others) + halved),
        [*others, at_inner, at_end],
        [vmem()] * (2 + len(others)),
        after=after,
        name="choose",
    )


def gate_kernel(count, *refs):
    for ref, half in zip(refs[:count], refs[-count:]):
        half[...] = ref[half.shape[0] :]


def gate(arrays, others, after):
    rows, cols = arrays[0].shape
    shapes = [jax.ShapeDtypeStruct((rows, cols), BF16)] * len(arrays)
    half = jax.ShapeDtypeStruct((rows // 2, cols), BF16)
    aliases = {len(after) + len(others) + i: i for i in range(len(arrays))}
    return kernel_call(
        functools.partial(gate_kernel, len(others)),
        shapes + [half] * len(others),
        [*others, *arrays],
        [vmem()] * (len(others) + len(arrays)),
        after=after,
        aliases=aliases,
        name="gate",
    )


def select_rows_kernel(inner, cols, w_ref, *out_refs):
    other = 1 - place(inner)[2]
    each = out_refs[0].shape[0]
    for j in range(each * len(out_refs)):
        start = pl.multiple_of((2 * j + other) * cols, 128)
        out_refs[j // each][j % each] = w_ref[pl.ds(start, cols), :]


def select_rows(inner, weight, cols, after=()):
    parts = 2
    each = OUTER * inner // parts
    return kernel_call(
        functools.partial(select_rows_kernel, inner, cols),
        [jax.ShapeDtypeStruct((each, cols, weight.shape[1]), weight.dtype)] * parts,
        [weight],
        [vmem()],
        after=after,
        name="select_rows",
    )


def turn_next_kernel(inner, cols, own_ref, gain_ref, rows_ref, h_ref, *refs):
    *other_refs, out_ref = refs
    each = other_refs[0].shape[0]
    core = place(inner)[2]
    for j in range(out_ref.shape[0]):
        shard = j * 2 + core
        for i in range(cols // ROT):
            block = shard * (cols // ROT) + i
            factor = rows_ref[1, pl.ds(block, 1), :] * (1.0 / (256.0 * math.sqrt(ROT)))
            rotation = (h_ref[...].astype(F32) * gain_ref[pl.ds(block, 1), :]).astype(BF16)
            part = slice(i * ROT, (i + 1) * ROT)
            own = own_ref[pl.ds(pl.multiple_of(block * ROT, ROT), ROT), :]
            for half, value in enumerate((own, other_refs[j // each][j % each, part, :])):
                turned = jnp.dot(rotation, value, preferred_element_type=F32)
                out_ref[j, part, half * HD : (half + 1) * HD] = (turned * factor).astype(BF16)


def turn_next(inner, weight, others, gain, rows, had, after=()):
    _, cols, width = others[0].shape
    return kernel_call(
        functools.partial(turn_next_kernel, inner, cols),
        jax.ShapeDtypeStruct((OUTER * inner, cols, 2 * width), BF16),
        [weight, gain, rows, had, *others],
        [vmem()] * (4 + len(others)),
        after=after,
        name="turn_next",
    )


def project_kernel(inner, places, has_acc, split, w_ref, rows_ref, *refs):
    outer, mid, core = place(inner)
    order = targets(outer)[::-1]
    acc_in = refs[0] if has_acc else None
    refs = refs[1:] if has_acc else refs
    count = sum(parts for _, _, parts in places)
    values_in = list(refs[:count])
    outs = refs[count:]
    cols, width = w_ref.shape[1:]
    acc = acc_in[:, :width] if has_acc else 0.0
    squares = acc_in[:, width:] if has_acc else 0.0
    for phase, shift, parts in places:
        block = order[phase] * inner + lax.rem(mid + inner - shift, inner)
        values = values_in.pop(0)[...]
        if parts == 3:
            at_inner, at_end = values_in.pop(0)[...], values_in.pop(0)[...]
            lower = jnp.where(is_inner(outer), at_inner, at_end)
            values = jnp.concatenate([values, lower], axis=0)
        acc = acc + jnp.dot(values, w_ref[block], preferred_element_type=F32)
        for i in range(cols // ROT):
            row = (block * 2 + core) * (cols // ROT) + i
            high = rows_ref[1, pl.ds(row, 1), :] * (1.0 / 256.0)
            value = values[:, i * ROT : (i + 1) * ROT].astype(F32) * high
            squares = squares + value * value
    if split:
        own_ref, other_ref = outs
        own_ref[:, :HD] = acc[:, :HD]
        own_ref[:, HD:] = squares
        other_ref[:, :HD] = acc[:, HD:]
        other_ref[:, HD:] = squares
    else:
        outs[0][:, :width] = acc
        outs[0][:, width:] = squares


def project(inner, weight, rows, acc, pieces, split=False, after=()):
    _, cols, width = weight.shape
    arrays = [part for _, _, parts in pieces for part in parts]
    first = pieces[0][2]
    tok = first[0].shape[0] * (1 if len(first) == 1 else 2)
    places = tuple((phase, shift, len(parts)) for phase, shift, parts in pieces)
    accs = [] if acc is None else [acc]
    if split:
        out = [jax.ShapeDtypeStruct((tok, HD + ROT), F32)] * 2
    else:
        out = jax.ShapeDtypeStruct((tok, width + ROT), F32)
    return kernel_call(
        functools.partial(project_kernel, inner, places, acc is not None, split),
        out,
        [weight, rows, *accs, *arrays],
        [vmem()] * (2 + len(accs) + len(arrays)),
        after=after,
        name="project",
    )


def finish_kernel(features, own_ref, other_ref, out_ref):
    squares = own_ref[:, HD:] + other_ref[:, HD:]
    mean = jnp.sum(squares, axis=1, keepdims=True) * (1.0 / features)
    value = (own_ref[:, :HD] + other_ref[:, :HD]) * lax.rsqrt(mean + 1e-05)
    out_ref[...] = value.astype(BF16)


def finish(own, other, features):
    tok = own.shape[0]
    return kernel_call(
        functools.partial(finish_kernel, features),
        jax.ShapeDtypeStruct((tok, HD), BF16),
        [own, other],
        [vmem()] * 2,
        name="finish",
    )


def body(
    size,
    queries,
    cache_keys,
    cache_values,
    query_positions,
    out_weight,
    residual,
    scale_table,
    norm_gain,
    next_query_weight,
):
    inner = size // (2 * OUTER)
    cols = residual.shape[1]
    had = jnp.asarray(hadamard(ROT), BF16)
    shifts = range(1, inner)

    def permute(value, move):
        moves = []
        for i in range(size):
            spot = move(i // (2 * inner), (i // 2) % inner, i % 2)
            moves.append((i, (spot[0] * inner + spot[1]) * 2 + spot[2]))
        return lax.ppermute(value, "tp", moves)

    def swap_core(value):
        return permute(value, lambda a, b, c: (a, b, 1 - c))

    def shift_mid(value, shift):
        return permute(value, lambda a, b, c: (a, (b + shift) % inner, c))

    def swap_pairs(value):
        return permute(value, lambda a, b, c: (a ^ 1, b, c))

    def swap_middle(value):
        return permute(value, lambda a, b, c: (a, b, 1 - c) if a in (0, 3) else (3 - a, b, c))

    everything = range(inner)
    context, rows, send1, out_weight, had = attend(
        inner, cols, queries, cache_keys, cache_values, out_weight, query_positions, scale_table, had
    )
    other1 = swap_core(send1)
    away1 = tuple((0, s) for s in shifts)
    def phase_blocks(phase):
        return tuple((phase, s) for s in everything)

    def grid_blocks(work, after=()):
        return partials(inner, cols, work, context, out_weight, rows, had, after=after)

    blocks2 = ((0, 0),) + tuple((1, s) for s in shifts)
    keep1, keep2, *send2 = grid_blocks(
        ((True, away1), (True, blocks2), *((False, (block,)) for block in blocks2))
    )
    other2 = [swap_core(send) for send in send2]
    items1 = [[(0, s - 1, False, None), (1, s - 1, False, None)] for s in shifts]
    first = add_up(
        inner,
        [keep1, other1],
        [(items, UPPER) for items in items1] + [(items, LOWER) for items in items1],
        after=[keep2],
    )
    pay1, low1 = first[: len(shifts)], first[len(shifts) :]
    come1 = [shift_mid(pay, s) for s, pay in zip(shifts, pay1)]
    low_pairs = [swap_pairs(low) for low in low1]
    low_middle = [swap_middle(low) for low in low1]
    near_block = ((1, 0),)
    send2n, send3 = grid_blocks(((False, near_block), (False, phase_blocks(2))), pay1[:1])
    other2n, other3 = swap_core(send2n), swap_core(send3)
    send4, keep2n, keep3, keep4 = grid_blocks(
        (
            (False, phase_blocks(3)),
            (True, near_block),
            (True, phase_blocks(2)),
            (True, phase_blocks(3)),
        ),
        [send3],
    )
    other4 = swap_core(send4)

    def sums(arrays, outputs, after=()):
        names = list(arrays)
        items = [
            ([(names.index(name), *rest) for name, *rest in output], None) for output in outputs
        ]
        return add_up(inner, list(arrays.values()), items, after=after)

    def named(name, blocks):
        return {f"{name}_{s}": block for s, block in zip(shifts, blocks)}

    def added(names, half=None):
        return [(name, None, False, half) for name in names]

    own2 = {"keep2": keep2} | {f"other2_{i}": other for i, other in enumerate(other2)}
    own2n = {"keep2n": keep2n, "other2n": other2n}
    own3 = {"keep3": keep3, "other3": other3}
    own4 = {"keep4": keep4, "other4": other4}

    def part2(i):
        return [("keep2", i, False, None), (f"other2_{i}", 0, False, None)]

    def part(step, s):
        return [(f"keep{step}", s, False, None), (f"other{step}", s, False, None)]

    def passed(name, s):
        return [(f"{name}_{s}", None, True, LOWER)]

    def relayed(name):
        return [(name, None, True, None)]

    came1, from_pairs = named("came1", come1), named("pairs", low_pairs)
    from_middle = named("middle", low_middle)
    near1 = part2(0) + added(came1, UPPER)
    *pay2, end1 = sums(
        own2 | came1 | from_pairs,
        [*(part2(s) + passed("pairs", s) for s in shifts), near1],
        after=[*come1, send4],
    )
    came2 = named("came2", [shift_mid(pay, s) for s, pay in zip(shifts, pay2)])
    from_end1 = {"end1": swap_pairs(end1)}
    turned_residual, factors = turn_residual(inner, residual, rows, had, after=[end1])
    picked = select_rows(inner, next_query_weight, cols, after=[factors])
    next_other = [swap_core(part) for part in picked]

    near2 = part("2n", 0) + added(came2)
    *pay3, sum2 = sums(
        came2 | from_end1 | own2n | own3,
        [*(part(3, s) for s in shifts), near2 + relayed("end1")],
        after=[*picked[:1], *low_middle],
    )
    came3 = named("came3", [shift_mid(pay, s) for s, pay in zip(shifts, pay3)])
    from_end2 = {"end2": swap_pairs(sum2)}
    from_mid2 = {"mid2": swap_middle(sum2)}

    *pay4, near3, mid3 = sums(
        came3 | from_end2 | from_mid2 | own2 | own3 | own4 | came1 | from_middle,
        [
            *(part(4, s) + passed("middle", s) for s in shifts),
            part(3, 0) + added(came3) + relayed("mid2"),
            near1 + relayed("end2"),
        ],
    )
    come4 = [shift_mid(pay, s) for s, pay in zip(shifts, pay4)]
    from_mid3 = swap_middle(mid3)
    from_near3 = swap_pairs(near3)

    gain = norm_gain.astype(F32).reshape(-1, ROT)

    last = [*come4, from_near3, from_mid3, keep4, other4]
    items = [(None, False)] * (len(come4) + 1) + [(None, True)] + [(0, False)] * 2
    grid = regrid(inner, items, turned_residual, factors, last)

    x1 = [shift_mid(grid, s) for s in shifts]
    near = swap_pairs(grid)
    mid1 = swap_middle(grid)
    hidden_out, mark = hidden(inner, items, residual, factors, had, last, after=[grid])
    near, *low1 = gate([near], x1, after=[mark])
    x2 = [shift_mid(near, s) for s in shifts]
    ends2 = swap_pairs(mid1)
    mids2 = swap_middle(near)
    (third,) = choose(inner, mids2, ends2, after=x2)
    x3 = [shift_mid(third, s) for s in shifts]
    ends3 = swap_pairs(third)
    side_middle = [swap_middle(low) for low in low1]
    turned_next = turn_next(inner, next_query_weight, next_other, gain, rows, had, after=[third])
    fourth, *low3, up4 = choose(inner, mid1, ends3, x3, True, after=[turned_next])
    x4 = [shift_mid(up4, s) for s in shifts]
    side_pairs = [swap_pairs(low) for low in low3]
    acc = project(
        inner,
        turned_next,
        rows,
        None,
        [(0, 0, [grid]), (1, 0, [near]), (2, 0, [third]), (3, 0, [fourth])]
        + [(phase, s, [x[s - 1]]) for phase, x in enumerate((x1, x2, x3)) for s in shifts],
    )
    own, other = project(
        inner,
        turned_next,
        rows,
        acc,
        [(3, s, [x4[s - 1], side_middle[s - 1], side_pairs[s - 1]]) for s in shifts],
        split=True,
    )
    query_next = finish(own, swap_core(other), norm_gain.shape[0])
    return (hidden_out, query_next)


def solution(mesh):
    placed = (
        P("tp", "groups", None),
        P("tp", "groups", None),
        P("tp", "groups", None),
        P("groups"),
        P("tp", None),
        P("groups", "tp"),
        P(),
        P(),
        P(None, "tp"),
    )
    return jax.shard_map(
        functools.partial(body, mesh.shape["tp"]),
        mesh=mesh,
        in_specs=placed,
        out_specs=(P("groups", "tp"), P("groups", "tp")),
        check_vma=False,
    )
```

```python
import functools
import math

import jax
import jax.numpy as jnp
import numpy as np
from jax import lax
from jax.experimental import pallas as pl
from jax.experimental.pallas import tpu as pltpu
from jax.sharding import PartitionSpec as P

HD = 128
ROT = 128
OUTER = 4

F32 = jnp.float32
BF16 = jnp.bfloat16
MIB = 1024 * 1024


def hadamard(length):
    rows = np.arange(length)
    common = rows[:, None] & rows[None, :]
    parity = np.zeros((length, length), np.int64)
    for bit in range(length.bit_length()):
        parity += (common >> bit) & 1
    return (1 - 2 * (parity & 1)).astype(np.float32)


def vmem():
    return pl.BlockSpec(memory_space=pltpu.VMEM)


def anywhere():
    return pl.BlockSpec(memory_space=pl.ANY)


def place(inner):
    index = lax.axis_index("tp")
    return lax.div(index, 2 * inner), lax.rem(lax.div(index, 2), inner), lax.rem(index, 2)


def targets(outer):
    near = outer + 1 - 2 * lax.rem(outer, 2)
    return OUTER - 1 - outer, lax.rem(outer + 2, OUTER), near, outer


def is_inner(outer):
    return jnp.logical_or(outer == 1, outer == 2)


def kernel_call(kernel, out_shape, arrays, specs, after=(), scratch=(), aliases=None, limit=24, name=None):
    extra = len(after)

    def ordered(*refs):
        kernel(*refs[extra:])

    return pl.pallas_call(
        ordered,
        out_shape=out_shape,
        in_specs=[anywhere()] * extra + list(specs),
        out_specs=jax.tree.map(lambda _: vmem(), out_shape),
        scratch_shapes=list(scratch),
        input_output_aliases=aliases or {},
        cost_estimate=pl.CostEstimate(flops=0, bytes_accessed=0, transcendentals=0),
        compiler_params=pltpu.CompilerParams(vmem_limit_bytes=limit * MIB),
        name=name,
    )(*after, *arrays)


def gridded(context, h_ref, weight, scale_row, store):
    cols = weight.shape[1]
    count = cols // ROT
    value = jnp.dot(context, weight, preferred_element_type=F32).astype(BF16)
    stacked = jnp.concatenate([value[:, i * ROT : (i + 1) * ROT] for i in range(count)], axis=0)
    turned = jnp.dot(stacked, h_ref[...], preferred_element_type=F32)
    tok = value.shape[0]
    for i in range(count):
        part = turned[i * tok : (i + 1) * tok] * scale_row(i)
        store(i, jnp.clip(part, -127.0, 127.0).astype(BF16))


def attend_kernel(
    inner, cols, chunk, q_hbm, k_hbm, v_hbm, w_hbm, pos_hbm, table_hbm, h_hbm,
    ctx_ref, rows_ref, send_ref, w_ref, h_ref, k_ref, v_ref, s_ref, q_ref, pos_ref, table_ref, sems,
):
    tok = q_ref.shape[0]
    slots = k_ref.shape[0]
    steps = slots // chunk
    outer, mid, core = place(inner)
    dest = targets(outer)[0]

    copies = min(4, steps)
    per_copy = steps // copies
    size = slots // copies

    def copy_k(j):
        part = pl.ds(j * size, size)
        return pltpu.make_async_copy(k_hbm.at[0, part], k_ref.at[part], sems.at[1 + j])

    def copy_v(j):
        part = pl.ds(j * size, size)
        return pltpu.make_async_copy(v_hbm.at[0, part], v_ref.at[part], sems.at[1 + steps + j])

    def shard_of(shift):
        return (dest * inner + lax.rem(mid + shift, inner)) * 2 + 1 - core

    copy_w = pltpu.make_async_copy(w_hbm, w_ref, sems.at[2 * steps + 1])
    copy_q = pltpu.make_async_copy(q_hbm.at[0], q_ref, sems.at[0])
    copy_pos = pltpu.make_async_copy(pos_hbm, pos_ref, sems.at[2 * steps + 2])
    copy_table = pltpu.make_async_copy(table_hbm, table_ref, sems.at[2 * steps + 3])
    copy_h = pltpu.make_async_copy(h_hbm, h_ref, sems.at[2 * steps + 4])
    copy_q.start()
    copy_pos.start()
    for j in range(copies):
        copy_k(j).start()
    copy_table.start()
    copy_h.start()
    for j in range(copies):
        copy_v(j).start()
    copy_w.start()

    copy_pos.wait()
    positions = jnp.broadcast_to(pos_ref[...].astype(F32), (ROT, tok)).T
    ahead = positions.astype(jnp.int32) - lax.broadcasted_iota(jnp.int32, (tok, ROT), 1)

    copy_q.wait()
    queries = q_ref[...]
    peak = jnp.full((tok, ROT), -jnp.inf, F32)
    for j in range(steps):
        if j % per_copy == 0:
            copy_k(j // per_copy).wait()
        scores = lax.dot_general(
            queries, k_ref[j * chunk : (j + 1) * chunk], (((1,), (1,)), ((), ())),
            preferred_element_type=F32,
        )
        for i in range(chunk // ROT):
            base = j * chunk + i * ROT
            part = jnp.where(ahead >= base, scores[:, i * ROT : (i + 1) * ROT], -jnp.inf)
            s_ref[:, base : base + ROT] = part
            peak = jnp.maximum(peak, part)
    copy_table.wait()
    table = table_ref[...].astype(F32)
    count = table.shape[1]
    for i in range(2):
        rows_ref[i] = jnp.broadcast_to(table[i : i + 1], (ROT, count)).T
    largest = jnp.max(peak, axis=1, keepdims=True)
    factor = math.log2(math.e) / math.sqrt(HD)
    total = jnp.zeros((tok, ROT), F32)
    acc = jnp.zeros((tok, HD), F32)
    for j in range(copies):
        copy_v(j).wait()
    for j in range(steps):
        pieces = []
        for i in range(chunk // ROT):
            base = j * chunk + i * ROT
            raised = jnp.exp2((s_ref[:, base : base + ROT] - largest) * factor)
            total = total + raised
            pieces.append(raised.astype(BF16))
        acc = acc + jnp.dot(
            jnp.concatenate(pieces, axis=1), v_ref[j * chunk : (j + 1) * chunk],
            preferred_element_type=F32,
        )
    context = (acc / jnp.sum(total, axis=1, keepdims=True)).astype(BF16)
    ctx_ref[...] = context

    per = cols // ROT
    copy_h.wait()
    copy_w.wait()
    for shift in range(1, inner):
        first = shard_of(shift) * per
        start = pl.multiple_of(shard_of(shift) * cols, 128)

        def scale_row(i):
            return (65536.0 / math.sqrt(ROT)) / rows_ref[0, pl.ds(first + i, 1), :]

        def store(i, value):
            send_ref[shift - 1, :, i * ROT : (i + 1) * ROT] = value

        gridded(context, h_ref, w_ref[:, pl.ds(start, cols)], scale_row, store)


def attend(inner, cols, queries, keys, values, weight, positions, table, had):
    tok, slots = queries.shape[1], keys.shape[1]
    chunk = min(1024, slots)
    steps = slots // chunk
    blocks = table.shape[1]
    arrays = [queries, keys, values, weight, positions[None, :], table, had]
    return kernel_call(
        functools.partial(attend_kernel, inner, cols, chunk),
        [
            pltpu.VMEM((tok, HD), BF16),
            pltpu.VMEM((2, blocks, ROT), F32),
            pltpu.VMEM((inner - 1, tok, cols), BF16),
            pltpu.VMEM(weight.shape, BF16),
            pltpu.VMEM(had.shape, BF16),
        ],
        [pltpu.with_memory_space_constraint(array, pltpu.HBM) for array in arrays],
        [pl.BlockSpec(memory_space=pltpu.HBM)] * len(arrays),
        scratch=[
            pltpu.VMEM((slots, HD), BF16),
            pltpu.VMEM((slots, HD), BF16),
            pltpu.VMEM((tok, slots), F32),
            pltpu.VMEM((tok, HD), BF16),
            pltpu.VMEM((1, tok), positions.dtype),
            pltpu.VMEM(table.shape, table.dtype),
            pltpu.SemaphoreType.DMA((2 * steps + 5,)),
        ],
        limit=28,
        name="attend",
    )


def partial_kernel(inner, work, ctx_ref, w_ref, rows_ref, h_ref, *out_refs):
    cols = out_refs[0].shape[2]
    per = cols // ROT
    outer, mid, core = place(inner)
    dests = targets(outer)
    context = ctx_ref[...]
    for out_ref, (mine, blocks) in zip(out_refs, work):
        for at, (phase, shift) in enumerate(blocks):
            shard = (dests[phase] * inner + lax.rem(mid + shift, inner)) * 2
            shard = shard + (core if mine else 1 - core)

            def scale_row(i):
                return (65536.0 / math.sqrt(ROT)) / rows_ref[0, pl.ds(shard * per + i, 1), :]

            def store(i, value):
                out_ref[at, :, i * ROT : (i + 1) * ROT] = value

            start = pl.multiple_of(shard * cols, 128)
            gridded(context, h_ref, w_ref[:, pl.ds(start, cols)], scale_row, store)


def partials(inner, cols, work, context, weight, rows, had, after=()):
    tok = context.shape[0]
    count = sum(len(blocks) for _, blocks in work)
    return kernel_call(
        functools.partial(partial_kernel, inner, work),
        [jax.ShapeDtypeStruct((len(blocks), tok, cols), BF16) for _, blocks in work],
        [context, weight, rows, had],
        [vmem()] * 4,
        after=after,
        name="partials",
    )


UPPER, LOWER = 0, 1


def add_kernel(inner, inputs, outputs, *refs):
    ins, outs = refs[:inputs], refs[inputs:]
    outer = place(inner)[0]
    rows = ins[0].shape[-2] // 2
    for out_ref, (items, which_half) in zip(outs, outputs):
        for half in (UPPER, LOWER) if which_half is None else (which_half,):
            part = slice(half * rows, (half + 1) * rows)
            total = None
            for which, at, inner_only, item_half in items:
                if item_half is not None and item_half != half:
                    continue
                ref = ins[which] if at is None else ins[which].at[at]
                value = (ref[part] if item_half is None else ref[...]).astype(F32)
                if inner_only:
                    value = jnp.where(is_inner(outer), value, 0.0)
                total = value if total is None else total + value
            if which_half is None:
                out_ref[part] = total.astype(BF16)
            else:
                out_ref[...] = total.astype(BF16)


def add_up(inner, arrays, outputs, after=()):
    rows, cols = arrays[0].shape[-2:]
    shapes = [
        jax.ShapeDtypeStruct((rows if half is None else rows // 2, cols), BF16) for _, half in outputs
    ]
    return kernel_call(
        functools.partial(add_kernel, inner, len(arrays), outputs),
        shapes,
        arrays,
        [vmem()] * len(arrays),
        after=after,
        name="add_up",
    )


def turn_residual_kernel(inner, res_ref, rows_ref, h_ref, out_ref, factor_ref):
    per = res_ref.shape[1] // ROT
    first = lax.axis_index("tp") * per
    for i in range(per):
        part = slice(i * ROT, (i + 1) * ROT)
        high = 256.0 / rows_ref[1, pl.ds(first + i, 1), :]
        low = rows_ref[0, pl.ds(first + i, 1), :] * (1.0 / 65536.0)
        turned = jnp.dot(res_ref[:, part], h_ref[...], preferred_element_type=F32)
        out_ref[:, part] = turned * (high * (1.0 / math.sqrt(ROT)))
        factor_ref[0:1, part] = low * high
        factor_ref[1:2, part] = low


def turn_residual(inner, residual, rows, had, after=()):
    return kernel_call(
        functools.partial(turn_residual_kernel, inner),
        [
            jax.ShapeDtypeStruct(residual.shape, F32),
            jax.ShapeDtypeStruct((2, residual.shape[1]), F32),
        ],
        [residual, rows, had],
        [vmem()] * 3,
        after=after,
        name="turn_residual",
    )


def summed_at(inner, items, ins, part):
    outer = place(inner)[0]
    total = None
    for (at, inner_only), ref in zip(items, ins):
        value = (ref[:, part] if at is None else ref[at, :, part]).astype(F32)
        if inner_only:
            value = jnp.where(is_inner(outer), value, 0.0)
        total = value if total is None else total + value
    return total


def regrid_kernel(inner, items, *refs):
    *ins, turned_ref, factor_ref, grid_ref = refs
    for i in range(turned_ref.shape[1] // ROT):
        part = slice(i * ROT, (i + 1) * ROT)
        value = turned_ref[:, part] + summed_at(inner, items, ins, part) * factor_ref[0:1, part]
        grid_ref[:, part] = jnp.clip(value, -127.0, 127.0).astype(BF16)


def regrid(inner, items, turned, factors, arrays, after=()):
    return kernel_call(
        functools.partial(regrid_kernel, inner, items),
        jax.ShapeDtypeStruct(turned.shape, BF16),
        [*arrays, turned, factors],
        [vmem()] * (2 + len(arrays)),
        after=after,
        name="regrid",
    )


def hidden_kernel(inner, items, res_ref, factor_ref, h_ref, *refs):
    *ins, out_ref, mark_ref = refs
    mark_ref[...] = jnp.zeros_like(mark_ref)
    for i in range(res_ref.shape[1] // ROT):
        part = slice(i * ROT, (i + 1) * ROT)
        value = summed_at(inner, items, ins, part) * factor_ref[1:2, part]
        upper = value.astype(BF16)
        lower = (value - upper.astype(F32)).astype(BF16)
        turned = jnp.dot(upper, h_ref[...], preferred_element_type=F32)
        turned = turned + jnp.dot(lower, h_ref[...], preferred_element_type=F32)
        stream = res_ref[:, part].astype(F32) + turned * (1.0 / math.sqrt(ROT))
        out_ref[:, part] = stream.astype(BF16)


def hidden(inner, items, residual, factors, had, arrays, after=()):
    return kernel_call(
        functools.partial(hidden_kernel, inner, items),
        [jax.ShapeDtypeStruct(residual.shape, BF16), jax.ShapeDtypeStruct((8, ROT), F32)],
        [residual, factors, had, *arrays],
        [vmem()] * (3 + len(arrays)),
        after=after,
        name="hidden",
    )


def choose_kernel(inner, count, *refs):
    inside = is_inner(place(inner)[0])
    inner_ref, end_ref, *refs = refs
    others, (out_ref, *outs) = refs[:count], refs[count:]
    lower, upper = outs[:count], outs[count:]

    def put(ref):
        out_ref[...] = ref[...]
        for half in upper:
            half[...] = ref[: half.shape[0]]

    @pl.when(inside)
    def _():
        put(inner_ref)

    @pl.when(jnp.logical_not(inside))
    def _():
        put(end_ref)

    for ref, half in zip(others, lower):
        half[...] = ref[half.shape[0] :]


def choose(inner, at_inner, at_end, others=(), halved=False, after=()):
    rows, cols = at_inner.shape
    half = jax.ShapeDtypeStruct((rows // 2, cols), BF16)
    return kernel_call(
        functools.partial(choose_kernel, inner, len(others)),
        [jax.ShapeDtypeStruct((rows, cols), BF16)] + [half] * (len(others) + halved),
        [at_inner, at_end, *others],
        [vmem()] * (2 + len(others)),
        after=after,
        name="choose",
    )


def gate_kernel(count, *refs):
    for ref, half in zip(refs[:count], refs[-count:]):
        half[...] = ref[half.shape[0] :]


def gate(arrays, others, after):
    rows, cols = arrays[0].shape
    shapes = [jax.ShapeDtypeStruct((rows, cols), BF16)] * len(arrays)
    half = jax.ShapeDtypeStruct((rows // 2, cols), BF16)
    aliases = {len(after) + len(others) + i: i for i in range(len(arrays))}
    return kernel_call(
        functools.partial(gate_kernel, len(others)),
        shapes + [half] * len(others),
        [*others, *arrays],
        [vmem()] * (len(others) + len(arrays)),
        after=after,
        aliases=aliases,
        name="gate",
    )


def select_rows_kernel(inner, cols, w_ref, *out_refs):
    other = 1 - place(inner)[2]
    each = out_refs[0].shape[0]
    for j in range(each * len(out_refs)):
        start = pl.multiple_of((2 * j + other) * cols, 128)
        out_refs[j // each][j % each] = w_ref[pl.ds(start, cols), :]


def select_rows(inner, weight, cols, after=()):
    parts = 2
    each = OUTER * inner // parts
    return kernel_call(
        functools.partial(select_rows_kernel, inner, cols),
        [jax.ShapeDtypeStruct((each, cols, weight.shape[1]), weight.dtype)] * parts,
        [weight],
        [vmem()],
        after=after,
        name="select_rows",
    )


def turn_next_kernel(inner, cols, own_ref, gain_ref, rows_ref, h_ref, *refs):
    *other_refs, out_ref = refs
    each = other_refs[0].shape[0]
    core = place(inner)[2]
    for j in range(out_ref.shape[0]):
        shard = j * 2 + core
        for i in range(cols // ROT):
            block = shard * (cols // ROT) + i
            factor = rows_ref[1, pl.ds(block, 1), :] * (1.0 / (256.0 * math.sqrt(ROT)))
            rotation = (h_ref[...].astype(F32) * gain_ref[pl.ds(block, 1), :]).astype(BF16)
            part = slice(i * ROT, (i + 1) * ROT)
            own = own_ref[pl.ds(pl.multiple_of(block * ROT, ROT), ROT), :]
            for half, value in enumerate((own, other_refs[j // each][j % each, part, :])):
                turned = jnp.dot(rotation, value, preferred_element_type=F32)
                out_ref[j, part, half * HD : (half + 1) * HD] = (turned * factor).astype(BF16)


def turn_next(inner, weight, others, gain, rows, had, after=()):
    _, cols, width = others[0].shape
    return kernel_call(
        functools.partial(turn_next_kernel, inner, cols),
        jax.ShapeDtypeStruct((OUTER * inner, cols, 2 * width), BF16),
        [weight, gain, rows, had, *others],
        [vmem()] * (4 + len(others)),
        after=after,
        name="turn_next",
    )


def project_kernel(inner, places, has_acc, split, w_ref, rows_ref, *refs):
    outer, mid, core = place(inner)
    order = targets(outer)[::-1]
    acc_in = refs[0] if has_acc else None
    refs = refs[1:] if has_acc else refs
    count = sum(parts for _, _, parts in places)
    values_in = list(refs[:count])
    outs = refs[count:]
    cols, width = w_ref.shape[1:]
    acc = acc_in[:, :width] if has_acc else 0.0
    squares = acc_in[:, width:] if has_acc else 0.0
    for phase, shift, parts in places:
        block = order[phase] * inner + lax.rem(mid + inner - shift, inner)
        values = values_in.pop(0)[...]
        if parts == 3:
            at_inner, at_end = values_in.pop(0)[...], values_in.pop(0)[...]
            lower = jnp.where(is_inner(outer), at_inner, at_end)
            values = jnp.concatenate([values, lower], axis=0)
        acc = acc + jnp.dot(values, w_ref[block], preferred_element_type=F32)
        for i in range(cols // ROT):
            row = (block * 2 + core) * (cols // ROT) + i
            high = rows_ref[1, pl.ds(row, 1), :] * (1.0 / 256.0)
            value = values[:, i * ROT : (i + 1) * ROT].astype(F32) * high
            squares = squares + value * value
    if split:
        own_ref, other_ref = outs
        own_ref[:, :HD] = acc[:, :HD]
        own_ref[:, HD:] = squares
        other_ref[:, :HD] = acc[:, HD:]
        other_ref[:, HD:] = squares
    else:
        outs[0][:, :width] = acc
        outs[0][:, width:] = squares


def project(inner, weight, rows, acc, pieces, split=False, after=()):
    _, cols, width = weight.shape
    arrays = [part for _, _, parts in pieces for part in parts]
    first = pieces[0][2]
    tok = first[0].shape[0] * (1 if len(first) == 1 else 2)
    places = tuple((phase, shift, len(parts)) for phase, shift, parts in pieces)
    accs = [] if acc is None else [acc]
    if split:
        out = [jax.ShapeDtypeStruct((tok, HD + ROT), F32)] * 2
    else:
        out = jax.ShapeDtypeStruct((tok, width + ROT), F32)
    return kernel_call(
        functools.partial(project_kernel, inner, places, acc is not None, split),
        out,
        [weight, rows, *accs, *arrays],
        [vmem()] * (2 + len(accs) + len(arrays)),
        after=after,
        name="project",
    )


def finish_kernel(features, own_ref, other_ref, out_ref):
    squares = own_ref[:, HD:] + other_ref[:, HD:]
    mean = jnp.sum(squares, axis=1, keepdims=True) * (1.0 / features)
    value = (own_ref[:, :HD] + other_ref[:, :HD]) * lax.rsqrt(mean + 1e-05)
    out_ref[...] = value.astype(BF16)


def finish(own, other, features):
    tok = own.shape[0]
    return kernel_call(
        functools.partial(finish_kernel, features),
        jax.ShapeDtypeStruct((tok, HD), BF16),
        [own, other],
        [vmem()] * 2,
        name="finish",
    )


def body(
    size,
    queries,
    cache_keys,
    cache_values,
    query_positions,
    out_weight,
    residual,
    scale_table,
    norm_gain,
    next_query_weight,
):
    inner = size // (2 * OUTER)
    cols = residual.shape[1]
    had = jnp.asarray(hadamard(ROT), BF16)
    shifts = range(1, inner)

    def permute(value, move):
        moves = []
        for i in range(size):
            spot = move(i // (2 * inner), (i // 2) % inner, i % 2)
            moves.append((i, (spot[0] * inner + spot[1]) * 2 + spot[2]))
        return lax.ppermute(value, "tp", moves)

    def swap_core(value):
        return permute(value, lambda a, b, c: (a, b, 1 - c))

    def shift_mid(value, shift):
        return permute(value, lambda a, b, c: (a, (b + shift) % inner, c))

    def swap_pairs(value):
        return permute(value, lambda a, b, c: (a ^ 1, b, c))

    def swap_middle(value):
        return permute(value, lambda a, b, c: (a, b, 1 - c) if a in (0, 3) else (3 - a, b, c))

    everything = range(inner)
    context, rows, send1, out_weight, had = attend(
        inner, cols, queries, cache_keys, cache_values, out_weight, query_positions, scale_table, had
    )
    other1 = swap_core(send1)
    away1 = tuple((0, s) for s in shifts)
    def phase_blocks(phase):
        return tuple((phase, s) for s in everything)

    def grid_blocks(work, after=()):
        return partials(inner, cols, work, context, out_weight, rows, had, after=after)

    blocks2 = ((0, 0),) + tuple((1, s) for s in shifts)
    keep1, keep2, *send2 = grid_blocks(
        ((True, away1), (True, blocks2), *((False, (block,)) for block in blocks2))
    )
    other2 = [swap_core(send) for send in send2]
    items1 = [[(0, s - 1, False, None), (1, s - 1, False, None)] for s in shifts]
    first = add_up(
        inner,
        [keep1, other1],
        [(items, UPPER) for items in items1] + [(items, LOWER) for items in items1],
        after=[keep2],
    )
    pay1, low1 = first[: len(shifts)], first[len(shifts) :]
    come1 = [shift_mid(pay, s) for s, pay in zip(shifts, pay1)]
    low_pairs = [swap_pairs(low) for low in low1]
    low_middle = [swap_middle(low) for low in low1]
    near_block = ((1, 0),)
    send2n, send3 = grid_blocks(((False, near_block), (False, phase_blocks(2))), pay1[:1])
    other2n, other3 = swap_core(send2n), swap_core(send3)
    send4, keep2n, keep3, keep4 = grid_blocks(
        (
            (False, phase_blocks(3)),
            (True, near_block),
            (True, phase_blocks(2)),
            (True, phase_blocks(3)),
        ),
        [send3],
    )
    other4 = swap_core(send4)

    def sums(arrays, outputs, after=()):
        names = list(arrays)
        items = [
            ([(names.index(name), *rest) for name, *rest in output], None) for output in outputs
        ]
        return add_up(inner, list(arrays.values()), items, after=after)

    def named(name, blocks):
        return {f"{name}_{s}": block for s, block in zip(shifts, blocks)}

    def added(names, half=None):
        return [(name, None, False, half) for name in names]

    own2 = {"keep2": keep2} | {f"other2_{i}": other for i, other in enumerate(other2)}
    own2n = {"keep2n": keep2n, "other2n": other2n}
    own3 = {"keep3": keep3, "other3": other3}
    own4 = {"keep4": keep4, "other4": other4}

    def part2(i):
        return [("keep2", i, False, None), (f"other2_{i}", 0, False, None)]

    def part(step, s):
        return [(f"keep{step}", s, False, None), (f"other{step}", s, False, None)]

    def passed(name, s):
        return [(f"{name}_{s}", None, True, LOWER)]

    def relayed(name):
        return [(name, None, True, None)]

    came1, from_pairs = named("came1", come1), named("pairs", low_pairs)
    from_middle = named("middle", low_middle)
    near1 = part2(0) + added(came1, UPPER)
    *pay2, end1 = sums(
        own2 | came1 | from_pairs,
        [*(part2(s) + passed("pairs", s) for s in shifts), near1],
        after=[*come1, send4],
    )
    came2 = named("came2", [shift_mid(pay, s) for s, pay in zip(shifts, pay2)])
    from_end1 = {"end1": swap_pairs(end1)}
    turned_residual, factors = turn_residual(inner, residual, rows, had, after=[end1])
    picked = select_rows(inner, next_query_weight, cols, after=[factors])
    next_other = [swap_core(part) for part in picked]

    near2 = part("2n", 0) + added(came2)
    *pay3, sum2 = sums(
        came2 | from_end1 | own2n | own3,
        [*(part(3, s) for s in shifts), near2 + relayed("end1")],
        after=[*picked[:1], *low_middle],
    )
    came3 = named("came3", [shift_mid(pay, s) for s, pay in zip(shifts, pay3)])
    from_end2 = {"end2": swap_pairs(sum2)}
    from_mid2 = {"mid2": swap_middle(sum2)}

    *pay4, near3, mid3 = sums(
        came3 | from_end2 | from_mid2 | own2 | own3 | own4 | came1 | from_middle,
        [
            *(part(4, s) + passed("middle", s) for s in shifts),
            part(3, 0) + added(came3) + relayed("mid2"),
            near1 + relayed("end2"),
        ],
    )
    come4 = [shift_mid(pay, s) for s, pay in zip(shifts, pay4)]
    from_mid3 = swap_middle(mid3)
    from_near3 = swap_pairs(near3)

    gain = norm_gain.astype(F32).reshape(-1, ROT)

    last = [*come4, from_near3, from_mid3, keep4, other4]
    items = [(None, False)] * (len(come4) + 1) + [(None, True)] + [(0, False)] * 2
    grid = regrid(inner, items, turned_residual, factors, last)

    x1 = [shift_mid(grid, s) for s in shifts]
    near = swap_pairs(grid)
    mid1 = swap_middle(grid)
    hidden_out, mark = hidden(inner, items, residual, factors, had, last, after=[grid])
    near, mid1, *low1 = gate([near, mid1], x1, after=[mark])
    x2 = [shift_mid(near, s) for s in shifts]
    ends2 = swap_pairs(mid1)
    mids2 = swap_middle(near)
    (third,) = choose(inner, mids2, ends2, after=x2)
    x3 = [shift_mid(third, s) for s in shifts]
    ends3 = swap_pairs(mids2)
    side_middle = [swap_middle(low) for low in low1]
    turned_next = turn_next(inner, next_query_weight, next_other, gain, rows, had, after=[third])
    fourth, *low3, up4 = choose(inner, mid1, ends3, x3, True, after=[turned_next])
    x4 = [shift_mid(up4, s) for s in shifts]
    side_pairs = [swap_pairs(low) for low in low3]
    acc = project(
        inner,
        turned_next,
        rows,
        None,
        [(0, 0, [grid]), (1, 0, [near]), (2, 0, [third]), (3, 0, [fourth])]
        + [(phase, s, [x[s - 1]]) for phase, x in enumerate((x1, x2, x3)) for s in shifts],
    )
    own, other = project(
        inner,
        turned_next,
        rows,
        acc,
        [(3, s, [x4[s - 1], side_middle[s - 1], side_pairs[s - 1]]) for s in shifts],
        split=True,
    )
    query_next = finish(own, swap_core(other), norm_gain.shape[0])
    return (hidden_out, query_next)


def solution(mesh):
    placed = (
        P("tp", "groups", None),
        P("tp", "groups", None),
        P("tp", "groups", None),
        P("groups"),
        P("tp", None),
        P("groups", "tp"),
        P(),
        P(),
        P(None, "tp"),
    )
    return jax.shard_map(
        functools.partial(body, mesh.shape["tp"]),
        mesh=mesh,
        in_specs=placed,
        out_specs=(P("groups", "tp"), P("groups", "tp")),
        check_vma=False,
    )
```

```python
import functools
import math

import jax
import jax.numpy as jnp
import numpy as np
from jax import lax
from jax.experimental import pallas as pl
from jax.experimental.pallas import tpu as pltpu
from jax.sharding import PartitionSpec as P

HD = 128
ROT = 128
OUTER = 4

F32 = jnp.float32
BF16 = jnp.bfloat16
MIB = 1024 * 1024


def hadamard(length):
    rows = np.arange(length)
    common = rows[:, None] & rows[None, :]
    parity = np.zeros((length, length), np.int64)
    for bit in range(length.bit_length()):
        parity += (common >> bit) & 1
    return (1 - 2 * (parity & 1)).astype(np.float32)


def vmem():
    return pl.BlockSpec(memory_space=pltpu.VMEM)


def anywhere():
    return pl.BlockSpec(memory_space=pl.ANY)


def place(inner):
    index = lax.axis_index("tp")
    return lax.div(index, 2 * inner), lax.rem(lax.div(index, 2), inner), lax.rem(index, 2)


def targets(outer):
    near = outer + 1 - 2 * lax.rem(outer, 2)
    return OUTER - 1 - outer, lax.rem(outer + 2, OUTER), near, outer


def is_inner(outer):
    return jnp.logical_or(outer == 1, outer == 2)


def kernel_call(kernel, out_shape, arrays, specs, after=(), scratch=(), aliases=None, limit=24, name=None):
    extra = len(after)

    def ordered(*refs):
        kernel(*refs[extra:])

    return pl.pallas_call(
        ordered,
        out_shape=out_shape,
        in_specs=[anywhere()] * extra + list(specs),
        out_specs=jax.tree.map(lambda _: vmem(), out_shape),
        scratch_shapes=list(scratch),
        input_output_aliases=aliases or {},
        cost_estimate=pl.CostEstimate(flops=0, bytes_accessed=0, transcendentals=0),
        compiler_params=pltpu.CompilerParams(vmem_limit_bytes=limit * MIB),
        name=name,
    )(*after, *arrays)


def gridded(context, h_ref, weight, scale_row, store):
    cols = weight.shape[1]
    count = cols // ROT
    value = jnp.dot(context, weight, preferred_element_type=F32).astype(BF16)
    stacked = jnp.concatenate([value[:, i * ROT : (i + 1) * ROT] for i in range(count)], axis=0)
    turned = jnp.dot(stacked, h_ref[...], preferred_element_type=F32)
    tok = value.shape[0]
    for i in range(count):
        part = turned[i * tok : (i + 1) * tok] * scale_row(i)
        store(i, jnp.clip(part, -127.0, 127.0).astype(BF16))


def attend_kernel(
    inner, cols, chunk, q_hbm, k_hbm, v_hbm, w_hbm, pos_hbm, table_hbm, h_hbm,
    ctx_ref, rows_ref, send_ref, w_ref, h_ref, k_ref, v_ref, s_ref, q_ref, pos_ref, table_ref, sems,
):
    tok = q_ref.shape[0]
    slots = k_ref.shape[0]
    steps = slots // chunk
    outer, mid, core = place(inner)
    dest = targets(outer)[0]

    copies = min(4, steps)
    per_copy = steps // copies
    size = slots // copies

    def copy_k(j):
        part = pl.ds(j * size, size)
        return pltpu.make_async_copy(k_hbm.at[0, part], k_ref.at[part], sems.at[1 + j])

    def copy_v(j):
        part = pl.ds(j * size, size)
        return pltpu.make_async_copy(v_hbm.at[0, part], v_ref.at[part], sems.at[1 + steps + j])

    def shard_of(shift):
        return (dest * inner + lax.rem(mid + shift, inner)) * 2 + 1 - core

    copy_w = pltpu.make_async_copy(w_hbm, w_ref, sems.at[2 * steps + 1])
    copy_q = pltpu.make_async_copy(q_hbm.at[0], q_ref, sems.at[0])
    copy_pos = pltpu.make_async_copy(pos_hbm, pos_ref, sems.at[2 * steps + 2])
    copy_table = pltpu.make_async_copy(table_hbm, table_ref, sems.at[2 * steps + 3])
    copy_h = pltpu.make_async_copy(h_hbm, h_ref, sems.at[2 * steps + 4])
    copy_q.start()
    copy_pos.start()
    for j in range(copies):
        copy_k(j).start()
    copy_table.start()
    copy_h.start()
    for j in range(copies):
        copy_v(j).start()
    copy_w.start()

    copy_pos.wait()
    positions = jnp.broadcast_to(pos_ref[...].astype(F32), (ROT, tok)).T
    ahead = positions.astype(jnp.int32) - lax.broadcasted_iota(jnp.int32, (tok, ROT), 1)

    copy_q.wait()
    queries = q_ref[...]
    peak = jnp.full((tok, ROT), -jnp.inf, F32)
    for j in range(steps):
        if j % per_copy == 0:
            copy_k(j // per_copy).wait()
        scores = lax.dot_general(
            queries, k_ref[j * chunk : (j + 1) * chunk], (((1,), (1,)), ((), ())),
            preferred_element_type=F32,
        )
        for i in range(chunk // ROT):
            base = j * chunk + i * ROT
            part = jnp.where(ahead >= base, scores[:, i * ROT : (i + 1) * ROT], -jnp.inf)
            s_ref[:, base : base + ROT] = part
            peak = jnp.maximum(peak, part)
    copy_table.wait()
    table = table_ref[...].astype(F32)
    count = table.shape[1]
    for i in range(2):
        rows_ref[i] = jnp.broadcast_to(table[i : i + 1], (ROT, count)).T
    largest = jnp.max(peak, axis=1, keepdims=True)
    factor = math.log2(math.e) / math.sqrt(HD)
    total = jnp.zeros((tok, ROT), F32)
    acc = jnp.zeros((tok, HD), F32)
    for j in range(copies):
        copy_v(j).wait()
    for j in range(steps):
        pieces = []
        for i in range(chunk // ROT):
            base = j * chunk + i * ROT
            raised = jnp.exp2((s_ref[:, base : base + ROT] - largest) * factor)
            total = total + raised
            pieces.append(raised.astype(BF16))
        acc = acc + jnp.dot(
            jnp.concatenate(pieces, axis=1), v_ref[j * chunk : (j + 1) * chunk],
            preferred_element_type=F32,
        )
    context = (acc / jnp.sum(total, axis=1, keepdims=True)).astype(BF16)
    ctx_ref[...] = context

    per = cols // ROT
    copy_h.wait()
    copy_w.wait()
    for shift in range(1, inner):
        first = shard_of(shift) * per
        start = pl.multiple_of(shard_of(shift) * cols, 128)

        def scale_row(i):
            return (65536.0 / math.sqrt(ROT)) / rows_ref[0, pl.ds(first + i, 1), :]

        def store(i, value):
            send_ref[shift - 1, :, i * ROT : (i + 1) * ROT] = value

        gridded(context, h_ref, w_ref[:, pl.ds(start, cols)], scale_row, store)


def attend(inner, cols, queries, keys, values, weight, positions, table, had):
    tok, slots = queries.shape[1], keys.shape[1]
    chunk = min(1024, slots)
    steps = slots // chunk
    blocks = table.shape[1]
    arrays = [queries, keys, values, weight, positions[None, :], table, had]
    return kernel_call(
        functools.partial(attend_kernel, inner, cols, chunk),
        [
            pltpu.VMEM((tok, HD), BF16),
            pltpu.VMEM((2, blocks, ROT), F32),
            pltpu.VMEM((inner - 1, tok, cols), BF16),
            pltpu.VMEM(weight.shape, BF16),
            pltpu.VMEM(had.shape, BF16),
        ],
        [pltpu.with_memory_space_constraint(array, pltpu.HBM) for array in arrays],
        [pl.BlockSpec(memory_space=pltpu.HBM)] * len(arrays),
        scratch=[
            pltpu.VMEM((slots, HD), BF16),
            pltpu.VMEM((slots, HD), BF16),
            pltpu.VMEM((tok, slots), F32),
            pltpu.VMEM((tok, HD), BF16),
            pltpu.VMEM((1, tok), positions.dtype),
            pltpu.VMEM(table.shape, table.dtype),
            pltpu.SemaphoreType.DMA((2 * steps + 5,)),
        ],
        limit=28,
        name="attend",
    )


def partial_kernel(inner, work, ctx_ref, w_ref, rows_ref, h_ref, *out_refs):
    cols = out_refs[0].shape[2]
    per = cols // ROT
    outer, mid, core = place(inner)
    dests = targets(outer)
    context = ctx_ref[...]
    for out_ref, (mine, blocks) in zip(out_refs, work):
        for at, (phase, shift) in enumerate(blocks):
            shard = (dests[phase] * inner + lax.rem(mid + shift, inner)) * 2
            shard = shard + (core if mine else 1 - core)

            def scale_row(i):
                return (65536.0 / math.sqrt(ROT)) / rows_ref[0, pl.ds(shard * per + i, 1), :]

            def store(i, value):
                out_ref[at, :, i * ROT : (i + 1) * ROT] = value

            start = pl.multiple_of(shard * cols, 128)
            gridded(context, h_ref, w_ref[:, pl.ds(start, cols)], scale_row, store)


def partials(inner, cols, work, context, weight, rows, had, after=()):
    tok = context.shape[0]
    count = sum(len(blocks) for _, blocks in work)
    return kernel_call(
        functools.partial(partial_kernel, inner, work),
        [jax.ShapeDtypeStruct((len(blocks), tok, cols), BF16) for _, blocks in work],
        [context, weight, rows, had],
        [vmem()] * 4,
        after=after,
        name="partials",
    )


UPPER, LOWER = 0, 1


def add_kernel(inner, inputs, outputs, *refs):
    ins, outs = refs[:inputs], refs[inputs:]
    outer = place(inner)[0]
    rows = ins[0].shape[-2] // 2
    for out_ref, (items, which_half) in zip(outs, outputs):
        for half in (UPPER, LOWER) if which_half is None else (which_half,):
            part = slice(half * rows, (half + 1) * rows)
            total = None
            for which, at, inner_only, item_half in items:
                if item_half is not None and item_half != half:
                    continue
                ref = ins[which] if at is None else ins[which].at[at]
                value = (ref[part] if item_half is None else ref[...]).astype(F32)
                if inner_only:
                    value = jnp.where(is_inner(outer), value, 0.0)
                total = value if total is None else total + value
            if which_half is None:
                out_ref[part] = total.astype(BF16)
            else:
                out_ref[...] = total.astype(BF16)


def add_up(inner, arrays, outputs, after=()):
    rows, cols = arrays[0].shape[-2:]
    shapes = [
        jax.ShapeDtypeStruct((rows if half is None else rows // 2, cols), BF16) for _, half in outputs
    ]
    return kernel_call(
        functools.partial(add_kernel, inner, len(arrays), outputs),
        shapes,
        arrays,
        [vmem()] * len(arrays),
        after=after,
        name="add_up",
    )


def turn_residual_kernel(inner, res_ref, rows_ref, h_ref, out_ref, factor_ref):
    per = res_ref.shape[1] // ROT
    first = lax.axis_index("tp") * per
    for i in range(per):
        part = slice(i * ROT, (i + 1) * ROT)
        high = 256.0 / rows_ref[1, pl.ds(first + i, 1), :]
        low = rows_ref[0, pl.ds(first + i, 1), :] * (1.0 / 65536.0)
        turned = jnp.dot(res_ref[:, part], h_ref[...], preferred_element_type=F32)
        out_ref[:, part] = turned * (high * (1.0 / math.sqrt(ROT)))
        factor_ref[0:1, part] = low * high
        factor_ref[1:2, part] = low


def turn_residual(inner, residual, rows, had, after=()):
    return kernel_call(
        functools.partial(turn_residual_kernel, inner),
        [
            jax.ShapeDtypeStruct(residual.shape, F32),
            jax.ShapeDtypeStruct((2, residual.shape[1]), F32),
        ],
        [residual, rows, had],
        [vmem()] * 3,
        after=after,
        name="turn_residual",
    )


def summed_at(inner, items, ins, part):
    outer = place(inner)[0]
    total = None
    for (at, inner_only), ref in zip(items, ins):
        value = (ref[:, part] if at is None else ref[at, :, part]).astype(F32)
        if inner_only:
            value = jnp.where(is_inner(outer), value, 0.0)
        total = value if total is None else total + value
    return total


def regrid_kernel(inner, items, *refs):
    *ins, turned_ref, factor_ref, grid_ref = refs
    for i in range(turned_ref.shape[1] // ROT):
        part = slice(i * ROT, (i + 1) * ROT)
        value = turned_ref[:, part] + summed_at(inner, items, ins, part) * factor_ref[0:1, part]
        grid_ref[:, part] = jnp.clip(value, -127.0, 127.0).astype(BF16)


def regrid(inner, items, turned, factors, arrays, after=()):
    return kernel_call(
        functools.partial(regrid_kernel, inner, items),
        jax.ShapeDtypeStruct(turned.shape, BF16),
        [*arrays, turned, factors],
        [vmem()] * (2 + len(arrays)),
        after=after,
        name="regrid",
    )


def hidden_kernel(inner, items, res_ref, factor_ref, h_ref, *refs):
    *ins, out_ref, mark_ref = refs
    mark_ref[...] = jnp.zeros_like(mark_ref)
    for i in range(res_ref.shape[1] // ROT):
        part = slice(i * ROT, (i + 1) * ROT)
        value = summed_at(inner, items, ins, part) * factor_ref[1:2, part]
        upper = value.astype(BF16)
        lower = (value - upper.astype(F32)).astype(BF16)
        turned = jnp.dot(upper, h_ref[...], preferred_element_type=F32)
        turned = turned + jnp.dot(lower, h_ref[...], preferred_element_type=F32)
        stream = res_ref[:, part].astype(F32) + turned * (1.0 / math.sqrt(ROT))
        out_ref[:, part] = stream.astype(BF16)


def hidden(inner, items, residual, factors, had, arrays, after=()):
    return kernel_call(
        functools.partial(hidden_kernel, inner, items),
        [jax.ShapeDtypeStruct(residual.shape, BF16), jax.ShapeDtypeStruct((8, ROT), F32)],
        [residual, factors, had, *arrays],
        [vmem()] * (3 + len(arrays)),
        after=after,
        name="hidden",
    )


def choose_kernel(inner, count, *refs):
    inside = is_inner(place(inner)[0])
    inner_ref, end_ref, *refs = refs
    others, (out_ref, *outs) = refs[:count], refs[count:]
    lower, upper = outs[:count], outs[count:]

    def put(ref):
        out_ref[...] = ref[...]
        for half in upper:
            half[...] = ref[: half.shape[0]]

    @pl.when(inside)
    def _():
        put(inner_ref)

    @pl.when(jnp.logical_not(inside))
    def _():
        put(end_ref)

    for ref, half in zip(others, lower):
        half[...] = ref[half.shape[0] :]


def choose(inner, at_inner, at_end, others=(), halved=False, after=()):
    rows, cols = at_inner.shape
    half = jax.ShapeDtypeStruct((rows // 2, cols), BF16)
    return kernel_call(
        functools.partial(choose_kernel, inner, len(others)),
        [jax.ShapeDtypeStruct((rows, cols), BF16)] + [half] * (len(others) + halved),
        [at_inner, at_end, *others],
        [vmem()] * (2 + len(others)),
        after=after,
        name="choose",
    )


def gate_kernel(skip, count, *refs):
    for ref, half in zip(refs[skip : skip + count], refs[-count:]):
        half[...] = ref[half.shape[0] :]


def gate(arrays, others, after):
    rows, cols = arrays[0].shape
    shapes = [jax.ShapeDtypeStruct((rows, cols), BF16)] * len(arrays)
    half = jax.ShapeDtypeStruct((rows // 2, cols), BF16)
    aliases = {len(after) + i: i for i in range(len(arrays))}
    return kernel_call(
        functools.partial(gate_kernel, len(arrays), len(others)),
        shapes + [half] * len(others),
        [*arrays, *others],
        [vmem()] * (len(others) + len(arrays)),
        after=after,
        aliases=aliases,
        name="gate",
    )


def select_rows_kernel(inner, cols, w_ref, *out_refs):
    other = 1 - place(inner)[2]
    each = out_refs[0].shape[0]
    for j in range(each * len(out_refs)):
        start = pl.multiple_of((2 * j + other) * cols, 128)
        out_refs[j // each][j % each] = w_ref[pl.ds(start, cols), :]


def select_rows(inner, weight, cols, after=()):
    parts = 2
    each = OUTER * inner // parts
    return kernel_call(
        functools.partial(select_rows_kernel, inner, cols),
        [jax.ShapeDtypeStruct((each, cols, weight.shape[1]), weight.dtype)] * parts,
        [weight],
        [vmem()],
        after=after,
        name="select_rows",
    )


def turn_next_kernel(inner, cols, own_ref, gain_ref, rows_ref, h_ref, *refs):
    *other_refs, out_ref = refs
    each = other_refs[0].shape[0]
    core = place(inner)[2]
    for j in range(out_ref.shape[0]):
        shard = j * 2 + core
        for i in range(cols // ROT):
            block = shard * (cols // ROT) + i
            factor = rows_ref[1, pl.ds(block, 1), :] * (1.0 / (256.0 * math.sqrt(ROT)))
            rotation = (h_ref[...].astype(F32) * gain_ref[pl.ds(block, 1), :]).astype(BF16)
            part = slice(i * ROT, (i + 1) * ROT)
            own = own_ref[pl.ds(pl.multiple_of(block * ROT, ROT), ROT), :]
            for half, value in enumerate((own, other_refs[j // each][j % each, part, :])):
                turned = jnp.dot(rotation, value, preferred_element_type=F32)
                out_ref[j, part, half * HD : (half + 1) * HD] = (turned * factor).astype(BF16)


def turn_next(inner, weight, others, gain, rows, had, after=()):
    _, cols, width = others[0].shape
    return kernel_call(
        functools.partial(turn_next_kernel, inner, cols),
        jax.ShapeDtypeStruct((OUTER * inner, cols, 2 * width), BF16),
        [weight, gain, rows, had, *others],
        [vmem()] * (4 + len(others)),
        after=after,
        name="turn_next",
    )


def project_kernel(inner, places, has_acc, split, w_ref, rows_ref, *refs):
    outer, mid, core = place(inner)
    order = targets(outer)[::-1]
    acc_in = refs[0] if has_acc else None
    refs = refs[1:] if has_acc else refs
    count = sum(parts for _, _, parts in places)
    values_in = list(refs[:count])
    outs = refs[count:]
    cols, width = w_ref.shape[1:]
    acc = acc_in[:, :width] if has_acc else 0.0
    squares = acc_in[:, width:] if has_acc else 0.0
    for phase, shift, parts in places:
        block = order[phase] * inner + lax.rem(mid + inner - shift, inner)
        values = values_in.pop(0)[...]
        if parts == 3:
            at_inner, at_end = values_in.pop(0)[...], values_in.pop(0)[...]
            lower = jnp.where(is_inner(outer), at_inner, at_end)
            values = jnp.concatenate([values, lower], axis=0)
        acc = acc + jnp.dot(values, w_ref[block], preferred_element_type=F32)
        for i in range(cols // ROT):
            row = (block * 2 + core) * (cols // ROT) + i
            high = rows_ref[1, pl.ds(row, 1), :] * (1.0 / 256.0)
            value = values[:, i * ROT : (i + 1) * ROT].astype(F32) * high
            squares = squares + value * value
    if split:
        own_ref, other_ref = outs
        own_ref[:, :HD] = acc[:, :HD]
        own_ref[:, HD:] = squares
        other_ref[:, :HD] = acc[:, HD:]
        other_ref[:, HD:] = squares
    else:
        outs[0][:, :width] = acc
        outs[0][:, width:] = squares


def project(inner, weight, rows, acc, pieces, split=False, after=()):
    _, cols, width = weight.shape
    arrays = [part for _, _, parts in pieces for part in parts]
    first = pieces[0][2]
    tok = first[0].shape[0] * (1 if len(first) == 1 else 2)
    places = tuple((phase, shift, len(parts)) for phase, shift, parts in pieces)
    accs = [] if acc is None else [acc]
    if split:
        out = [jax.ShapeDtypeStruct((tok, HD + ROT), F32)] * 2
    else:
        out = jax.ShapeDtypeStruct((tok, width + ROT), F32)
    return kernel_call(
        functools.partial(project_kernel, inner, places, acc is not None, split),
        out,
        [weight, rows, *accs, *arrays],
        [vmem()] * (2 + len(accs) + len(arrays)),
        after=after,
        name="project",
    )


def finish_kernel(features, own_ref, other_ref, out_ref):
    squares = own_ref[:, HD:] + other_ref[:, HD:]
    mean = jnp.sum(squares, axis=1, keepdims=True) * (1.0 / features)
    value = (own_ref[:, :HD] + other_ref[:, :HD]) * lax.rsqrt(mean + 1e-05)
    out_ref[...] = value.astype(BF16)


def finish(own, other, features):
    tok = own.shape[0]
    return kernel_call(
        functools.partial(finish_kernel, features),
        jax.ShapeDtypeStruct((tok, HD), BF16),
        [own, other],
        [vmem()] * 2,
        name="finish",
    )


def body(
    size,
    queries,
    cache_keys,
    cache_values,
    query_positions,
    out_weight,
    residual,
    scale_table,
    norm_gain,
    next_query_weight,
):
    inner = size // (2 * OUTER)
    cols = residual.shape[1]
    had = jnp.asarray(hadamard(ROT), BF16)
    shifts = range(1, inner)

    def permute(value, move):
        moves = []
        for i in range(size):
            spot = move(i // (2 * inner), (i // 2) % inner, i % 2)
            moves.append((i, (spot[0] * inner + spot[1]) * 2 + spot[2]))
        return lax.ppermute(value, "tp", moves)

    def swap_core(value):
        return permute(value, lambda a, b, c: (a, b, 1 - c))

    def shift_mid(value, shift):
        return permute(value, lambda a, b, c: (a, (b + shift) % inner, c))

    def swap_pairs(value):
        return permute(value, lambda a, b, c: (a ^ 1, b, c))

    def swap_middle(value):
        return permute(value, lambda a, b, c: (a, b, 1 - c) if a in (0, 3) else (3 - a, b, c))

    everything = range(inner)
    context, rows, send1, out_weight, had = attend(
        inner, cols, queries, cache_keys, cache_values, out_weight, query_positions, scale_table, had
    )
    other1 = swap_core(send1)
    away1 = tuple((0, s) for s in shifts)
    def phase_blocks(phase):
        return tuple((phase, s) for s in everything)

    def grid_blocks(work, after=()):
        return partials(inner, cols, work, context, out_weight, rows, had, after=after)

    blocks2 = ((0, 0),) + tuple((1, s) for s in shifts)
    keep1, keep2, *send2 = grid_blocks(
        ((True, away1), (True, blocks2), *((False, (block,)) for block in blocks2))
    )
    other2 = [swap_core(send) for send in send2]
    items1 = [[(0, s - 1, False, None), (1, s - 1, False, None)] for s in shifts]
    first = add_up(
        inner,
        [keep1, other1],
        [(items, UPPER) for items in items1] + [(items, LOWER) for items in items1],
        after=[keep2],
    )
    pay1, low1 = first[: len(shifts)], first[len(shifts) :]
    come1 = [shift_mid(pay, s) for s, pay in zip(shifts, pay1)]
    low_pairs = [swap_pairs(low) for low in low1]
    low_middle = [swap_middle(low) for low in low1]
    near_block = ((1, 0),)
    send2n, send3 = grid_blocks(((False, near_block), (False, phase_blocks(2))), pay1[:1])
    other2n, other3 = swap_core(send2n), swap_core(send3)
    send4, keep2n, keep3, keep4 = grid_blocks(
        (
            (False, phase_blocks(3)),
            (True, near_block),
            (True, phase_blocks(2)),
            (True, phase_blocks(3)),
        ),
        [send3],
    )
    other4 = swap_core(send4)

    def sums(arrays, outputs, after=()):
        names = list(arrays)
        items = [
            ([(names.index(name), *rest) for name, *rest in output], None) for output in outputs
        ]
        return add_up(inner, list(arrays.values()), items, after=after)

    def named(name, blocks):
        return {f"{name}_{s}": block for s, block in zip(shifts, blocks)}

    def added(names, half=None):
        return [(name, None, False, half) for name in names]

    own2 = {"keep2": keep2} | {f"other2_{i}": other for i, other in enumerate(other2)}
    own2n = {"keep2n": keep2n, "other2n": other2n}
    own3 = {"keep3": keep3, "other3": other3}
    own4 = {"keep4": keep4, "other4": other4}

    def part2(i):
        return [("keep2", i, False, None), (f"other2_{i}", 0, False, None)]

    def part(step, s):
        return [(f"keep{step}", s, False, None), (f"other{step}", s, False, None)]

    def passed(name, s):
        return [(f"{name}_{s}", None, True, LOWER)]

    def relayed(name):
        return [(name, None, True, None)]

    came1, from_pairs = named("came1", come1), named("pairs", low_pairs)
    from_middle = named("middle", low_middle)
    near1 = part2(0) + added(came1, UPPER)
    *pay2, end1 = sums(
        own2 | came1 | from_pairs,
        [*(part2(s) + passed("pairs", s) for s in shifts), near1],
        after=[*come1, send4],
    )
    came2 = named("came2", [shift_mid(pay, s) for s, pay in zip(shifts, pay2)])
    from_end1 = {"end1": swap_pairs(end1)}
    turned_residual, factors = turn_residual(inner, residual, rows, had, after=[end1])
    picked = select_rows(inner, next_query_weight, cols, after=[factors])
    next_other = [swap_core(part) for part in picked]

    near2 = part("2n", 0) + added(came2)
    *pay3, sum2 = sums(
        came2 | from_end1 | own2n | own3,
        [*(part(3, s) for s in shifts), near2 + relayed("end1")],
        after=[*picked[:1], *low_middle],
    )
    came3 = named("came3", [shift_mid(pay, s) for s, pay in zip(shifts, pay3)])
    from_end2 = {"end2": swap_pairs(sum2)}
    from_mid2 = {"mid2": swap_middle(sum2)}

    *pay4, near3, mid3 = sums(
        came3 | from_end2 | from_mid2 | own2 | own3 | own4 | came1 | from_middle,
        [
            *(part(4, s) + passed("middle", s) for s in shifts),
            part(3, 0) + added(came3) + relayed("mid2"),
            near1 + relayed("end2"),
        ],
    )
    come4 = [shift_mid(pay, s) for s, pay in zip(shifts, pay4)]
    from_mid3 = swap_middle(mid3)
    from_near3 = swap_pairs(near3)

    gain = norm_gain.astype(F32).reshape(-1, ROT)

    last = [*come4, from_near3, from_mid3, keep4, other4]
    items = [(None, False)] * (len(come4) + 1) + [(None, True)] + [(0, False)] * 2
    grid = regrid(inner, items, turned_residual, factors, last)

    x1 = [shift_mid(grid, s) for s in shifts]
    near = swap_pairs(grid)
    mid1 = swap_middle(grid)
    hidden_out, mark = hidden(inner, items, residual, factors, had, last, after=[grid])
    near, mid1, *low1 = gate([near, mid1], x1, after=[mark])
    x2 = [shift_mid(near, s) for s in shifts]
    ends2 = swap_pairs(mid1)
    mids2 = swap_middle(near)
    (third,) = choose(inner, mids2, ends2, after=x2)
    x3 = [shift_mid(third, s) for s in shifts]
    ends3 = swap_pairs(mids2)
    side_middle = [swap_middle(low) for low in low1]
    turned_next = turn_next(inner, next_query_weight, next_other, gain, rows, had, after=[third])
    fourth, *low3, up4 = choose(inner, mid1, ends3, x3, True, after=[turned_next])
    x4 = [shift_mid(up4, s) for s in shifts]
    side_pairs = [swap_pairs(low) for low in low3]
    acc = project(
        inner,
        turned_next,
        rows,
        None,
        [(0, 0, [grid]), (1, 0, [near]), (2, 0, [third]), (3, 0, [fourth])]
        + [(phase, s, [x[s - 1]]) for phase, x in enumerate((x1, x2, x3)) for s in shifts],
    )
    own, other = project(
        inner,
        turned_next,
        rows,
        acc,
        [(3, s, [x4[s - 1], side_middle[s - 1], side_pairs[s - 1]]) for s in shifts],
        split=True,
    )
    query_next = finish(own, swap_core(other), norm_gain.shape[0])
    return (hidden_out, query_next)


def solution(mesh):
    placed = (
        P("tp", "groups", None),
        P("tp", "groups", None),
        P("tp", "groups", None),
        P("groups"),
        P("tp", None),
        P("groups", "tp"),
        P(),
        P(),
        P(None, "tp"),
    )
    return jax.shard_map(
        functools.partial(body, mesh.shape["tp"]),
        mesh=mesh,
        in_specs=placed,
        out_specs=(P("groups", "tp"), P("groups", "tp")),
        check_vma=False,
    )
```

```python
import functools
import math

import jax
import jax.numpy as jnp
import numpy as np
from jax import lax
from jax.experimental import pallas as pl
from jax.experimental.pallas import tpu as pltpu
from jax.sharding import PartitionSpec as P

HD = 128
ROT = 128
OUTER = 4

F32 = jnp.float32
BF16 = jnp.bfloat16
MIB = 1024 * 1024


def hadamard(length):
    rows = np.arange(length)
    common = rows[:, None] & rows[None, :]
    parity = np.zeros((length, length), np.int64)
    for bit in range(length.bit_length()):
        parity += (common >> bit) & 1
    return (1 - 2 * (parity & 1)).astype(np.float32)


def vmem():
    return pl.BlockSpec(memory_space=pltpu.VMEM)


def anywhere():
    return pl.BlockSpec(memory_space=pl.ANY)


def place(inner):
    index = lax.axis_index("tp")
    return lax.div(index, 2 * inner), lax.rem(lax.div(index, 2), inner), lax.rem(index, 2)


def targets(outer):
    near = outer + 1 - 2 * lax.rem(outer, 2)
    return OUTER - 1 - outer, lax.rem(outer + 2, OUTER), near, outer


def is_inner(outer):
    return jnp.logical_or(outer == 1, outer == 2)


def kernel_call(kernel, out_shape, arrays, specs, after=(), scratch=(), aliases=None, limit=24, name=None):
    extra = len(after)

    def ordered(*refs):
        kernel(*refs[extra:])

    return pl.pallas_call(
        ordered,
        out_shape=out_shape,
        in_specs=[anywhere()] * extra + list(specs),
        out_specs=jax.tree.map(lambda _: vmem(), out_shape),
        scratch_shapes=list(scratch),
        input_output_aliases=aliases or {},
        cost_estimate=pl.CostEstimate(flops=0, bytes_accessed=0, transcendentals=0),
        compiler_params=pltpu.CompilerParams(vmem_limit_bytes=limit * MIB),
        name=name,
    )(*after, *arrays)


def gridded(context, h_ref, weight, scale_row, store):
    cols = weight.shape[1]
    count = cols // ROT
    value = jnp.dot(context, weight, preferred_element_type=F32).astype(BF16)
    stacked = jnp.concatenate([value[:, i * ROT : (i + 1) * ROT] for i in range(count)], axis=0)
    turned = jnp.dot(stacked, h_ref[...], preferred_element_type=F32)
    tok = value.shape[0]
    for i in range(count):
        part = turned[i * tok : (i + 1) * tok] * scale_row(i)
        store(i, jnp.clip(part, -127.0, 127.0).astype(BF16))


def attend_kernel(
    inner, cols, chunk, q_hbm, k_hbm, v_hbm, w_hbm, pos_hbm, table_hbm, h_hbm,
    ctx_ref, rows_ref, send_ref, w_ref, h_ref, k_ref, v_ref, s_ref, q_ref, pos_ref, table_ref, sems,
):
    tok = q_ref.shape[0]
    slots = k_ref.shape[0]
    steps = slots // chunk
    outer, mid, core = place(inner)
    dest = targets(outer)[0]

    copies = min(4, steps)
    per_copy = steps // copies
    size = slots // copies

    def copy_k(j):
        part = pl.ds(j * size, size)
        return pltpu.make_async_copy(k_hbm.at[0, part], k_ref.at[part], sems.at[1 + j])

    def copy_v(j):
        part = pl.ds(j * size, size)
        return pltpu.make_async_copy(v_hbm.at[0, part], v_ref.at[part], sems.at[1 + steps + j])

    def shard_of(shift):
        return (dest * inner + lax.rem(mid + shift, inner)) * 2 + 1 - core

    copy_w = pltpu.make_async_copy(w_hbm, w_ref, sems.at[2 * steps + 1])
    copy_q = pltpu.make_async_copy(q_hbm.at[0], q_ref, sems.at[0])
    copy_pos = pltpu.make_async_copy(pos_hbm, pos_ref, sems.at[2 * steps + 2])
    copy_table = pltpu.make_async_copy(table_hbm, table_ref, sems.at[2 * steps + 3])
    copy_h = pltpu.make_async_copy(h_hbm, h_ref, sems.at[2 * steps + 4])
    copy_q.start()
    copy_pos.start()
    for j in range(copies):
        copy_k(j).start()
    copy_table.start()
    copy_h.start()
    for j in range(copies):
        copy_v(j).start()
    copy_w.start()

    copy_pos.wait()
    positions = jnp.broadcast_to(pos_ref[...].astype(F32), (ROT, tok)).T
    ahead = positions.astype(jnp.int32) - lax.broadcasted_iota(jnp.int32, (tok, ROT), 1)

    copy_q.wait()
    queries = q_ref[...]
    peak = jnp.full((tok, ROT), -jnp.inf, F32)
    for j in range(steps):
        if j % per_copy == 0:
            copy_k(j // per_copy).wait()
        scores = lax.dot_general(
            queries, k_ref[j * chunk : (j + 1) * chunk], (((1,), (1,)), ((), ())),
            preferred_element_type=F32,
        )
        for i in range(chunk // ROT):
            base = j * chunk + i * ROT
            part = jnp.where(ahead >= base, scores[:, i * ROT : (i + 1) * ROT], -jnp.inf)
            s_ref[:, base : base + ROT] = part
            peak = jnp.maximum(peak, part)
    copy_table.wait()
    table = table_ref[...].astype(F32)
    count = table.shape[1]
    for i in range(2):
        rows_ref[i] = jnp.broadcast_to(table[i : i + 1], (ROT, count)).T
    largest = jnp.max(peak, axis=1, keepdims=True)
    factor = math.log2(math.e) / math.sqrt(HD)
    total = jnp.zeros((tok, ROT), F32)
    acc = jnp.zeros((tok, HD), F32)
    for j in range(copies):
        copy_v(j).wait()
    for j in range(steps):
        pieces = []
        for i in range(chunk // ROT):
            base = j * chunk + i * ROT
            raised = jnp.exp2((s_ref[:, base : base + ROT] - largest) * factor)
            total = total + raised
            pieces.append(raised.astype(BF16))
        acc = acc + jnp.dot(
            jnp.concatenate(pieces, axis=1), v_ref[j * chunk : (j + 1) * chunk],
            preferred_element_type=F32,
        )
    context = (acc / jnp.sum(total, axis=1, keepdims=True)).astype(BF16)
    ctx_ref[...] = context

    per = cols // ROT
    copy_h.wait()
    copy_w.wait()
    for shift in range(1, inner):
        first = shard_of(shift) * per
        start = pl.multiple_of(shard_of(shift) * cols, 128)

        def scale_row(i):
            return (65536.0 / math.sqrt(ROT)) / rows_ref[0, pl.ds(first + i, 1), :]

        def store(i, value):
            send_ref[shift - 1, :, i * ROT : (i + 1) * ROT] = value

        gridded(context, h_ref, w_ref[:, pl.ds(start, cols)], scale_row, store)


def attend(inner, cols, queries, keys, values, weight, positions, table, had):
    tok, slots = queries.shape[1], keys.shape[1]
    chunk = min(1024, slots)
    steps = slots // chunk
    blocks = table.shape[1]
    arrays = [queries, keys, values, weight, positions[None, :], table, had]
    return kernel_call(
        functools.partial(attend_kernel, inner, cols, chunk),
        [
            pltpu.VMEM((tok, HD), BF16),
            pltpu.VMEM((2, blocks, ROT), F32),
            pltpu.VMEM((inner - 1, tok, cols), BF16),
            pltpu.VMEM(weight.shape, BF16),
            pltpu.VMEM(had.shape, BF16),
        ],
        [pltpu.with_memory_space_constraint(array, pltpu.HBM) for array in arrays],
        [pl.BlockSpec(memory_space=pltpu.HBM)] * len(arrays),
        scratch=[
            pltpu.VMEM((slots, HD), BF16),
            pltpu.VMEM((slots, HD), BF16),
            pltpu.VMEM((tok, slots), F32),
            pltpu.VMEM((tok, HD), BF16),
            pltpu.VMEM((1, tok), positions.dtype),
            pltpu.VMEM(table.shape, table.dtype),
            pltpu.SemaphoreType.DMA((2 * steps + 5,)),
        ],
        limit=28,
        name="attend",
    )


def partial_kernel(inner, work, ctx_ref, w_ref, rows_ref, h_ref, *out_refs):
    cols = out_refs[0].shape[2]
    per = cols // ROT
    outer, mid, core = place(inner)
    dests = targets(outer)
    context = ctx_ref[...]
    for out_ref, (mine, blocks) in zip(out_refs, work):
        for at, (phase, shift) in enumerate(blocks):
            shard = (dests[phase] * inner + lax.rem(mid + shift, inner)) * 2
            shard = shard + (core if mine else 1 - core)

            def scale_row(i):
                return (65536.0 / math.sqrt(ROT)) / rows_ref[0, pl.ds(shard * per + i, 1), :]

            def store(i, value):
                out_ref[at, :, i * ROT : (i + 1) * ROT] = value

            start = pl.multiple_of(shard * cols, 128)
            gridded(context, h_ref, w_ref[:, pl.ds(start, cols)], scale_row, store)


def partials(inner, cols, work, context, weight, rows, had, after=()):
    tok = context.shape[0]
    count = sum(len(blocks) for _, blocks in work)
    return kernel_call(
        functools.partial(partial_kernel, inner, work),
        [jax.ShapeDtypeStruct((len(blocks), tok, cols), BF16) for _, blocks in work],
        [context, weight, rows, had],
        [vmem()] * 4,
        after=after,
        name="partials",
    )


UPPER, LOWER = 0, 1


def add_kernel(inner, inputs, outputs, *refs):
    ins, outs = refs[:inputs], refs[inputs:]
    outer = place(inner)[0]
    rows = ins[0].shape[-2] // 2
    for out_ref, (items, which_half) in zip(outs, outputs):
        for half in (UPPER, LOWER) if which_half is None else (which_half,):
            part = slice(half * rows, (half + 1) * rows)
            total = None
            for which, at, inner_only, item_half in items:
                if item_half is not None and item_half != half:
                    continue
                ref = ins[which] if at is None else ins[which].at[at]
                value = (ref[part] if item_half is None else ref[...]).astype(F32)
                if inner_only:
                    value = jnp.where(is_inner(outer), value, 0.0)
                total = value if total is None else total + value
            if which_half is None:
                out_ref[part] = total.astype(BF16)
            else:
                out_ref[...] = total.astype(BF16)


def add_up(inner, arrays, outputs, after=()):
    rows, cols = arrays[0].shape[-2:]
    shapes = [
        jax.ShapeDtypeStruct((rows if half is None else rows // 2, cols), BF16) for _, half in outputs
    ]
    return kernel_call(
        functools.partial(add_kernel, inner, len(arrays), outputs),
        shapes,
        arrays,
        [vmem()] * len(arrays),
        after=after,
        name="add_up",
    )


def turn_residual_kernel(inner, res_ref, rows_ref, h_ref, out_ref, factor_ref):
    per = res_ref.shape[1] // ROT
    first = lax.axis_index("tp") * per
    for i in range(per):
        part = slice(i * ROT, (i + 1) * ROT)
        high = 256.0 / rows_ref[1, pl.ds(first + i, 1), :]
        low = rows_ref[0, pl.ds(first + i, 1), :] * (1.0 / 65536.0)
        turned = jnp.dot(res_ref[:, part], h_ref[...], preferred_element_type=F32)
        out_ref[:, part] = turned * (high * (1.0 / math.sqrt(ROT)))
        factor_ref[0:1, part] = low * high
        factor_ref[1:2, part] = low


def turn_residual(inner, residual, rows, had, after=()):
    return kernel_call(
        functools.partial(turn_residual_kernel, inner),
        [
            jax.ShapeDtypeStruct(residual.shape, F32),
            jax.ShapeDtypeStruct((2, residual.shape[1]), F32),
        ],
        [residual, rows, had],
        [vmem()] * 3,
        after=after,
        name="turn_residual",
    )


def summed_at(inner, items, ins, part):
    outer = place(inner)[0]
    total = None
    for (at, inner_only), ref in zip(items, ins):
        value = (ref[:, part] if at is None else ref[at, :, part]).astype(F32)
        if inner_only:
            value = jnp.where(is_inner(outer), value, 0.0)
        total = value if total is None else total + value
    return total


def regrid_kernel(inner, items, *refs):
    *ins, turned_ref, factor_ref, grid_ref, mark_ref = refs
    mark_ref[...] = jnp.zeros_like(mark_ref)
    for i in range(turned_ref.shape[1] // ROT):
        part = slice(i * ROT, (i + 1) * ROT)
        value = turned_ref[:, part] + summed_at(inner, items, ins, part) * factor_ref[0:1, part]
        grid_ref[:, part] = jnp.clip(value, -127.0, 127.0).astype(BF16)


def regrid(inner, items, turned, factors, arrays, after=()):
    return kernel_call(
        functools.partial(regrid_kernel, inner, items),
        [jax.ShapeDtypeStruct(turned.shape, BF16), jax.ShapeDtypeStruct((8, ROT), F32)],
        [*arrays, turned, factors],
        [vmem()] * (2 + len(arrays)),
        after=after,
        name="regrid",
    )


def hidden_kernel(inner, items, res_ref, factor_ref, h_ref, *refs):
    *ins, out_ref, mark_ref = refs
    mark_ref[...] = jnp.zeros_like(mark_ref)
    for i in range(res_ref.shape[1] // ROT):
        part = slice(i * ROT, (i + 1) * ROT)
        value = summed_at(inner, items, ins, part) * factor_ref[1:2, part]
        upper = value.astype(BF16)
        lower = (value - upper.astype(F32)).astype(BF16)
        turned = jnp.dot(upper, h_ref[...], preferred_element_type=F32)
        turned = turned + jnp.dot(lower, h_ref[...], preferred_element_type=F32)
        stream = res_ref[:, part].astype(F32) + turned * (1.0 / math.sqrt(ROT))
        out_ref[:, part] = stream.astype(BF16)


def hidden(inner, items, residual, factors, had, arrays, after=()):
    return kernel_call(
        functools.partial(hidden_kernel, inner, items),
        [jax.ShapeDtypeStruct(residual.shape, BF16), jax.ShapeDtypeStruct((8, ROT), F32)],
        [residual, factors, had, *arrays],
        [vmem()] * (3 + len(arrays)),
        after=after,
        name="hidden",
    )


def choose_kernel(inner, count, *refs):
    inside = is_inner(place(inner)[0])
    inner_ref, end_ref, *refs = refs
    others, (out_ref, *outs) = refs[:count], refs[count:]
    lower, upper = outs[:count], outs[count:]

    def put(ref):
        out_ref[...] = ref[...]
        for half in upper:
            half[...] = ref[: half.shape[0]]

    @pl.when(inside)
    def _():
        put(inner_ref)

    @pl.when(jnp.logical_not(inside))
    def _():
        put(end_ref)

    for ref, half in zip(others, lower):
        half[...] = ref[half.shape[0] :]


def choose(inner, at_inner, at_end, others=(), halved=False, after=()):
    rows, cols = at_inner.shape
    half = jax.ShapeDtypeStruct((rows // 2, cols), BF16)
    return kernel_call(
        functools.partial(choose_kernel, inner, len(others)),
        [jax.ShapeDtypeStruct((rows, cols), BF16)] + [half] * (len(others) + halved),
        [at_inner, at_end, *others],
        [vmem()] * (2 + len(others)),
        after=after,
        name="choose",
    )


def gate_kernel(count, *refs):
    for ref, half in zip(refs[:count], refs[len(refs) - count :]):
        half[...] = ref[half.shape[0] :]


def gate(arrays, others, after):
    rows, cols = arrays[0].shape
    shapes = [jax.ShapeDtypeStruct((rows, cols), BF16)] * len(arrays)
    half = jax.ShapeDtypeStruct((rows // 2, cols), BF16)
    aliases = {len(after) + len(others) + i: i for i in range(len(arrays))}
    return kernel_call(
        functools.partial(gate_kernel, len(others)),
        shapes + [half] * len(others),
        [*others, *arrays],
        [vmem()] * (len(others) + len(arrays)),
        after=after,
        aliases=aliases,
        name="gate",
    )


def select_rows_kernel(inner, cols, w_ref, *out_refs):
    other = 1 - place(inner)[2]
    each = out_refs[0].shape[0]
    for j in range(each * len(out_refs)):
        start = pl.multiple_of((2 * j + other) * cols, 128)
        out_refs[j // each][j % each] = w_ref[pl.ds(start, cols), :]


def select_rows(inner, weight, cols, after=()):
    parts = 2
    each = OUTER * inner // parts
    return kernel_call(
        functools.partial(select_rows_kernel, inner, cols),
        [jax.ShapeDtypeStruct((each, cols, weight.shape[1]), weight.dtype)] * parts,
        [weight],
        [vmem()],
        after=after,
        name="select_rows",
    )


def turn_next_kernel(inner, cols, own_ref, gain_ref, rows_ref, h_ref, *refs):
    *other_refs, out_ref = refs
    each = other_refs[0].shape[0]
    core = place(inner)[2]
    for j in range(out_ref.shape[0]):
        shard = j * 2 + core
        for i in range(cols // ROT):
            block = shard * (cols // ROT) + i
            factor = rows_ref[1, pl.ds(block, 1), :] * (1.0 / (256.0 * math.sqrt(ROT)))
            rotation = (h_ref[...].astype(F32) * gain_ref[pl.ds(block, 1), :]).astype(BF16)
            part = slice(i * ROT, (i + 1) * ROT)
            own = own_ref[pl.ds(pl.multiple_of(block * ROT, ROT), ROT), :]
            for half, value in enumerate((own, other_refs[j // each][j % each, part, :])):
                turned = jnp.dot(rotation, value, preferred_element_type=F32)
                out_ref[j, part, half * HD : (half + 1) * HD] = (turned * factor).astype(BF16)


def turn_next(inner, weight, others, gain, rows, had, after=()):
    _, cols, width = others[0].shape
    return kernel_call(
        functools.partial(turn_next_kernel, inner, cols),
        jax.ShapeDtypeStruct((OUTER * inner, cols, 2 * width), BF16),
        [weight, gain, rows, had, *others],
        [vmem()] * (4 + len(others)),
        after=after,
        name="turn_next",
    )


def project_kernel(inner, places, has_acc, split, w_ref, rows_ref, *refs):
    outer, mid, core = place(inner)
    order = targets(outer)[::-1]
    acc_in = refs[0] if has_acc else None
    refs = refs[1:] if has_acc else refs
    count = sum(parts for _, _, parts in places)
    values_in = list(refs[:count])
    outs = refs[count:]
    cols, width = w_ref.shape[1:]
    acc = acc_in[:, :width] if has_acc else 0.0
    squares = acc_in[:, width:] if has_acc else 0.0
    for phase, shift, parts in places:
        block = order[phase] * inner + lax.rem(mid + inner - shift, inner)
        values = values_in.pop(0)[...]
        if parts == 3:
            at_inner, at_end = values_in.pop(0)[...], values_in.pop(0)[...]
            lower = jnp.where(is_inner(outer), at_inner, at_end)
            values = jnp.concatenate([values, lower], axis=0)
        acc = acc + jnp.dot(values, w_ref[block], preferred_element_type=F32)
        for i in range(cols // ROT):
            row = (block * 2 + core) * (cols // ROT) + i
            high = rows_ref[1, pl.ds(row, 1), :] * (1.0 / 256.0)
            value = values[:, i * ROT : (i + 1) * ROT].astype(F32) * high
            squares = squares + value * value
    if split:
        own_ref, other_ref = outs
        own_ref[:, :HD] = acc[:, :HD]
        own_ref[:, HD:] = squares
        other_ref[:, :HD] = acc[:, HD:]
        other_ref[:, HD:] = squares
    else:
        outs[0][:, :width] = acc
        outs[0][:, width:] = squares


def project(inner, weight, rows, acc, pieces, split=False, after=()):
    _, cols, width = weight.shape
    arrays = [part for _, _, parts in pieces for part in parts]
    first = pieces[0][2]
    tok = first[0].shape[0] * (1 if len(first) == 1 else 2)
    places = tuple((phase, shift, len(parts)) for phase, shift, parts in pieces)
    accs = [] if acc is None else [acc]
    if split:
        out = [jax.ShapeDtypeStruct((tok, HD + ROT), F32)] * 2
    else:
        out = jax.ShapeDtypeStruct((tok, width + ROT), F32)
    return kernel_call(
        functools.partial(project_kernel, inner, places, acc is not None, split),
        out,
        [weight, rows, *accs, *arrays],
        [vmem()] * (2 + len(accs) + len(arrays)),
        after=after,
        name="project",
    )


def finish_kernel(features, own_ref, other_ref, out_ref):
    squares = own_ref[:, HD:] + other_ref[:, HD:]
    mean = jnp.sum(squares, axis=1, keepdims=True) * (1.0 / features)
    value = (own_ref[:, :HD] + other_ref[:, :HD]) * lax.rsqrt(mean + 1e-05)
    out_ref[...] = value.astype(BF16)


def finish(own, other, features):
    tok = own.shape[0]
    return kernel_call(
        functools.partial(finish_kernel, features),
        jax.ShapeDtypeStruct((tok, HD), BF16),
        [own, other],
        [vmem()] * 2,
        name="finish",
    )


def body(
    size,
    queries,
    cache_keys,
    cache_values,
    query_positions,
    out_weight,
    residual,
    scale_table,
    norm_gain,
    next_query_weight,
):
    inner = size // (2 * OUTER)
    cols = residual.shape[1]
    had = jnp.asarray(hadamard(ROT), BF16)
    shifts = range(1, inner)

    def permute(value, move):
        moves = []
        for i in range(size):
            spot = move(i // (2 * inner), (i // 2) % inner, i % 2)
            moves.append((i, (spot[0] * inner + spot[1]) * 2 + spot[2]))
        return lax.ppermute(value, "tp", moves)

    def swap_core(value):
        return permute(value, lambda a, b, c: (a, b, 1 - c))

    def shift_mid(value, shift):
        return permute(value, lambda a, b, c: (a, (b + shift) % inner, c))

    def swap_pairs(value):
        return permute(value, lambda a, b, c: (a ^ 1, b, c))

    def swap_middle(value):
        return permute(value, lambda a, b, c: (a, b, 1 - c) if a in (0, 3) else (3 - a, b, c))

    everything = range(inner)
    context, rows, send1, out_weight, had = attend(
        inner, cols, queries, cache_keys, cache_values, out_weight, query_positions, scale_table, had
    )
    other1 = swap_core(send1)
    away1 = tuple((0, s) for s in shifts)
    def phase_blocks(phase):
        return tuple((phase, s) for s in everything)

    def grid_blocks(work, after=()):
        return partials(inner, cols, work, context, out_weight, rows, had, after=after)

    blocks2 = ((0, 0),) + tuple((1, s) for s in shifts)
    keep1, keep2, *send2 = grid_blocks(
        ((True, away1), (True, blocks2), *((False, (block,)) for block in blocks2))
    )
    other2 = [swap_core(send) for send in send2]
    items1 = [[(0, s - 1, False, None), (1, s - 1, False, None)] for s in shifts]
    first = add_up(
        inner,
        [keep1, other1],
        [(items, UPPER) for items in items1] + [(items, LOWER) for items in items1],
        after=[keep2],
    )
    pay1, low1 = first[: len(shifts)], first[len(shifts) :]
    come1 = [shift_mid(pay, s) for s, pay in zip(shifts, pay1)]
    low_pairs = [swap_pairs(low) for low in low1]
    low_middle = [swap_middle(low) for low in low1]
    near_block = ((1, 0),)
    send2n, send3 = grid_blocks(((False, near_block), (False, phase_blocks(2))), pay1[:1])
    other2n, other3 = swap_core(send2n), swap_core(send3)
    send4, keep2n, keep3, keep4 = grid_blocks(
        (
            (False, phase_blocks(3)),
            (True, near_block),
            (True, phase_blocks(2)),
            (True, phase_blocks(3)),
        ),
        [send3],
    )
    other4 = swap_core(send4)

    def sums(arrays, outputs, after=()):
        names = list(arrays)
        items = [
            ([(names.index(name), *rest) for name, *rest in output], None) for output in outputs
        ]
        return add_up(inner, list(arrays.values()), items, after=after)

    def named(name, blocks):
        return {f"{name}_{s}": block for s, block in zip(shifts, blocks)}

    def added(names, half=None):
        return [(name, None, False, half) for name in names]

    own2 = {"keep2": keep2} | {f"other2_{i}": other for i, other in enumerate(other2)}
    own2n = {"keep2n": keep2n, "other2n": other2n}
    own3 = {"keep3": keep3, "other3": other3}
    own4 = {"keep4": keep4, "other4": other4}

    def part2(i):
        return [("keep2", i, False, None), (f"other2_{i}", 0, False, None)]

    def part(step, s):
        return [(f"keep{step}", s, False, None), (f"other{step}", s, False, None)]

    def passed(name, s):
        return [(f"{name}_{s}", None, True, LOWER)]

    def relayed(name):
        return [(name, None, True, None)]

    came1, from_pairs = named("came1", come1), named("pairs", low_pairs)
    from_middle = named("middle", low_middle)
    near1 = part2(0) + added(came1, UPPER)
    *pay2, end1 = sums(
        own2 | came1 | from_pairs,
        [*(part2(s) + passed("pairs", s) for s in shifts), near1],
        after=[*come1, send4],
    )
    came2 = named("came2", [shift_mid(pay, s) for s, pay in zip(shifts, pay2)])
    from_end1 = {"end1": swap_pairs(end1)}
    turned_residual, factors = turn_residual(inner, residual, rows, had, after=[end1])
    picked = select_rows(inner, next_query_weight, cols, after=[factors])
    next_other = [swap_core(part) for part in picked]

    near2 = part("2n", 0) + added(came2)
    *pay3, sum2 = sums(
        came2 | from_end1 | own2n | own3,
        [*(part(3, s) for s in shifts), near2 + relayed("end1")],
        after=[*picked[:1], *low_middle],
    )
    came3 = named("came3", [shift_mid(pay, s) for s, pay in zip(shifts, pay3)])
    from_end2 = {"end2": swap_pairs(sum2)}
    from_mid2 = {"mid2": swap_middle(sum2)}

    *pay4, near3, mid3 = sums(
        came3 | from_end2 | from_mid2 | own2 | own3 | own4 | came1 | from_middle,
        [
            *(part(4, s) + passed("middle", s) for s in shifts),
            part(3, 0) + added(came3) + relayed("mid2"),
            near1 + relayed("end2"),
        ],
    )
    come4 = [shift_mid(pay, s) for s, pay in zip(shifts, pay4)]
    from_mid3 = swap_middle(mid3)
    from_near3 = swap_pairs(near3)

    gain = norm_gain.astype(F32).reshape(-1, ROT)

    last = [*come4, from_near3, from_mid3, keep4, other4]
    items = [(None, False)] * (len(come4) + 1) + [(None, True)] + [(0, False)] * 2
    grid, meet = regrid(inner, items, turned_residual, factors, last)
    (grid,) = gate([grid], [], after=[swap_core(meet)])

    x1 = [shift_mid(grid, s) for s in shifts]
    near = swap_pairs(grid)
    mid1 = swap_middle(grid)
    hidden_out, mark = hidden(inner, items, residual, factors, had, last, after=[grid])
    near, mid1, *low1 = gate([near, mid1], x1, after=[mark])
    x2 = [shift_mid(near, s) for s in shifts]
    ends2 = swap_pairs(mid1)
    mids2 = swap_middle(near)
    (third,) = choose(inner, mids2, ends2, after=x2)
    x3 = [shift_mid(third, s) for s in shifts]
    ends3 = swap_pairs(mids2)
    side_middle = [swap_middle(low) for low in low1]
    turned_next = turn_next(inner, next_query_weight, next_other, gain, rows, had, after=[third])
    fourth, *low3, up4 = choose(inner, mid1, ends3, x3, True, after=[turned_next])
    x4 = [shift_mid(up4, s) for s in shifts]
    side_pairs = [swap_pairs(low) for low in low3]
    acc = project(
        inner,
        turned_next,
        rows,
        None,
        [(0, 0, [grid]), (1, 0, [near]), (2, 0, [third]), (3, 0, [fourth])]
        + [(phase, s, [x[s - 1]]) for phase, x in enumerate((x1, x2, x3)) for s in shifts],
    )
    own, other = project(
        inner,
        turned_next,
        rows,
        acc,
        [(3, s, [x4[s - 1], side_middle[s - 1], side_pairs[s - 1]]) for s in shifts],
        split=True,
    )
    query_next = finish(own, swap_core(other), norm_gain.shape[0])
    return (hidden_out, query_next)


def solution(mesh):
    placed = (
        P("tp", "groups", None),
        P("tp", "groups", None),
        P("tp", "groups", None),
        P("groups"),
        P("tp", None),
        P("groups", "tp"),
        P(),
        P(),
        P(None, "tp"),
    )
    return jax.shard_map(
        functools.partial(body, mesh.shape["tp"]),
        mesh=mesh,
        in_specs=placed,
        out_specs=(P("groups", "tp"), P("groups", "tp")),
        check_vma=False,
    )
```

```python
import functools
import math

import jax
import jax.numpy as jnp
import numpy as np
from jax import lax
from jax.experimental import pallas as pl
from jax.experimental.pallas import tpu as pltpu
from jax.sharding import PartitionSpec as P

HD = 128
ROT = 128
OUTER = 4

F32 = jnp.float32
BF16 = jnp.bfloat16
MIB = 1024 * 1024


def hadamard(length):
    rows = np.arange(length)
    common = rows[:, None] & rows[None, :]
    parity = np.zeros((length, length), np.int64)
    for bit in range(length.bit_length()):
        parity += (common >> bit) & 1
    return (1 - 2 * (parity & 1)).astype(np.float32)


def vmem():
    return pl.BlockSpec(memory_space=pltpu.VMEM)


def anywhere():
    return pl.BlockSpec(memory_space=pl.ANY)


def place(inner):
    index = lax.axis_index("tp")
    return lax.div(index, 2 * inner), lax.rem(lax.div(index, 2), inner), lax.rem(index, 2)


def targets(outer):
    near = outer + 1 - 2 * lax.rem(outer, 2)
    return OUTER - 1 - outer, lax.rem(outer + 2, OUTER), near, outer


def is_inner(outer):
    return jnp.logical_or(outer == 1, outer == 2)


def kernel_call(kernel, out_shape, arrays, specs, after=(), scratch=(), aliases=None, limit=24, name=None):
    extra = len(after)

    def ordered(*refs):
        kernel(*refs[extra:])

    return pl.pallas_call(
        ordered,
        out_shape=out_shape,
        in_specs=[anywhere()] * extra + list(specs),
        out_specs=jax.tree.map(lambda _: vmem(), out_shape),
        scratch_shapes=list(scratch),
        input_output_aliases=aliases or {},
        cost_estimate=pl.CostEstimate(flops=0, bytes_accessed=0, transcendentals=0),
        compiler_params=pltpu.CompilerParams(vmem_limit_bytes=limit * MIB),
        name=name,
    )(*after, *arrays)


def gridded(context, h_ref, weight, scale_row, store):
    cols = weight.shape[1]
    count = cols // ROT
    value = jnp.dot(context, weight, preferred_element_type=F32).astype(BF16)
    stacked = jnp.concatenate([value[:, i * ROT : (i + 1) * ROT] for i in range(count)], axis=0)
    turned = jnp.dot(stacked, h_ref[...], preferred_element_type=F32)
    tok = value.shape[0]
    for i in range(count):
        part = turned[i * tok : (i + 1) * tok] * scale_row(i)
        store(i, jnp.clip(part, -127.0, 127.0).astype(BF16))


def attend_kernel(
    inner, cols, chunk, q_hbm, k_hbm, v_hbm, w_hbm, pos_hbm, table_hbm, h_hbm,
    ctx_ref, rows_ref, send_ref, w_ref, h_ref, k_ref, v_ref, s_ref, q_ref, pos_ref, table_ref, sems,
):
    tok = q_ref.shape[0]
    slots = k_ref.shape[0]
    steps = slots // chunk
    outer, mid, core = place(inner)
    dest = targets(outer)[0]

    copies = min(4, steps)
    per_copy = steps // copies
    size = slots // copies

    def copy_k(j):
        part = pl.ds(j * size, size)
        return pltpu.make_async_copy(k_hbm.at[0, part], k_ref.at[part], sems.at[1 + j])

    def copy_v(j):
        part = pl.ds(j * size, size)
        return pltpu.make_async_copy(v_hbm.at[0, part], v_ref.at[part], sems.at[1 + steps + j])

    def shard_of(shift):
        return (dest * inner + lax.rem(mid + shift, inner)) * 2 + 1 - core

    copy_w = pltpu.make_async_copy(w_hbm, w_ref, sems.at[2 * steps + 1])
    copy_q = pltpu.make_async_copy(q_hbm.at[0], q_ref, sems.at[0])
    copy_pos = pltpu.make_async_copy(pos_hbm, pos_ref, sems.at[2 * steps + 2])
    copy_table = pltpu.make_async_copy(table_hbm, table_ref, sems.at[2 * steps + 3])
    copy_h = pltpu.make_async_copy(h_hbm, h_ref, sems.at[2 * steps + 4])
    copy_q.start()
    copy_pos.start()
    for j in range(copies):
        copy_k(j).start()
    copy_table.start()
    copy_h.start()

    copy_pos.wait()
    positions = jnp.broadcast_to(pos_ref[...].astype(F32), (ROT, tok)).T
    ahead = positions.astype(jnp.int32) - lax.broadcasted_iota(jnp.int32, (tok, ROT), 1)

    copy_q.wait()
    queries = q_ref[...]
    peak = jnp.full((tok, ROT), -jnp.inf, F32)
    for j in range(steps):
        if j % per_copy == 0:
            copy_k(j // per_copy).wait()
        if j == 0:
            for i in range(copies):
                copy_v(i).start()
        if j == min(per_copy, steps - 1):
            copy_w.start()
        scores = lax.dot_general(
            queries, k_ref[j * chunk : (j + 1) * chunk], (((1,), (1,)), ((), ())),
            preferred_element_type=F32,
        )
        for i in range(chunk // ROT):
            base = j * chunk + i * ROT
            part = jnp.where(ahead >= base, scores[:, i * ROT : (i + 1) * ROT], -jnp.inf)
            s_ref[:, base : base + ROT] = part
            peak = jnp.maximum(peak, part)
    copy_table.wait()
    table = table_ref[...].astype(F32)
    count = table.shape[1]
    for i in range(2):
        rows_ref[i] = jnp.broadcast_to(table[i : i + 1], (ROT, count)).T
    largest = jnp.max(peak, axis=1, keepdims=True)
    factor = math.log2(math.e) / math.sqrt(HD)
    total = jnp.zeros((tok, ROT), F32)
    acc = jnp.zeros((tok, HD), F32)
    for j in range(copies):
        copy_v(j).wait()
    for j in range(steps):
        pieces = []
        for i in range(chunk // ROT):
            base = j * chunk + i * ROT
            raised = jnp.exp2((s_ref[:, base : base + ROT] - largest) * factor)
            total = total + raised
            pieces.append(raised.astype(BF16))
        acc = acc + jnp.dot(
            jnp.concatenate(pieces, axis=1), v_ref[j * chunk : (j + 1) * chunk],
            preferred_element_type=F32,
        )
    context = (acc / jnp.sum(total, axis=1, keepdims=True)).astype(BF16)
    ctx_ref[...] = context

    per = cols // ROT
    copy_h.wait()
    copy_w.wait()
    for shift in range(1, inner):
        first = shard_of(shift) * per
        start = pl.multiple_of(shard_of(shift) * cols, 128)

        def scale_row(i):
            return (65536.0 / math.sqrt(ROT)) / rows_ref[0, pl.ds(first + i, 1), :]

        def store(i, value):
            send_ref[shift - 1, :, i * ROT : (i + 1) * ROT] = value

        gridded(context, h_ref, w_ref[:, pl.ds(start, cols)], scale_row, store)


def attend(inner, cols, queries, keys, values, weight, positions, table, had):
    tok, slots = queries.shape[1], keys.shape[1]
    chunk = min(1024, slots)
    steps = slots // chunk
    blocks = table.shape[1]
    arrays = [queries, keys, values, weight, positions[None, :], table, had]
    return kernel_call(
        functools.partial(attend_kernel, inner, cols, chunk),
        [
            pltpu.VMEM((tok, HD), BF16),
            pltpu.VMEM((2, blocks, ROT), F32),
            pltpu.VMEM((inner - 1, tok, cols), BF16),
            pltpu.VMEM(weight.shape, BF16),
            pltpu.VMEM(had.shape, BF16),
        ],
        [pltpu.with_memory_space_constraint(array, pltpu.HBM) for array in arrays],
        [pl.BlockSpec(memory_space=pltpu.HBM)] * len(arrays),
        scratch=[
            pltpu.VMEM((slots, HD), BF16),
            pltpu.VMEM((slots, HD), BF16),
            pltpu.VMEM((tok, slots), F32),
            pltpu.VMEM((tok, HD), BF16),
            pltpu.VMEM((1, tok), positions.dtype),
            pltpu.VMEM(table.shape, table.dtype),
            pltpu.SemaphoreType.DMA((2 * steps + 5,)),
        ],
        limit=28,
        name="attend",
    )


def partial_kernel(inner, work, ctx_ref, w_ref, rows_ref, h_ref, *out_refs):
    cols = out_refs[0].shape[2]
    per = cols // ROT
    outer, mid, core = place(inner)
    dests = targets(outer)
    context = ctx_ref[...]
    for out_ref, (mine, blocks) in zip(out_refs, work):
        for at, (phase, shift) in enumerate(blocks):
            shard = (dests[phase] * inner + lax.rem(mid + shift, inner)) * 2
            shard = shard + (core if mine else 1 - core)

            def scale_row(i):
                return (65536.0 / math.sqrt(ROT)) / rows_ref[0, pl.ds(shard * per + i, 1), :]

            def store(i, value):
                out_ref[at, :, i * ROT : (i + 1) * ROT] = value

            start = pl.multiple_of(shard * cols, 128)
            gridded(context, h_ref, w_ref[:, pl.ds(start, cols)], scale_row, store)


def partials(inner, cols, work, context, weight, rows, had, after=()):
    tok = context.shape[0]
    count = sum(len(blocks) for _, blocks in work)
    return kernel_call(
        functools.partial(partial_kernel, inner, work),
        [jax.ShapeDtypeStruct((len(blocks), tok, cols), BF16) for _, blocks in work],
        [context, weight, rows, had],
        [vmem()] * 4,
        after=after,
        name="partials",
    )


UPPER, LOWER = 0, 1


def add_kernel(inner, inputs, outputs, *refs):
    ins, outs = refs[:inputs], refs[inputs:]
    outer = place(inner)[0]
    rows = ins[0].shape[-2] // 2
    for out_ref, (items, which_half) in zip(outs, outputs):
        for half in (UPPER, LOWER) if which_half is None else (which_half,):
            part = slice(half * rows, (half + 1) * rows)
            total = None
            for which, at, inner_only, item_half in items:
                if item_half is not None and item_half != half:
                    continue
                ref = ins[which] if at is None else ins[which].at[at]
                value = (ref[part] if item_half is None else ref[...]).astype(F32)
                if inner_only:
                    value = jnp.where(is_inner(outer), value, 0.0)
                total = value if total is None else total + value
            if which_half is None:
                out_ref[part] = total.astype(BF16)
            else:
                out_ref[...] = total.astype(BF16)


def add_up(inner, arrays, outputs, after=()):
    rows, cols = arrays[0].shape[-2:]
    shapes = [
        jax.ShapeDtypeStruct((rows if half is None else rows // 2, cols), BF16) for _, half in outputs
    ]
    return kernel_call(
        functools.partial(add_kernel, inner, len(arrays), outputs),
        shapes,
        arrays,
        [vmem()] * len(arrays),
        after=after,
        name="add_up",
    )


def turn_residual_kernel(inner, res_ref, rows_ref, h_ref, out_ref, factor_ref):
    per = res_ref.shape[1] // ROT
    first = lax.axis_index("tp") * per
    for i in range(per):
        part = slice(i * ROT, (i + 1) * ROT)
        high = 256.0 / rows_ref[1, pl.ds(first + i, 1), :]
        low = rows_ref[0, pl.ds(first + i, 1), :] * (1.0 / 65536.0)
        turned = jnp.dot(res_ref[:, part], h_ref[...], preferred_element_type=F32)
        out_ref[:, part] = turned * (high * (1.0 / math.sqrt(ROT)))
        factor_ref[0:1, part] = low * high
        factor_ref[1:2, part] = low


def turn_residual(inner, residual, rows, had, after=()):
    return kernel_call(
        functools.partial(turn_residual_kernel, inner),
        [
            jax.ShapeDtypeStruct(residual.shape, F32),
            jax.ShapeDtypeStruct((2, residual.shape[1]), F32),
        ],
        [residual, rows, had],
        [vmem()] * 3,
        after=after,
        name="turn_residual",
    )


def summed_at(inner, items, ins, part):
    outer = place(inner)[0]
    total = None
    for (at, inner_only), ref in zip(items, ins):
        value = (ref[:, part] if at is None else ref[at, :, part]).astype(F32)
        if inner_only:
            value = jnp.where(is_inner(outer), value, 0.0)
        total = value if total is None else total + value
    return total


def regrid_kernel(inner, items, *refs):
    *ins, turned_ref, factor_ref, grid_ref = refs
    for i in range(turned_ref.shape[1] // ROT):
        part = slice(i * ROT, (i + 1) * ROT)
        value = turned_ref[:, part] + summed_at(inner, items, ins, part) * factor_ref[0:1, part]
        grid_ref[:, part] = jnp.clip(value, -127.0, 127.0).astype(BF16)


def regrid(inner, items, turned, factors, arrays, after=()):
    return kernel_call(
        functools.partial(regrid_kernel, inner, items),
        jax.ShapeDtypeStruct(turned.shape, BF16),
        [*arrays, turned, factors],
        [vmem()] * (2 + len(arrays)),
        after=after,
        name="regrid",
    )


def hidden_kernel(inner, items, res_ref, factor_ref, h_ref, *refs):
    *ins, out_ref, mark_ref = refs
    mark_ref[...] = jnp.zeros_like(mark_ref)
    for i in range(res_ref.shape[1] // ROT):
        part = slice(i * ROT, (i + 1) * ROT)
        value = summed_at(inner, items, ins, part) * factor_ref[1:2, part]
        upper = value.astype(BF16)
        lower = (value - upper.astype(F32)).astype(BF16)
        turned = jnp.dot(upper, h_ref[...], preferred_element_type=F32)
        turned = turned + jnp.dot(lower, h_ref[...], preferred_element_type=F32)
        stream = res_ref[:, part].astype(F32) + turned * (1.0 / math.sqrt(ROT))
        out_ref[:, part] = stream.astype(BF16)


def hidden(inner, items, residual, factors, had, arrays, after=()):
    return kernel_call(
        functools.partial(hidden_kernel, inner, items),
        [jax.ShapeDtypeStruct(residual.shape, BF16), jax.ShapeDtypeStruct((8, ROT), F32)],
        [residual, factors, had, *arrays],
        [vmem()] * (3 + len(arrays)),
        after=after,
        name="hidden",
    )


def choose_kernel(inner, count, *refs):
    inside = is_inner(place(inner)[0])
    inner_ref, end_ref, *refs = refs
    others, (out_ref, *outs) = refs[:count], refs[count:]
    lower, upper = outs[:count], outs[count:]

    def put(ref):
        out_ref[...] = ref[...]
        for half in upper:
            half[...] = ref[: half.shape[0]]

    @pl.when(inside)
    def _():
        put(inner_ref)

    @pl.when(jnp.logical_not(inside))
    def _():
        put(end_ref)

    for ref, half in zip(others, lower):
        half[...] = ref[half.shape[0] :]


def choose(inner, at_inner, at_end, others=(), halved=False, after=()):
    rows, cols = at_inner.shape
    half = jax.ShapeDtypeStruct((rows // 2, cols), BF16)
    return kernel_call(
        functools.partial(choose_kernel, inner, len(others)),
        [jax.ShapeDtypeStruct((rows, cols), BF16)] + [half] * (len(others) + halved),
        [at_inner, at_end, *others],
        [vmem()] * (2 + len(others)),
        after=after,
        name="choose",
    )


def gate_kernel(count, *refs):
    for ref, half in zip(refs[:count], refs[-count:]):
        half[...] = ref[half.shape[0] :]


def gate(arrays, others, after):
    rows, cols = arrays[0].shape
    shapes = [jax.ShapeDtypeStruct((rows, cols), BF16)] * len(arrays)
    half = jax.ShapeDtypeStruct((rows // 2, cols), BF16)
    aliases = {len(after) + len(others) + i: i for i in range(len(arrays))}
    return kernel_call(
        functools.partial(gate_kernel, len(others)),
        shapes + [half] * len(others),
        [*others, *arrays],
        [vmem()] * (len(others) + len(arrays)),
        after=after,
        aliases=aliases,
        name="gate",
    )


def select_rows_kernel(inner, cols, w_ref, *out_refs):
    other = 1 - place(inner)[2]
    each = out_refs[0].shape[0]
    for j in range(each * len(out_refs)):
        start = pl.multiple_of((2 * j + other) * cols, 128)
        out_refs[j // each][j % each] = w_ref[pl.ds(start, cols), :]


def select_rows(inner, weight, cols, after=()):
    parts = 2
    each = OUTER * inner // parts
    return kernel_call(
        functools.partial(select_rows_kernel, inner, cols),
        [jax.ShapeDtypeStruct((each, cols, weight.shape[1]), weight.dtype)] * parts,
        [weight],
        [vmem()],
        after=after,
        name="select_rows",
    )


def turn_next_kernel(inner, cols, own_ref, gain_ref, rows_ref, h_ref, *refs):
    *other_refs, out_ref = refs
    each = other_refs[0].shape[0]
    core = place(inner)[2]
    for j in range(out_ref.shape[0]):
        shard = j * 2 + core
        for i in range(cols // ROT):
            block = shard * (cols // ROT) + i
            factor = rows_ref[1, pl.ds(block, 1), :] * (1.0 / (256.0 * math.sqrt(ROT)))
            rotation = (h_ref[...].astype(F32) * gain_ref[pl.ds(block, 1), :]).astype(BF16)
            part = slice(i * ROT, (i + 1) * ROT)
            own = own_ref[pl.ds(pl.multiple_of(block * ROT, ROT), ROT), :]
            for half, value in enumerate((own, other_refs[j // each][j % each, part, :])):
                turned = jnp.dot(rotation, value, preferred_element_type=F32)
                out_ref[j, part, half * HD : (half + 1) * HD] = (turned * factor).astype(BF16)


def turn_next(inner, weight, others, gain, rows, had, after=()):
    _, cols, width = others[0].shape
    return kernel_call(
        functools.partial(turn_next_kernel, inner, cols),
        jax.ShapeDtypeStruct((OUTER * inner, cols, 2 * width), BF16),
        [weight, gain, rows, had, *others],
        [vmem()] * (4 + len(others)),
        after=after,
        name="turn_next",
    )


def project_kernel(inner, places, has_acc, split, w_ref, rows_ref, *refs):
    outer, mid, core = place(inner)
    order = targets(outer)[::-1]
    acc_in = refs[0] if has_acc else None
    refs = refs[1:] if has_acc else refs
    count = sum(parts for _, _, parts in places)
    values_in = list(refs[:count])
    outs = refs[count:]
    cols, width = w_ref.shape[1:]
    acc = acc_in[:, :width] if has_acc else 0.0
    squares = acc_in[:, width:] if has_acc else 0.0
    for phase, shift, parts in places:
        block = order[phase] * inner + lax.rem(mid + inner - shift, inner)
        values = values_in.pop(0)[...]
        if parts == 3:
            at_inner, at_end = values_in.pop(0)[...], values_in.pop(0)[...]
            lower = jnp.where(is_inner(outer), at_inner, at_end)
            values = jnp.concatenate([values, lower], axis=0)
        acc = acc + jnp.dot(values, w_ref[block], preferred_element_type=F32)
        for i in range(cols // ROT):
            row = (block * 2 + core) * (cols // ROT) + i
            high = rows_ref[1, pl.ds(row, 1), :] * (1.0 / 256.0)
            value = values[:, i * ROT : (i + 1) * ROT].astype(F32) * high
            squares = squares + value * value
    if split:
        own_ref, other_ref = outs
        own_ref[:, :HD] = acc[:, :HD]
        own_ref[:, HD:] = squares
        other_ref[:, :HD] = acc[:, HD:]
        other_ref[:, HD:] = squares
    else:
        outs[0][:, :width] = acc
        outs[0][:, width:] = squares


def project(inner, weight, rows, acc, pieces, split=False, after=()):
    _, cols, width = weight.shape
    arrays = [part for _, _, parts in pieces for part in parts]
    first = pieces[0][2]
    tok = first[0].shape[0] * (1 if len(first) == 1 else 2)
    places = tuple((phase, shift, len(parts)) for phase, shift, parts in pieces)
    accs = [] if acc is None else [acc]
    if split:
        out = [jax.ShapeDtypeStruct((tok, HD + ROT), F32)] * 2
    else:
        out = jax.ShapeDtypeStruct((tok, width + ROT), F32)
    return kernel_call(
        functools.partial(project_kernel, inner, places, acc is not None, split),
        out,
        [weight, rows, *accs, *arrays],
        [vmem()] * (2 + len(accs) + len(arrays)),
        after=after,
        name="project",
    )


def finish_kernel(features, own_ref, other_ref, out_ref):
    squares = own_ref[:, HD:] + other_ref[:, HD:]
    mean = jnp.sum(squares, axis=1, keepdims=True) * (1.0 / features)
    value = (own_ref[:, :HD] + other_ref[:, :HD]) * lax.rsqrt(mean + 1e-05)
    out_ref[...] = value.astype(BF16)


def finish(own, other, features):
    tok = own.shape[0]
    return kernel_call(
        functools.partial(finish_kernel, features),
        jax.ShapeDtypeStruct((tok, HD), BF16),
        [own, other],
        [vmem()] * 2,
        name="finish",
    )


def body(
    size,
    queries,
    cache_keys,
    cache_values,
    query_positions,
    out_weight,
    residual,
    scale_table,
    norm_gain,
    next_query_weight,
):
    inner = size // (2 * OUTER)
    cols = residual.shape[1]
    had = jnp.asarray(hadamard(ROT), BF16)
    shifts = range(1, inner)

    def permute(value, move):
        moves = []
        for i in range(size):
            spot = move(i // (2 * inner), (i // 2) % inner, i % 2)
            moves.append((i, (spot[0] * inner + spot[1]) * 2 + spot[2]))
        return lax.ppermute(value, "tp", moves)

    def swap_core(value):
        return permute(value, lambda a, b, c: (a, b, 1 - c))

    def shift_mid(value, shift):
        return permute(value, lambda a, b, c: (a, (b + shift) % inner, c))

    def swap_pairs(value):
        return permute(value, lambda a, b, c: (a ^ 1, b, c))

    def swap_middle(value):
        return permute(value, lambda a, b, c: (a, b, 1 - c) if a in (0, 3) else (3 - a, b, c))

    everything = range(inner)
    context, rows, send1, out_weight, had = attend(
        inner, cols, queries, cache_keys, cache_values, out_weight, query_positions, scale_table, had
    )
    other1 = swap_core(send1)
    away1 = tuple((0, s) for s in shifts)
    def phase_blocks(phase):
        return tuple((phase, s) for s in everything)

    def grid_blocks(work, after=()):
        return partials(inner, cols, work, context, out_weight, rows, had, after=after)

    blocks2 = ((0, 0),) + tuple((1, s) for s in shifts)
    keep1, keep2, *send2 = grid_blocks(
        ((True, away1), (True, blocks2), *((False, (block,)) for block in blocks2))
    )
    other2 = [swap_core(send) for send in send2]
    items1 = [[(0, s - 1, False, None), (1, s - 1, False, None)] for s in shifts]
    first = add_up(
        inner,
        [keep1, other1],
        [(items, UPPER) for items in items1] + [(items, LOWER) for items in items1],
        after=[keep2],
    )
    pay1, low1 = first[: len(shifts)], first[len(shifts) :]
    come1 = [shift_mid(pay, s) for s, pay in zip(shifts, pay1)]
    low_pairs = [swap_pairs(low) for low in low1]
    low_middle = [swap_middle(low) for low in low1]
    near_block = ((1, 0),)
    send2n, send3 = grid_blocks(((False, near_block), (False, phase_blocks(2))), pay1[:1])
    other2n, other3 = swap_core(send2n), swap_core(send3)
    send4, keep2n, keep3, keep4 = grid_blocks(
        (
            (False, phase_blocks(3)),
            (True, near_block),
            (True, phase_blocks(2)),
            (True, phase_blocks(3)),
        ),
        [send3],
    )
    other4 = swap_core(send4)

    def sums(arrays, outputs, after=()):
        names = list(arrays)
        items = [
            ([(names.index(name), *rest) for name, *rest in output], None) for output in outputs
        ]
        return add_up(inner, list(arrays.values()), items, after=after)

    def named(name, blocks):
        return {f"{name}_{s}": block for s, block in zip(shifts, blocks)}

    def added(names, half=None):
        return [(name, None, False, half) for name in names]

    own2 = {"keep2": keep2} | {f"other2_{i}": other for i, other in enumerate(other2)}
    own2n = {"keep2n": keep2n, "other2n": other2n}
    own3 = {"keep3": keep3, "other3": other3}
    own4 = {"keep4": keep4, "other4": other4}

    def part2(i):
        return [("keep2", i, False, None), (f"other2_{i}", 0, False, None)]

    def part(step, s):
        return [(f"keep{step}", s, False, None), (f"other{step}", s, False, None)]

    def passed(name, s):
        return [(f"{name}_{s}", None, True, LOWER)]

    def relayed(name):
        return [(name, None, True, None)]

    came1, from_pairs = named("came1", come1), named("pairs", low_pairs)
    from_middle = named("middle", low_middle)
    near1 = part2(0) + added(came1, UPPER)
    *pay2, end1 = sums(
        own2 | came1 | from_pairs,
        [*(part2(s) + passed("pairs", s) for s in shifts), near1],
        after=[*come1, send4],
    )
    came2 = named("came2", [shift_mid(pay, s) for s, pay in zip(shifts, pay2)])
    from_end1 = {"end1": swap_pairs(end1)}
    turned_residual, factors = turn_residual(inner, residual, rows, had, after=[end1])
    picked = select_rows(inner, next_query_weight, cols, after=[factors])
    next_other = [swap_core(part) for part in picked]

    near2 = part("2n", 0) + added(came2)
    *pay3, sum2 = sums(
        came2 | from_end1 | own2n | own3,
        [*(part(3, s) for s in shifts), near2 + relayed("end1")],
        after=[*picked[:1], *low_middle],
    )
    came3 = named("came3", [shift_mid(pay, s) for s, pay in zip(shifts, pay3)])
    from_end2 = {"end2": swap_pairs(sum2)}
    from_mid2 = {"mid2": swap_middle(sum2)}

    *pay4, near3, mid3 = sums(
        came3 | from_end2 | from_mid2 | own2 | own3 | own4 | came1 | from_middle,
        [
            *(part(4, s) + passed("middle", s) for s in shifts),
            part(3, 0) + added(came3) + relayed("mid2"),
            near1 + relayed("end2"),
        ],
    )
    come4 = [shift_mid(pay, s) for s, pay in zip(shifts, pay4)]
    from_mid3 = swap_middle(mid3)
    from_near3 = swap_pairs(near3)

    gain = norm_gain.astype(F32).reshape(-1, ROT)

    last = [*come4, from_near3, from_mid3, keep4, other4]
    items = [(None, False)] * (len(come4) + 1) + [(None, True)] + [(0, False)] * 2
    grid = regrid(inner, items, turned_residual, factors, last)

    x1 = [shift_mid(grid, s) for s in shifts]
    near = swap_pairs(grid)
    mid1 = swap_middle(grid)
    hidden_out, mark = hidden(inner, items, residual, factors, had, last, after=[grid])
    near, mid1, *low1 = gate([near, mid1], x1, after=[mark])
    x2 = [shift_mid(near, s) for s in shifts]
    ends2 = swap_pairs(mid1)
    mids2 = swap_middle(near)
    (third,) = choose(inner, mids2, ends2, after=x2)
    x3 = [shift_mid(third, s) for s in shifts]
    ends3 = swap_pairs(mids2)
    side_middle = [swap_middle(low) for low in low1]
    turned_next = turn_next(inner, next_query_weight, next_other, gain, rows, had, after=[third])
    fourth, *low3, up4 = choose(inner, mid1, ends3, x3, True, after=[turned_next])
    x4 = [shift_mid(up4, s) for s in shifts]
    side_pairs = [swap_pairs(low) for low in low3]
    acc = project(
        inner,
        turned_next,
        rows,
        None,
        [(0, 0, [grid]), (1, 0, [near]), (2, 0, [third]), (3, 0, [fourth])]
        + [(phase, s, [x[s - 1]]) for phase, x in enumerate((x1, x2, x3)) for s in shifts],
    )
    own, other = project(
        inner,
        turned_next,
        rows,
        acc,
        [(3, s, [x4[s - 1], side_middle[s - 1], side_pairs[s - 1]]) for s in shifts],
        split=True,
    )
    query_next = finish(own, swap_core(other), norm_gain.shape[0])
    return (hidden_out, query_next)


def solution(mesh):
    placed = (
        P("tp", "groups", None),
        P("tp", "groups", None),
        P("tp", "groups", None),
        P("groups"),
        P("tp", None),
        P("groups", "tp"),
        P(),
        P(),
        P(None, "tp"),
    )
    return jax.shard_map(
        functools.partial(body, mesh.shape["tp"]),
        mesh=mesh,
        in_specs=placed,
        out_specs=(P("groups", "tp"), P("groups", "tp")),
        check_vma=False,
    )
```

```python
import functools
import math

import jax
import jax.numpy as jnp
import numpy as np
from jax import lax
from jax.experimental import pallas as pl
from jax.experimental.pallas import tpu as pltpu
from jax.sharding import PartitionSpec as P

HD = 128
ROT = 128
OUTER = 4

F32 = jnp.float32
BF16 = jnp.bfloat16
MIB = 1024 * 1024


def hadamard(length):
    rows = np.arange(length)
    common = rows[:, None] & rows[None, :]
    parity = np.zeros((length, length), np.int64)
    for bit in range(length.bit_length()):
        parity += (common >> bit) & 1
    return (1 - 2 * (parity & 1)).astype(np.float32)


def vmem():
    return pl.BlockSpec(memory_space=pltpu.VMEM)


def anywhere():
    return pl.BlockSpec(memory_space=pl.ANY)


def place(inner):
    index = lax.axis_index("tp")
    return lax.div(index, 2 * inner), lax.rem(lax.div(index, 2), inner), lax.rem(index, 2)


def targets(outer):
    near = outer + 1 - 2 * lax.rem(outer, 2)
    return OUTER - 1 - outer, lax.rem(outer + 2, OUTER), near, outer


def is_inner(outer):
    return jnp.logical_or(outer == 1, outer == 2)


def kernel_call(kernel, out_shape, arrays, specs, after=(), scratch=(), aliases=None, limit=24, name=None):
    extra = len(after)

    def ordered(*refs):
        kernel(*refs[extra:])

    return pl.pallas_call(
        ordered,
        out_shape=out_shape,
        in_specs=[anywhere()] * extra + list(specs),
        out_specs=jax.tree.map(lambda _: vmem(), out_shape),
        scratch_shapes=list(scratch),
        input_output_aliases=aliases or {},
        cost_estimate=pl.CostEstimate(flops=0, bytes_accessed=0, transcendentals=0),
        compiler_params=pltpu.CompilerParams(vmem_limit_bytes=limit * MIB),
        name=name,
    )(*after, *arrays)


def gridded(context, h_ref, weight, scale_row, store):
    cols = weight.shape[1]
    count = cols // ROT
    value = jnp.dot(context, weight, preferred_element_type=F32).astype(BF16)
    stacked = jnp.concatenate([value[:, i * ROT : (i + 1) * ROT] for i in range(count)], axis=0)
    turned = jnp.dot(stacked, h_ref[...], preferred_element_type=F32)
    tok = value.shape[0]
    for i in range(count):
        part = turned[i * tok : (i + 1) * tok] * scale_row(i)
        store(i, jnp.clip(part, -127.0, 127.0).astype(BF16))


def attend_kernel(
    inner, cols, chunk, q_hbm, k_hbm, v_hbm, w_hbm, pos_hbm, table_hbm, h_hbm,
    ctx_ref, rows_ref, send_ref, w_ref, h_ref, k_ref, v_ref, s_ref, q_ref, pos_ref, table_ref, sems,
):
    tok = q_ref.shape[0]
    slots = k_ref.shape[0]
    steps = slots // chunk
    outer, mid, core = place(inner)
    dest = targets(outer)[0]

    copies = min(2, steps)
    per_copy = steps // copies
    size = slots // copies

    def copy_k(j):
        part = pl.ds(j * size, size)
        return pltpu.make_async_copy(k_hbm.at[0, part], k_ref.at[part], sems.at[1 + j])

    def copy_v(j):
        part = pl.ds(j * size, size)
        return pltpu.make_async_copy(v_hbm.at[0, part], v_ref.at[part], sems.at[1 + steps + j])

    def shard_of(shift):
        return (dest * inner + lax.rem(mid + shift, inner)) * 2 + 1 - core

    copy_w = pltpu.make_async_copy(w_hbm, w_ref, sems.at[2 * steps + 1])
    copy_q = pltpu.make_async_copy(q_hbm.at[0], q_ref, sems.at[0])
    copy_pos = pltpu.make_async_copy(pos_hbm, pos_ref, sems.at[2 * steps + 2])
    copy_table = pltpu.make_async_copy(table_hbm, table_ref, sems.at[2 * steps + 3])
    copy_h = pltpu.make_async_copy(h_hbm, h_ref, sems.at[2 * steps + 4])
    copy_q.start()
    copy_pos.start()
    for j in range(copies):
        copy_k(j).start()
    copy_table.start()
    copy_h.start()
    for j in range(copies):
        copy_v(j).start()
    copy_w.start()

    copy_pos.wait()
    positions = jnp.broadcast_to(pos_ref[...].astype(F32), (ROT, tok)).T
    ahead = positions.astype(jnp.int32) - lax.broadcasted_iota(jnp.int32, (tok, ROT), 1)

    copy_q.wait()
    queries = q_ref[...]
    peak = jnp.full((tok, ROT), -jnp.inf, F32)
    for j in range(steps):
        if j % per_copy == 0:
            copy_k(j // per_copy).wait()
        scores = lax.dot_general(
            queries, k_ref[j * chunk : (j + 1) * chunk], (((1,), (1,)), ((), ())),
            preferred_element_type=F32,
        )
        for i in range(chunk // ROT):
            base = j * chunk + i * ROT
            part = jnp.where(ahead >= base, scores[:, i * ROT : (i + 1) * ROT], -jnp.inf)
            s_ref[:, base : base + ROT] = part
            peak = jnp.maximum(peak, part)
    copy_table.wait()
    table = table_ref[...].astype(F32)
    count = table.shape[1]
    for i in range(2):
        rows_ref[i] = jnp.broadcast_to(table[i : i + 1], (ROT, count)).T
    largest = jnp.max(peak, axis=1, keepdims=True)
    factor = math.log2(math.e) / math.sqrt(HD)
    total = jnp.zeros((tok, ROT), F32)
    acc = jnp.zeros((tok, HD), F32)
    for j in range(copies):
        copy_v(j).wait()
    for j in range(steps):
        pieces = []
        for i in range(chunk // ROT):
            base = j * chunk + i * ROT
            raised = jnp.exp2((s_ref[:, base : base + ROT] - largest) * factor)
            total = total + raised
            pieces.append(raised.astype(BF16))
        acc = acc + jnp.dot(
            jnp.concatenate(pieces, axis=1), v_ref[j * chunk : (j + 1) * chunk],
            preferred_element_type=F32,
        )
    context = (acc / jnp.sum(total, axis=1, keepdims=True)).astype(BF16)
    ctx_ref[...] = context

    per = cols // ROT
    copy_h.wait()
    copy_w.wait()
    for shift in range(1, inner):
        first = shard_of(shift) * per
        start = pl.multiple_of(shard_of(shift) * cols, 128)

        def scale_row(i):
            return (65536.0 / math.sqrt(ROT)) / rows_ref[0, pl.ds(first + i, 1), :]

        def store(i, value):
            send_ref[shift - 1, :, i * ROT : (i + 1) * ROT] = value

        gridded(context, h_ref, w_ref[:, pl.ds(start, cols)], scale_row, store)


def attend(inner, cols, queries, keys, values, weight, positions, table, had):
    tok, slots = queries.shape[1], keys.shape[1]
    chunk = min(1024, slots)
    steps = slots // chunk
    blocks = table.shape[1]
    arrays = [queries, keys, values, weight, positions[None, :], table, had]
    return kernel_call(
        functools.partial(attend_kernel, inner, cols, chunk),
        [
            pltpu.VMEM((tok, HD), BF16),
            pltpu.VMEM((2, blocks, ROT), F32),
            pltpu.VMEM((inner - 1, tok, cols), BF16),
            pltpu.VMEM(weight.shape, BF16),
            pltpu.VMEM(had.shape, BF16),
        ],
        [pltpu.with_memory_space_constraint(array, pltpu.HBM) for array in arrays],
        [pl.BlockSpec(memory_space=pltpu.HBM)] * len(arrays),
        scratch=[
            pltpu.VMEM((slots, HD), BF16),
            pltpu.VMEM((slots, HD), BF16),
            pltpu.VMEM((tok, slots), F32),
            pltpu.VMEM((tok, HD), BF16),
            pltpu.VMEM((1, tok), positions.dtype),
            pltpu.VMEM(table.shape, table.dtype),
            pltpu.SemaphoreType.DMA((2 * steps + 5,)),
        ],
        limit=28,
        name="attend",
    )


def partial_kernel(inner, work, ctx_ref, w_ref, rows_ref, h_ref, *out_refs):
    cols = out_refs[0].shape[2]
    per = cols // ROT
    outer, mid, core = place(inner)
    dests = targets(outer)
    context = ctx_ref[...]
    for out_ref, (mine, blocks) in zip(out_refs, work):
        for at, (phase, shift) in enumerate(blocks):
            shard = (dests[phase] * inner + lax.rem(mid + shift, inner)) * 2
            shard = shard + (core if mine else 1 - core)

            def scale_row(i):
                return (65536.0 / math.sqrt(ROT)) / rows_ref[0, pl.ds(shard * per + i, 1), :]

            def store(i, value):
                out_ref[at, :, i * ROT : (i + 1) * ROT] = value

            start = pl.multiple_of(shard * cols, 128)
            gridded(context, h_ref, w_ref[:, pl.ds(start, cols)], scale_row, store)


def partials(inner, cols, work, context, weight, rows, had, after=()):
    tok = context.shape[0]
    count = sum(len(blocks) for _, blocks in work)
    return kernel_call(
        functools.partial(partial_kernel, inner, work),
        [jax.ShapeDtypeStruct((len(blocks), tok, cols), BF16) for _, blocks in work],
        [context, weight, rows, had],
        [vmem()] * 4,
        after=after,
        name="partials",
    )


UPPER, LOWER = 0, 1


def add_kernel(inner, inputs, outputs, *refs):
    ins, outs = refs[:inputs], refs[inputs:]
    outer = place(inner)[0]
    rows = ins[0].shape[-2] // 2
    for out_ref, (items, which_half) in zip(outs, outputs):
        for half in (UPPER, LOWER) if which_half is None else (which_half,):
            part = slice(half * rows, (half + 1) * rows)
            total = None
            for which, at, inner_only, item_half in items:
                if item_half is not None and item_half != half:
                    continue
                ref = ins[which] if at is None else ins[which].at[at]
                value = (ref[part] if item_half is None else ref[...]).astype(F32)
                if inner_only:
                    value = jnp.where(is_inner(outer), value, 0.0)
                total = value if total is None else total + value
            if which_half is None:
                out_ref[part] = total.astype(BF16)
            else:
                out_ref[...] = total.astype(BF16)


def add_up(inner, arrays, outputs, after=()):
    rows, cols = arrays[0].shape[-2:]
    shapes = [
        jax.ShapeDtypeStruct((rows if half is None else rows // 2, cols), BF16) for _, half in outputs
    ]
    return kernel_call(
        functools.partial(add_kernel, inner, len(arrays), outputs),
        shapes,
        arrays,
        [vmem()] * len(arrays),
        after=after,
        name="add_up",
    )


def turn_residual_kernel(inner, res_ref, rows_ref, h_ref, out_ref, factor_ref):
    per = res_ref.shape[1] // ROT
    first = lax.axis_index("tp") * per
    for i in range(per):
        part = slice(i * ROT, (i + 1) * ROT)
        high = 256.0 / rows_ref[1, pl.ds(first + i, 1), :]
        low = rows_ref[0, pl.ds(first + i, 1), :] * (1.0 / 65536.0)
        turned = jnp.dot(res_ref[:, part], h_ref[...], preferred_element_type=F32)
        out_ref[:, part] = turned * (high * (1.0 / math.sqrt(ROT)))
        factor_ref[0:1, part] = low * high
        factor_ref[1:2, part] = low


def turn_residual(inner, residual, rows, had, after=()):
    return kernel_call(
        functools.partial(turn_residual_kernel, inner),
        [
            jax.ShapeDtypeStruct(residual.shape, F32),
            jax.ShapeDtypeStruct((2, residual.shape[1]), F32),
        ],
        [residual, rows, had],
        [vmem()] * 3,
        after=after,
        name="turn_residual",
    )


def summed_at(inner, items, ins, part):
    outer = place(inner)[0]
    total = None
    for (at, inner_only), ref in zip(items, ins):
        value = (ref[:, part] if at is None else ref[at, :, part]).astype(F32)
        if inner_only:
            value = jnp.where(is_inner(outer), value, 0.0)
        total = value if total is None else total + value
    return total


def regrid_kernel(inner, items, *refs):
    *ins, turned_ref, factor_ref, grid_ref = refs
    for i in range(turned_ref.shape[1] // ROT):
        part = slice(i * ROT, (i + 1) * ROT)
        value = turned_ref[:, part] + summed_at(inner, items, ins, part) * factor_ref[0:1, part]
        grid_ref[:, part] = jnp.clip(value, -127.0, 127.0).astype(BF16)


def regrid(inner, items, turned, factors, arrays, after=()):
    return kernel_call(
        functools.partial(regrid_kernel, inner, items),
        jax.ShapeDtypeStruct(turned.shape, BF16),
        [*arrays, turned, factors],
        [vmem()] * (2 + len(arrays)),
        after=after,
        name="regrid",
    )


def hidden_kernel(inner, items, res_ref, factor_ref, h_ref, *refs):
    *ins, out_ref, mark_ref = refs
    mark_ref[...] = jnp.zeros_like(mark_ref)
    for i in range(res_ref.shape[1] // ROT):
        part = slice(i * ROT, (i + 1) * ROT)
        value = summed_at(inner, items, ins, part) * factor_ref[1:2, part]
        upper = value.astype(BF16)
        lower = (value - upper.astype(F32)).astype(BF16)
        turned = jnp.dot(upper, h_ref[...], preferred_element_type=F32)
        turned = turned + jnp.dot(lower, h_ref[...], preferred_element_type=F32)
        stream = res_ref[:, part].astype(F32) + turned * (1.0 / math.sqrt(ROT))
        out_ref[:, part] = stream.astype(BF16)


def hidden(inner, items, residual, factors, had, arrays, after=()):
    return kernel_call(
        functools.partial(hidden_kernel, inner, items),
        [jax.ShapeDtypeStruct(residual.shape, BF16), jax.ShapeDtypeStruct((8, ROT), F32)],
        [residual, factors, had, *arrays],
        [vmem()] * (3 + len(arrays)),
        after=after,
        name="hidden",
    )


def choose_kernel(inner, count, *refs):
    inside = is_inner(place(inner)[0])
    inner_ref, end_ref, *refs = refs
    others, (out_ref, *outs) = refs[:count], refs[count:]
    lower, upper = outs[:count], outs[count:]

    def put(ref):
        out_ref[...] = ref[...]
        for half in upper:
            half[...] = ref[: half.shape[0]]

    @pl.when(inside)
    def _():
        put(inner_ref)

    @pl.when(jnp.logical_not(inside))
    def _():
        put(end_ref)

    for ref, half in zip(others, lower):
        half[...] = ref[half.shape[0] :]


def choose(inner, at_inner, at_end, others=(), halved=False, after=()):
    rows, cols = at_inner.shape
    half = jax.ShapeDtypeStruct((rows // 2, cols), BF16)
    return kernel_call(
        functools.partial(choose_kernel, inner, len(others)),
        [jax.ShapeDtypeStruct((rows, cols), BF16)] + [half] * (len(others) + halved),
        [at_inner, at_end, *others],
        [vmem()] * (2 + len(others)),
        after=after,
        name="choose",
    )


def gate_kernel(count, *refs):
    for ref, half in zip(refs[:count], refs[-count:]):
        half[...] = ref[half.shape[0] :]


def gate(arrays, others, after):
    rows, cols = arrays[0].shape
    shapes = [jax.ShapeDtypeStruct((rows, cols), BF16)] * len(arrays)
    half = jax.ShapeDtypeStruct((rows // 2, cols), BF16)
    aliases = {len(after) + len(others) + i: i for i in range(len(arrays))}
    return kernel_call(
        functools.partial(gate_kernel, len(others)),
        shapes + [half] * len(others),
        [*others, *arrays],
        [vmem()] * (len(others) + len(arrays)),
        after=after,
        aliases=aliases,
        name="gate",
    )


def select_rows_kernel(inner, cols, w_ref, *out_refs):
    other = 1 - place(inner)[2]
    each = out_refs[0].shape[0]
    for j in range(each * len(out_refs)):
        start = pl.multiple_of((2 * j + other) * cols, 128)
        out_refs[j // each][j % each] = w_ref[pl.ds(start, cols), :]


def select_rows(inner, weight, cols, after=()):
    parts = 2
    each = OUTER * inner // parts
    return kernel_call(
        functools.partial(select_rows_kernel, inner, cols),
        [jax.ShapeDtypeStruct((each, cols, weight.shape[1]), weight.dtype)] * parts,
        [weight],
        [vmem()],
        after=after,
        name="select_rows",
    )


def turn_next_kernel(inner, cols, own_ref, gain_ref, rows_ref, h_ref, *refs):
    *other_refs, out_ref = refs
    each = other_refs[0].shape[0]
    core = place(inner)[2]
    for j in range(out_ref.shape[0]):
        shard = j * 2 + core
        for i in range(cols // ROT):
            block = shard * (cols // ROT) + i
            factor = rows_ref[1, pl.ds(block, 1), :] * (1.0 / (256.0 * math.sqrt(ROT)))
            rotation = (h_ref[...].astype(F32) * gain_ref[pl.ds(block, 1), :]).astype(BF16)
            part = slice(i * ROT, (i + 1) * ROT)
            own = own_ref[pl.ds(pl.multiple_of(block * ROT, ROT), ROT), :]
            for half, value in enumerate((own, other_refs[j // each][j % each, part, :])):
                turned = jnp.dot(rotation, value, preferred_element_type=F32)
                out_ref[j, part, half * HD : (half + 1) * HD] = (turned * factor).astype(BF16)


def turn_next(inner, weight, others, gain, rows, had, after=()):
    _, cols, width = others[0].shape
    return kernel_call(
        functools.partial(turn_next_kernel, inner, cols),
        jax.ShapeDtypeStruct((OUTER * inner, cols, 2 * width), BF16),
        [weight, gain, rows, had, *others],
        [vmem()] * (4 + len(others)),
        after=after,
        name="turn_next",
    )


def project_kernel(inner, places, has_acc, split, w_ref, rows_ref, *refs):
    outer, mid, core = place(inner)
    order = targets(outer)[::-1]
    acc_in = refs[0] if has_acc else None
    refs = refs[1:] if has_acc else refs
    count = sum(parts for _, _, parts in places)
    values_in = list(refs[:count])
    outs = refs[count:]
    cols, width = w_ref.shape[1:]
    acc = acc_in[:, :width] if has_acc else 0.0
    squares = acc_in[:, width:] if has_acc else 0.0
    for phase, shift, parts in places:
        block = order[phase] * inner + lax.rem(mid + inner - shift, inner)
        values = values_in.pop(0)[...]
        if parts == 3:
            at_inner, at_end = values_in.pop(0)[...], values_in.pop(0)[...]
            lower = jnp.where(is_inner(outer), at_inner, at_end)
            values = jnp.concatenate([values, lower], axis=0)
        acc = acc + jnp.dot(values, w_ref[block], preferred_element_type=F32)
        for i in range(cols // ROT):
            row = (block * 2 + core) * (cols // ROT) + i
            high = rows_ref[1, pl.ds(row, 1), :] * (1.0 / 256.0)
            value = values[:, i * ROT : (i + 1) * ROT].astype(F32) * high
            squares = squares + value * value
    if split:
        own_ref, other_ref = outs
        own_ref[:, :HD] = acc[:, :HD]
        own_ref[:, HD:] = squares
        other_ref[:, :HD] = acc[:, HD:]
        other_ref[:, HD:] = squares
    else:
        outs[0][:, :width] = acc
        outs[0][:, width:] = squares


def project(inner, weight, rows, acc, pieces, split=False, after=()):
    _, cols, width = weight.shape
    arrays = [part for _, _, parts in pieces for part in parts]
    first = pieces[0][2]
    tok = first[0].shape[0] * (1 if len(first) == 1 else 2)
    places = tuple((phase, shift, len(parts)) for phase, shift, parts in pieces)
    accs = [] if acc is None else [acc]
    if split:
        out = [jax.ShapeDtypeStruct((tok, HD + ROT), F32)] * 2
    else:
        out = jax.ShapeDtypeStruct((tok, width + ROT), F32)
    return kernel_call(
        functools.partial(project_kernel, inner, places, acc is not None, split),
        out,
        [weight, rows, *accs, *arrays],
        [vmem()] * (2 + len(accs) + len(arrays)),
        after=after,
        name="project",
    )


def finish_kernel(features, own_ref, other_ref, out_ref):
    squares = own_ref[:, HD:] + other_ref[:, HD:]
    mean = jnp.sum(squares, axis=1, keepdims=True) * (1.0 / features)
    value = (own_ref[:, :HD] + other_ref[:, :HD]) * lax.rsqrt(mean + 1e-05)
    out_ref[...] = value.astype(BF16)


def finish(own, other, features):
    tok = own.shape[0]
    return kernel_call(
        functools.partial(finish_kernel, features),
        jax.ShapeDtypeStruct((tok, HD), BF16),
        [own, other],
        [vmem()] * 2,
        name="finish",
    )


def body(
    size,
    queries,
    cache_keys,
    cache_values,
    query_positions,
    out_weight,
    residual,
    scale_table,
    norm_gain,
    next_query_weight,
):
    inner = size // (2 * OUTER)
    cols = residual.shape[1]
    had = jnp.asarray(hadamard(ROT), BF16)
    shifts = range(1, inner)

    def permute(value, move):
        moves = []
        for i in range(size):
            spot = move(i // (2 * inner), (i // 2) % inner, i % 2)
            moves.append((i, (spot[0] * inner + spot[1]) * 2 + spot[2]))
        return lax.ppermute(value, "tp", moves)

    def swap_core(value):
        return permute(value, lambda a, b, c: (a, b, 1 - c))

    def shift_mid(value, shift):
        return permute(value, lambda a, b, c: (a, (b + shift) % inner, c))

    def swap_pairs(value):
        return permute(value, lambda a, b, c: (a ^ 1, b, c))

    def swap_middle(value):
        return permute(value, lambda a, b, c: (a, b, 1 - c) if a in (0, 3) else (3 - a, b, c))

    everything = range(inner)
    context, rows, send1, out_weight, had = attend(
        inner, cols, queries, cache_keys, cache_values, out_weight, query_positions, scale_table, had
    )
    other1 = swap_core(send1)
    away1 = tuple((0, s) for s in shifts)
    def phase_blocks(phase):
        return tuple((phase, s) for s in everything)

    def grid_blocks(work, after=()):
        return partials(inner, cols, work, context, out_weight, rows, had, after=after)

    blocks2 = ((0, 0),) + tuple((1, s) for s in shifts)
    keep1, keep2, *send2 = grid_blocks(
        ((True, away1), (True, blocks2), *((False, (block,)) for block in blocks2))
    )
    other2 = [swap_core(send) for send in send2]
    items1 = [[(0, s - 1, False, None), (1, s - 1, False, None)] for s in shifts]
    first = add_up(
        inner,
        [keep1, other1],
        [(items, UPPER) for items in items1] + [(items, LOWER) for items in items1],
        after=[keep2],
    )
    pay1, low1 = first[: len(shifts)], first[len(shifts) :]
    come1 = [shift_mid(pay, s) for s, pay in zip(shifts, pay1)]
    low_pairs = [swap_pairs(low) for low in low1]
    low_middle = [swap_middle(low) for low in low1]
    near_block = ((1, 0),)
    send2n, send3 = grid_blocks(((False, near_block), (False, phase_blocks(2))), pay1[:1])
    other2n, other3 = swap_core(send2n), swap_core(send3)
    send4, keep2n, keep3, keep4 = grid_blocks(
        (
            (False, phase_blocks(3)),
            (True, near_block),
            (True, phase_blocks(2)),
            (True, phase_blocks(3)),
        ),
        [send3],
    )
    other4 = swap_core(send4)

    def sums(arrays, outputs, after=()):
        names = list(arrays)
        items = [
            ([(names.index(name), *rest) for name, *rest in output], None) for output in outputs
        ]
        return add_up(inner, list(arrays.values()), items, after=after)

    def named(name, blocks):
        return {f"{name}_{s}": block for s, block in zip(shifts, blocks)}

    def added(names, half=None):
        return [(name, None, False, half) for name in names]

    own2 = {"keep2": keep2} | {f"other2_{i}": other for i, other in enumerate(other2)}
    own2n = {"keep2n": keep2n, "other2n": other2n}
    own3 = {"keep3": keep3, "other3": other3}
    own4 = {"keep4": keep4, "other4": other4}

    def part2(i):
        return [("keep2", i, False, None), (f"other2_{i}", 0, False, None)]

    def part(step, s):
        return [(f"keep{step}", s, False, None), (f"other{step}", s, False, None)]

    def passed(name, s):
        return [(f"{name}_{s}", None, True, LOWER)]

    def relayed(name):
        return [(name, None, True, None)]

    came1, from_pairs = named("came1", come1), named("pairs", low_pairs)
    from_middle = named("middle", low_middle)
    near1 = part2(0) + added(came1, UPPER)
    *pay2, end1 = sums(
        own2 | came1 | from_pairs,
        [*(part2(s) + passed("pairs", s) for s in shifts), near1],
        after=[*come1, send4],
    )
    came2 = named("came2", [shift_mid(pay, s) for s, pay in zip(shifts, pay2)])
    from_end1 = {"end1": swap_pairs(end1)}
    turned_residual, factors = turn_residual(inner, residual, rows, had, after=[end1])
    picked = select_rows(inner, next_query_weight, cols, after=[factors])
    next_other = [swap_core(part) for part in picked]

    near2 = part("2n", 0) + added(came2)
    *pay3, sum2 = sums(
        came2 | from_end1 | own2n | own3,
        [*(part(3, s) for s in shifts), near2 + relayed("end1")],
        after=[*picked[:1], *low_middle],
    )
    came3 = named("came3", [shift_mid(pay, s) for s, pay in zip(shifts, pay3)])
    from_end2 = {"end2": swap_pairs(sum2)}
    from_mid2 = {"mid2": swap_middle(sum2)}

    *pay4, near3, mid3 = sums(
        came3 | from_end2 | from_mid2 | own2 | own3 | own4 | came1 | from_middle,
        [
            *(part(4, s) + passed("middle", s) for s in shifts),
            part(3, 0) + added(came3) + relayed("mid2"),
            near1 + relayed("end2"),
        ],
    )
    come4 = [shift_mid(pay, s) for s, pay in zip(shifts, pay4)]
    from_mid3 = swap_middle(mid3)
    from_near3 = swap_pairs(near3)

    gain = norm_gain.astype(F32).reshape(-1, ROT)

    last = [*come4, from_near3, from_mid3, keep4, other4]
    items = [(None, False)] * (len(come4) + 1) + [(None, True)] + [(0, False)] * 2
    grid = regrid(inner, items, turned_residual, factors, last)

    x1 = [shift_mid(grid, s) for s in shifts]
    near = swap_pairs(grid)
    mid1 = swap_middle(grid)
    hidden_out, mark = hidden(inner, items, residual, factors, had, last, after=[grid])
    near, mid1, *low1 = gate([near, mid1], x1, after=[mark])
    x2 = [shift_mid(near, s) for s in shifts]
    ends2 = swap_pairs(mid1)
    mids2 = swap_middle(near)
    (third,) = choose(inner, mids2, ends2, after=x2)
    x3 = [shift_mid(third, s) for s in shifts]
    ends3 = swap_pairs(mids2)
    side_middle = [swap_middle(low) for low in low1]
    turned_next = turn_next(inner, next_query_weight, next_other, gain, rows, had, after=[third])
    fourth, *low3, up4 = choose(inner, mid1, ends3, x3, True, after=[turned_next])
    x4 = [shift_mid(up4, s) for s in shifts]
    side_pairs = [swap_pairs(low) for low in low3]
    acc = project(
        inner,
        turned_next,
        rows,
        None,
        [(0, 0, [grid]), (1, 0, [near]), (2, 0, [third]), (3, 0, [fourth])]
        + [(phase, s, [x[s - 1]]) for phase, x in enumerate((x1, x2, x3)) for s in shifts],
    )
    own, other = project(
        inner,
        turned_next,
        rows,
        acc,
        [(3, s, [x4[s - 1], side_middle[s - 1], side_pairs[s - 1]]) for s in shifts],
        split=True,
    )
    query_next = finish(own, swap_core(other), norm_gain.shape[0])
    return (hidden_out, query_next)


def solution(mesh):
    placed = (
        P("tp", "groups", None),
        P("tp", "groups", None),
        P("tp", "groups", None),
        P("groups"),
        P("tp", None),
        P("groups", "tp"),
        P(),
        P(),
        P(None, "tp"),
    )
    return jax.shard_map(
        functools.partial(body, mesh.shape["tp"]),
        mesh=mesh,
        in_specs=placed,
        out_specs=(P("groups", "tp"), P("groups", "tp")),
        check_vma=False,
    )
```
